32 devices in a mesh: hi: 8 (over z, y), lo: 4 (over x, core).
Axes of the slice: x: 2, y: 2, z: 4, core: 2. Of those that a mesh axis runs over, the one named last changes fastest.
Arguments:
- state: bfloat16 [2, 8388608], P(None, ('hi', 'lo')), may hold values from -6 to 6
- gates: bfloat16 [4, 3, 2, 64, 64], replicated, may hold values from -0.5 to 0.5
- regroup: int32 [4], replicated, may hold values from 0 to 3, each once
Outputs:
- final_state: bfloat16 [2, 8388608], P(None, ('hi', 'lo'))
The draws below stay inside these ranges and needn't reach their ends.
Inputs may be any that keep to these rules, and one draw needn't show every extreme that they name: `regroup`: each value of 0 to 3 appears once.
All inputs are finite; a program needn't handle non-finite values.
Results may differ from the reference program's by a relative error of at most 0.02.
Values may be sent and summed in bfloat16 or wider, within the bound.
No kernel may reach another device: no remote copies, remote signals or barrier semaphores. Data moves between devices by JAX's collectives and lax.ppermute only.
A program may use at most 64 MiB of HBM per device.

```python
import jax
import jax.numpy as jnp
from jax import lax

GQ = 6
G = 64
Q = 262144
LAYERS = 4
AMPS = 8388608
NLO = 4
N_HI = 8
N_LO = 4


def block_scale(stream_key, shape, shards, smallest, top_value):
    factor_of = 1.0
    for axis_at, parts in shards:
        draws = jax.random.uniform(jax.random.fold_in(jax.random.fold_in(stream_key, 6), axis_at), (parts,), jnp.float32, smallest / len(shards), top_value / len(shards))
        factor_of = factor_of * jnp.repeat(jnp.exp(draws), shape[axis_at] // parts).reshape((-1,) + (1,) * (len(shape) - 1 - axis_at))
    return factor_of


def scatter_about(stream_key, dims, spread, bound, pieces=(), kind=jnp.bfloat16):
    array = spread * jax.random.normal(stream_key, dims, jnp.float32)
    if pieces:
        array = array * block_scale(stream_key, dims, pieces, -0.22, 0.18)
    return jnp.clip(array, -bound, bound).astype(kind)


def setup_inputs(seed: int = 0) -> dict:
    splits = jax.random.split(jax.random.key(seed), 4)
    return {
        "state": scatter_about(splits[0], (2, AMPS), 1.0, 6.0, ((1, 32),)),
        "gates": scatter_about(splits[1], (LAYERS, 3, 2, G, G), (2 * G) ** -0.5, 0.5),
        "regroup": jax.random.permutation(splits[2], NLO).astype(jnp.int32),
    }


def complex_block(gate):
    real_part = gate[0].astype(jnp.float32)
    imag_part = gate[1].astype(jnp.float32)
    upper = jnp.concatenate([real_part, -imag_part], axis=1)
    lower = jnp.concatenate([imag_part, real_part], axis=1)
    whole = jnp.concatenate([upper, lower], axis=0)
    return whole.reshape(2, G, 2, G)


def apply_gate(rows, matrix, block):
    inner = 2 ** (GQ * block)
    outer = Q // (inner * G)
    shaped = rows.reshape(2, rows.shape[1], outer, G, inner).astype(jnp.float32)
    result = jnp.einsum('qkpj,pnajb->qnakb', matrix, shaped)
    return result.astype(jnp.bfloat16).reshape(rows.shape)


def swap_hi(whole, hi_bit, local_bit):
    shaped = whole.reshape(2, N_HI // 2 ** (hi_bit + 1), 2, 2 ** hi_bit, N_LO, Q // 2 ** (local_bit + 1), 2, 2 ** local_bit)
    return jnp.swapaxes(shaped, 2, 6).reshape(whole.shape)


def reference(state, gates, regroup):
    whole = state.reshape(2, N_HI, N_LO, Q)
    hi_bits = int(N_HI).bit_length() - 1
    for layer in range(LAYERS):
        matrices = [complex_block(gates[layer, j]) for j in range(3)]

        def one_row(rows):
            for j in range(3):
                rows = apply_gate(rows, matrices[j], j)
            return rows

        moved = jnp.moveaxis(whole, 1, 0)
        moved = lax.map(one_row, moved)
        whole = jnp.moveaxis(moved, 0, 1)
        local_bit = 2 * GQ - 1 if layer % 2 == 0 else 3 * GQ - 1
        whole = swap_hi(whole, layer % hi_bits, local_bit)
        if layer == LAYERS // 2 - 1:
            shaped = whole.reshape(2, N_HI, N_LO, N_LO, Q // N_LO)
            taken = jnp.take(shaped, regroup.astype(jnp.int32), axis=3)
            whole = jnp.swapaxes(taken, 2, 3).reshape(2, N_HI, N_LO, Q)
    return whole.reshape(2, N_HI * N_LO * Q)
```

```python
import functools

import jax
import jax.numpy as jnp
from jax import lax
from jax.experimental import pallas as pl
from jax.experimental.pallas import tpu as pltpu
from jax.sharding import PartitionSpec as P

GQ = 6
G = 2**GQ
HALF = G // 2
BF = jnp.bfloat16
F32 = jnp.float32


def product(later, earlier):
    dot = functools.partial(jnp.einsum, "ij,jk->ik", precision=lax.Precision.HIGHEST, preferred_element_type=F32)
    real = dot(later[0], earlier[0]) - dot(later[1], earlier[1])
    imag = dot(later[0], earlier[1]) + dot(later[1], earlier[0])
    return jnp.stack([real, imag])


def as_real(gate):
    upper = jnp.stack([gate[0], -gate[1]], axis=1)
    lower = jnp.stack([gate[1], gate[0]], axis=1)
    return jnp.stack([upper, lower], axis=0)


def times_i(w, axis):
    first, second = jnp.split(w, 2, axis=axis)
    return jnp.concatenate([-second, first], axis=axis)


def flip(w, axis, bit):
    return jnp.where(bit == 0, w, jnp.flip(w, axis))


def first_weights(gate):
    m = as_real(gate).reshape(2, 2, HALF, 2, 2, HALF)
    w = jnp.einsum("pqrsuv,xy->qpxrsyuv", m, jnp.eye(2, dtype=m.dtype))
    return w.reshape(4 * G, 4 * G).astype(BF)


def right_weights(gate, in_low, in_bit, out_bit):
    m = as_real(gate)
    m = m.reshape(2, 2, HALF, 2, G)
    if in_low:
        m = m.reshape(2, 2, HALF, 2, HALF, 2)
        w = jnp.einsum("pirsht,xy->xsthiypr", m, jnp.eye(2, dtype=m.dtype))
    else:
        m = flip(m.reshape(2, 2, HALF, 2, 2, HALF), 4, in_bit)
        w = jnp.einsum("pirsjh,xy->jxshiypr", m, jnp.eye(2, dtype=m.dtype))
    w = flip(w, 4, out_bit)
    both = jnp.stack([w, times_i(w, 6)], axis=4)
    return both.reshape(4 * G, 8 * G).astype(BF)


def left_weights(gate, order, out_bit):
    g = jnp.concatenate([gate[0][:, order], gate[1][:, order]], axis=1)
    return flip(g.reshape(2, HALF, 2 * G), 0, out_bit).reshape(G, 2 * G).astype(BF)


def last_weights(gate, in_bit):
    m = as_real(gate).reshape(2, HALF, 2, 2, 2, HALF)
    m = flip(m, 4, in_bit)
    w = jnp.einsum("phtsjr,xy->ptxhjysr", m, jnp.eye(2, dtype=m.dtype))
    return w.reshape(4 * G, 4 * G).astype(BF)


def turn(parts):
    lane = lax.broadcasted_iota(jnp.int32, (parts[0].shape[0], 128), 1)
    wide = lane < 64
    narrow = (lane & 32) == 0
    out = [[None, None] for _ in range(8)]
    for n in range(2):
        for m in range(2):
            a = [parts[n * 4 + r][:, m * 128 : (m + 1) * 128] for r in range(4)]
            s = [None] * 4
            for r in range(2):
                s[r] = jnp.where(wide, a[r], pltpu.roll(a[r + 2], 64, 1))
                s[r + 2] = jnp.where(wide, pltpu.roll(a[r], 64, 1), a[r + 2])
            for r in (0, 2):
                out[m * 4 + r][n] = jnp.where(narrow, s[r], pltpu.roll(s[r + 1], 32, 1))
                out[m * 4 + r + 1][n] = jnp.where(narrow, pltpu.roll(s[r], 96, 1), s[r + 1])
    return out


NT = (((1,), (1,)), ((), ()))


def both_gates(x, w, g):
    n = x.shape[0]
    z = jnp.dot(x.reshape(n * G, 4 * G), w, preferred_element_type=F32).astype(BF)
    outs = []
    for k in range(n):
        rows = z[k * G : (k + 1) * G]
        s = jnp.concatenate([rows[:, : 4 * G], rows[:, 4 * G :]], axis=0)
        outs.append(jnp.dot(g, s, preferred_element_type=F32).astype(BF))
    return outs


def store_blocks(outs, at, blocks):
    for k, out in enumerate(outs):
        for i in range(2):
            for j in range(2):
                blocks[2 * i + j][at + k] = out[j * HALF : (j + 1) * HALF, i * 128 : (i + 1) * 128]


STEP = 8


def first_kernel(x_ref, w0_ref, w1_ref, g_ref, o00, o01, o10, o11, turned):
    def relayout(k, carry):
        rows = pl.ds(k * 256, 256)
        x = jnp.concatenate([x_ref[0, rows, :], x_ref[1, rows, :]], axis=1)
        r = lax.dot_general(w0_ref[...], x, NT, preferred_element_type=F32)
        tiles = turn([r[g * HALF : (g + 1) * HALF] for g in range(8)])
        for q in range(8):
            for n in range(2):
                turned[n, pl.ds(k * 8 + q, HALF, stride=G), :] = tiles[q][n]
        return carry

    lax.fori_loop(0, G // 8, relayout, 0)

    def gates(k, carry):
        rows = pl.ds(k * STEP * G, STEP * G)
        x = jnp.concatenate([turned[0, rows, :], turned[1, rows, :]], axis=1).astype(BF).reshape(STEP, G, 4 * G)
        store_blocks(both_gates(x, w1_ref[...], g_ref[...]), k * STEP, (o00, o01, o10, o11))
        return carry

    lax.fori_loop(0, HALF // STEP, gates, 0)


def middle_kernel(*refs):
    *ins, w1_ref, g_ref, o00, o01, o10, o11 = refs

    def gates(k, carry):
        at = pl.ds(k * STEP, STEP)
        halves = [jnp.concatenate([x[i, at] for x in ins], axis=1) for i in range(2)]
        x = jnp.concatenate(halves, axis=2)
        store_blocks(both_gates(x, w1_ref[...], g_ref[...]), k * STEP, (o00, o01, o10, o11))
        return carry

    lax.fori_loop(0, HALF // STEP, gates, 0)


def last_kernel(bit_ref, b00, b01, b10, b11, w_ref, o_ref, wide):
    bit = bit_ref[0]
    blocks = ((b00, b01), (b10, b11))

    def widen(k, carry):
        for i in range(2):
            for j in range(2):
                start = pl.multiple_of(k * G + (bit ^ j) * HALF, HALF)
                wide[i, pl.ds(start, HALF), :] = blocks[i][j][k].astype(F32)
        return carry

    lax.fori_loop(0, HALF, widen, 0)

    def relayout(k, carry):
        halves = [
            jnp.concatenate([wide[i, pl.ds(k * 8 + q, HALF, stride=G), :] for q in range(8)], axis=0) for i in range(2)
        ]
        x = jnp.concatenate(halves, axis=1).astype(BF)
        r = lax.dot_general(w_ref[...], x, NT, preferred_element_type=F32)
        tiles = turn([r[g * HALF : (g + 1) * HALF] for g in range(8)])
        for q in range(8):
            for n in range(2):
                o_ref[n, pl.ds(k * 256 + q * HALF, HALF), :] = tiles[q][n].astype(BF)
        return carry

    lax.fori_loop(0, G // 8, relayout, 0)


def pick_kernel(s_ref, b00, b01, b10, b11, *outs):
    blocks = ((b00, b01), (b10, b11))
    rows = outs[0].shape[2]
    for o, out in enumerate(outs):
        j = s_ref[o, 0]
        at = pl.ds(pl.multiple_of(s_ref[o, 1] * rows, rows), rows)
        for i in range(2):
            out[i] = jnp.where(j == 0, blocks[i][0][:, at, :], blocks[i][1][:, at, :])


VMEM = pl.BlockSpec(memory_space=pltpu.VMEM)
SMEM = pl.BlockSpec(memory_space=pltpu.SMEM)


def call(kernel, outs, args, specs=None, scratch=()):
    return pl.pallas_call(
        kernel,
        out_shape=outs,
        in_specs=specs or [VMEM] * len(args),
        out_specs=jax.tree.map(lambda _: VMEM, outs),
        scratch_shapes=scratch,
        compiler_params=pltpu.CompilerParams(vmem_limit_bytes=40 * 2**20),
    )(*args)


def exchange(blocks, b_bit, a_bit):
    size = lax.axis_size("hi")
    out = []
    for at, block in enumerate(blocks):
        apart = (at >> 1 << b_bit) | ((at & 1) << a_bit)
        out.append(lax.ppermute(block, "hi", [(d, d ^ apart) for d in range(size)]) if apart else block)
    return out


def on_device(state, gates, regroup):
    hi_bits = lax.axis_size("hi").bit_length() - 1
    groups = lax.axis_size("lo")
    hi = lax.axis_index("hi")
    lo = lax.axis_index("lo")
    bits = [k % hi_bits for k in range(4)]
    own = [hi >> bit & 1 for bit in bits]
    top = G // groups

    g = gates.astype(F32)
    w0 = first_weights(product(product(g[3, 0], g[2, 0]), product(g[1, 0], g[0, 0])))
    w1a = right_weights(g[0, 1], True, None, own[0])
    w1b = right_weights(product(g[2, 1], g[1, 1]), False, own[0], own[2])
    w1c = last_weights(g[3, 1], own[2])
    ga = left_weights(product(g[1, 2], g[0, 2]), jnp.arange(G), own[1])

    block = jax.ShapeDtypeStruct((HALF, HALF, 128), BF)
    x = state.reshape(2, -1, 128)
    blocks = call(
        first_kernel,
        [block] * 4,
        (x, w0, w1a, ga),
        scratch=[pltpu.VMEM((2, HALF * G, 128), F32)],
    )
    blocks = exchange(blocks, bits[0], bits[1])

    if groups == 4:
        order = (jnp.arange(G) // top ^ lo) * top + jnp.arange(G) % top
        sent = regroup[jnp.arange(groups) ^ lo]
        table = jnp.stack([sent // 2 ^ own[1], sent % 2], axis=1)
        part = jax.ShapeDtypeStruct((2, HALF, top, 128), BF)
        parts = call(pick_kernel, [part] * groups, (table, *blocks), specs=[SMEM] + [VMEM] * 4)
        parts = [parts[0]] + [
            lax.ppermute(parts[o], "lo", [(d, d ^ o) for d in range(groups)]) for o in range(1, groups)
        ]
    else:
        order = jnp.arange(G)
        whole = jnp.stack([flip(jnp.stack(blocks[2 * i : 2 * i + 2], 1), 1, own[1]) for i in range(2)])
        whole = whole.reshape(2, HALF, groups, top, 128)
        whole = lax.all_to_all(jnp.take(whole, regroup, axis=2), "lo", split_axis=2, concat_axis=2, tiled=True)
        parts = [whole.reshape(2, HALF, G, 128)]
    gb = left_weights(product(g[3, 2], g[2, 2]), order, own[3])
    blocks = call(middle_kernel, [block] * 4, (*parts, w1b, gb))
    blocks = exchange(blocks, bits[2], bits[3])

    out = call(
        last_kernel,
        jax.ShapeDtypeStruct(x.shape, BF),
        (own[3].reshape(1), *blocks, w1c),
        specs=[SMEM] + [VMEM] * 5,
        scratch=[pltpu.VMEM((2, HALF * G, 128), F32)],
    )
    return out.reshape(state.shape)


def solution(mesh):
    placed = (P(None, ("hi", "lo")), P(), P())
    return jax.shard_map(
        on_device, mesh=mesh, in_specs=placed, out_specs=P(None, ("hi", "lo")), check_vma=False
    )
```

```python
import functools

import jax
import jax.numpy as jnp
from jax import lax
from jax.experimental import pallas as pl
from jax.experimental.pallas import tpu as pltpu
from jax.sharding import PartitionSpec as P

GQ = 6
G = 2**GQ
HALF = G // 2
BF = jnp.bfloat16
F32 = jnp.float32


def iotas(rows, columns):
    shape = (rows, columns)
    return lax.broadcasted_iota(jnp.int32, shape, 0), lax.broadcasted_iota(jnp.int32, shape, 1)


def dot(x, y):
    return jnp.dot(x, y, preferred_element_type=F32)


def turned_dot(x, y):
    return lax.dot_general(x, y, (((1,), (1,)), ((), ())), preferred_element_type=F32)


def ones(where):
    return where.astype(F32).astype(BF)


def gate_of(ref, layer, block):
    return jnp.concatenate([ref[layer, block, 0], ref[layer, block, 1]], axis=1)


def squared(gate):
    return jnp.concatenate([gate, jnp.concatenate([-gate[:, G:], gate[:, :G]], axis=1)], axis=0)


def product(later, earlier):
    return dot(later, squared(earlier))


def wide_product(later, earlier):
    parts = []
    for x in (later, squared(earlier)):
        high = x.astype(BF)
        parts.append((high, (x - high.astype(F32)).astype(BF)))
    (lh, ll), (eh, el) = parts
    return dot(jnp.concatenate([lh, lh, ll], axis=1), jnp.concatenate([eh, el, eh], axis=0))


def first_weights(gate):
    real = jnp.concatenate([gate[:, :G], gate[:, :G]], axis=1)
    imag = jnp.concatenate([gate[:, G:], gate[:, G:]], axis=1)
    low = iotas(HALF, 2 * G)[1] < G
    rows = []
    for ch in range(2):
        r, i = (x[ch * HALF : (ch + 1) * HALF] for x in (real, imag))
        for pair in ((r, -i), (i, r)):
            for mask in (low, ~low):
                rows.append(jnp.concatenate([jnp.where(mask, x, 0.0) for x in pair], axis=1))
    return jnp.concatenate(rows, axis=0).astype(BF)


def right_weights(gate, low, in_bit, out_bit):
    k, b = iotas(G, G)
    order = ((k & (HALF - 1)) << 1 | k >> GQ - 1) if low else k ^ in_bit * HALF
    gate = gate.astype(BF)
    t = turned_dot(ones(b == order), jnp.concatenate([gate[:, :G], gate[:, G:]], axis=0)).astype(BF)
    at, n = iotas(2 * G, 8 * G)
    bit = lambda i: n >> i & 1
    to = ((bit(7) ^ out_bit) << GQ - 1) | n & (HALF - 1)
    turn_i = bit(8)
    part = bit(5) ^ turn_i
    sign_i = turn_i & (1 - bit(5))
    ch = iotas(G, 8 * G)[1] >> 6 & 1
    made = []
    for p in range(2):
        minus = sign_i ^ ((1 - part) & p)
        place = jnp.where(at == to + (part ^ p) * G, (1 - 2 * minus).astype(F32), 0.0).astype(BF)
        y = dot(t, place)
        made.append([jnp.where(ch == c, y, 0.0).astype(BF) for c in range(2)])
    if low:
        rows = [made[p][c] for c in range(2) for p in range(2)]
    else:
        rows = [made[p][c][i * HALF : (i + 1) * HALF] for i in range(2) for c in range(2) for p in range(2)]
    return jnp.concatenate(rows, axis=0)


def left_weights(gate, step, out_bit):
    k, a = iotas(G, G)
    rows = dot(ones(a == k ^ out_bit * HALF), gate.astype(BF)).astype(BF)
    k, a = iotas(2 * G, 2 * G)
    return dot(rows, ones(a == k ^ step)).astype(BF)


def last_weights(gate, in_bit):
    k, b = iotas(G, G)
    t = dot(ones(b == ((k & (HALF - 1)) << 1 | k >> GQ - 1)), gate).astype(BF)
    at, n = iotas(2 * G, 4 * G)
    p_in = n >> 5 & 1
    b_in = ((n >> 7 ^ in_bit) << GQ - 1) | n & (HALF - 1)
    ch = iotas(HALF, 4 * G)[1] >> 6 & 1
    rows = []
    for p in range(2):
        minus = (1 - p) * p_in
        place = jnp.where(at == b_in + (p_in ^ p) * G, (1 - 2 * minus).astype(F32), 0.0).astype(BF)
        y = dot(t, place)
        for b0 in range(2):
            for c in range(2):
                rows.append(jnp.where(ch == c, y[b0 * HALF : (b0 + 1) * HALF], 0.0).astype(BF))
    return jnp.concatenate(rows, axis=0)


def turn(parts):
    lane = lax.broadcasted_iota(jnp.int32, (parts[0].shape[0], 128), 1)
    wide = lane < 64
    narrow = (lane & 32) == 0
    out = [[None, None] for _ in range(8)]
    for n in range(2):
        for m in range(2):
            a = [parts[n * 4 + r][:, m * 128 : (m + 1) * 128] for r in range(4)]
            s = [None] * 4
            for r in range(2):
                s[r] = jnp.where(wide, a[r], pltpu.roll(a[r + 2], 64, 1))
                s[r + 2] = jnp.where(wide, pltpu.roll(a[r], 64, 1), a[r + 2])
            for r in (0, 2):
                out[m * 4 + r][n] = jnp.where(narrow, s[r], pltpu.roll(s[r + 1], 32, 1))
                out[m * 4 + r + 1][n] = jnp.where(narrow, pltpu.roll(s[r], 96, 1), s[r + 1])
    return out


def both_gates(x, w, g):
    n = x.shape[0]
    z = jnp.dot(x.reshape(n * G, 4 * G), w, preferred_element_type=F32).astype(BF)
    outs = []
    for k in range(n):
        rows = z[k * G : (k + 1) * G]
        s = jnp.concatenate([rows[:, : 4 * G], rows[:, 4 * G :]], axis=0)
        outs.append(jnp.dot(g, s, preferred_element_type=F32).astype(BF))
    return outs


def store_blocks(outs, at, blocks):
    for k, out in enumerate(outs):
        for i in range(2):
            for j in range(2):
                blocks[2 * i + j][at + k] = out[j * HALF : (j + 1) * HALF, i * 128 : (i + 1) * 128]


STEP = 8


def own_bits():
    hi_bits = lax.axis_size("hi").bit_length() - 1
    hi = lax.axis_index("hi")
    return [hi >> k % hi_bits & 1 for k in range(4)]


def first_kernel(x_ref, gates, o00, o01, o10, o11, spread, turned, w1_ref):
    own = own_bits()
    late = product(gate_of(gates, 3, 0), gate_of(gates, 2, 0))
    early = product(gate_of(gates, 1, 0), gate_of(gates, 0, 0))
    w0 = first_weights(wide_product(late, early))
    w1_ref[...] = right_weights(gate_of(gates, 0, 1), True, 0, own[0])
    g = left_weights(product(gate_of(gates, 1, 2), gate_of(gates, 0, 2)), 0, own[1])

    for k in range(G // 8):
        spread[k * 512 : (k + 1) * 512, :] = x_ref[k * 512 : (k + 1) * 512, :].astype(F32)
        x = jnp.concatenate([spread[pl.ds(k * 512 + p, 256, stride=2), :] for p in range(2)], axis=1).astype(BF)
        r = turned_dot(w0, x)
        tiles = turn([r[g * HALF : (g + 1) * HALF] for g in range(8)])
        for q in range(8):
            for n in range(2):
                turned[n, pl.ds(k * 8 + q, HALF, stride=G), :] = tiles[q][n]

    for k in range(0, HALF, STEP):
        rows = slice(k * G, (k + STEP) * G)
        x = jnp.concatenate([turned[0, rows, :], turned[1, rows, :]], axis=1).astype(BF).reshape(STEP, G, 4 * G)
        store_blocks(both_gates(x, w1_ref[...], g), k, (o00, o01, o10, o11))


def weights_kernel(top, gates, w1_ref, g_ref, w_ref):
    own = own_bits()
    w1_ref[...] = right_weights(product(gate_of(gates, 2, 1), gate_of(gates, 1, 1)), False, own[0], own[2])
    step = top * lax.axis_index("lo") if top else 0
    g_ref[...] = left_weights(product(gate_of(gates, 3, 2), gate_of(gates, 2, 2)), step, own[3])
    w_ref[...] = last_weights(gate_of(gates, 3, 1), own[2])


def middle_kernel(*refs):
    *ins, w1_ref, g_ref, o00, o01, o10, o11 = refs
    for k in range(0, HALF, STEP):
        halves = [jnp.concatenate([x[i, k : k + STEP] for x in ins], axis=1) for i in range(2)]
        x = jnp.concatenate(halves, axis=2)
        store_blocks(both_gates(x, w1_ref[...], g_ref[...]), k, (o00, o01, o10, o11))


def last_kernel(b00, b01, b10, b11, w_ref, o_ref, wide, spread):
    bit = own_bits()[3]
    blocks = ((b00, b01), (b10, b11))
    for k in range(HALF):
        for j in range(2):
            rows = pl.ds(pl.multiple_of(k * G + (bit ^ j) * HALF, HALF), HALF)
            for i in range(2):
                wide[i, rows, :] = blocks[i][j][k].astype(F32)
    for k in range(G // 8):
        halves = [
            jnp.concatenate([wide[i, pl.ds(k * 8 + q, HALF, stride=G), :] for q in range(8)], axis=0) for i in range(2)
        ]
        x = jnp.concatenate(halves, axis=1).astype(BF)
        r = turned_dot(w_ref[...], x)
        tiles = turn([r[g * HALF : (g + 1) * HALF] for g in range(8)])
        for q in range(8):
            for n in range(2):
                spread[pl.ds((k * 8 + q) * G + n, HALF, stride=2), :] = tiles[q][n]
        o_ref[k * 512 : (k + 1) * 512, :] = spread[k * 512 : (k + 1) * 512, :].astype(BF)


def pick_kernel(regroup, b00, b01, b10, b11, *outs):
    blocks = ((b00, b01), (b10, b11))
    own = own_bits()[1]
    lo = lax.axis_index("lo")
    rows = outs[0].shape[2]
    for o, out in enumerate(outs):
        t = regroup[lo ^ o]
        j = t >> 1 ^ own
        at = pl.ds(pl.multiple_of((t & 1) * rows, rows), rows)
        for i in range(2):
            out[i] = jnp.where(j == 0, blocks[i][0][:, at, :], blocks[i][1][:, at, :])


VMEM = pl.BlockSpec(memory_space=pltpu.VMEM)
SMEM = pl.BlockSpec(memory_space=pltpu.SMEM)


def call(kernel, outs, args, specs=None, scratch=()):
    return pl.pallas_call(
        kernel,
        out_shape=outs,
        in_specs=specs or [VMEM] * len(args),
        out_specs=jax.tree.map(lambda _: VMEM, outs),
        scratch_shapes=scratch,
        compiler_params=pltpu.CompilerParams(vmem_limit_bytes=40 * 2**20),
    )(*args)


def exchange(blocks, b_bit, a_bit):
    size = lax.axis_size("hi")
    out = []
    for at, block in enumerate(blocks):
        apart = (at >> 1 << b_bit) | ((at & 1) << a_bit)
        out.append(lax.ppermute(block, "hi", [(d, d ^ apart) for d in range(size)]) if apart else block)
    return out


def on_device(state, gates, regroup):
    hi_bits = lax.axis_size("hi").bit_length() - 1
    groups = lax.axis_size("lo")
    bits = [k % hi_bits for k in range(4)]
    top = G // groups
    whole = 2 * state.shape[1] // 128

    block = jax.ShapeDtypeStruct((HALF, HALF, 128), BF)
    turned = pltpu.VMEM((2, HALF * G, 128), F32)
    spread = pltpu.VMEM((whole, 128), F32)
    x = state.reshape(2, -1, 128).transpose(1, 0, 2).reshape(whole, 128)
    blocks = call(first_kernel, [block] * 4, (x, gates), scratch=[spread, turned, pltpu.VMEM((4 * G, 8 * G), BF)])
    blocks = exchange(blocks, bits[0], bits[1])
    shapes = [jax.ShapeDtypeStruct(shape, BF) for shape in ((4 * G, 8 * G), (G, 2 * G), (4 * G, 4 * G))]
    w1, g, w = call(functools.partial(weights_kernel, top if groups == 4 else 0), shapes, (gates,))

    if groups == 4:
        part = jax.ShapeDtypeStruct((2, HALF, top, 128), BF)
        parts = call(pick_kernel, [part] * groups, (regroup, *blocks), specs=[SMEM] + [VMEM] * 4)
        parts = [parts[0]] + [
            lax.ppermute(parts[o], "lo", [(d, d ^ o) for d in range(groups)]) for o in range(1, groups)
        ]
    else:
        own = lax.axis_index("hi") >> bits[1] & 1
        halves = [jnp.stack(blocks[2 * i : 2 * i + 2], 1) for i in range(2)]
        both = jnp.stack([jnp.where(own == 0, half, jnp.flip(half, 1)) for half in halves])
        both = jnp.take(both.reshape(2, HALF, groups, top, 128), regroup, axis=2)
        both = lax.all_to_all(both, "lo", split_axis=2, concat_axis=2, tiled=True)
        parts = [both.reshape(2, HALF, G, 128)]
    blocks = call(middle_kernel, [block] * 4, (*parts, w1, g))
    blocks = exchange(blocks, bits[2], bits[3])

    out = call(last_kernel, jax.ShapeDtypeStruct((whole, 128), BF), (*blocks, w), scratch=[turned, spread])
    return out.reshape(-1, 2, 128).transpose(1, 0, 2).reshape(state.shape)


def solution(mesh):
    placed = (P(None, ("hi", "lo")), P(), P())
    return jax.shard_map(
        on_device, mesh=mesh, in_specs=placed, out_specs=P(None, ("hi", "lo")), check_vma=False
    )
```

```python
import functools

import jax
import jax.numpy as jnp
from jax import lax
from jax.experimental import pallas as pl
from jax.experimental.pallas import tpu as pltpu
from jax.sharding import PartitionSpec as P

GQ = 6
G = 2**GQ
HALF = G // 2
BF = jnp.bfloat16
F32 = jnp.float32


def iotas(rows, columns):
    shape = (rows, columns)
    return lax.broadcasted_iota(jnp.int32, shape, 0), lax.broadcasted_iota(jnp.int32, shape, 1)


def dot(x, y):
    return jnp.dot(x, y, preferred_element_type=F32)


def turned_dot(x, y):
    return lax.dot_general(x, y, (((1,), (1,)), ((), ())), preferred_element_type=F32)


def ones(where):
    return where.astype(F32).astype(BF)


def gate_of(ref, layer, block):
    return jnp.concatenate([ref[layer, block, 0], ref[layer, block, 1]], axis=1)


def squared(gate):
    return jnp.concatenate([gate, jnp.concatenate([-gate[:, G:], gate[:, :G]], axis=1)], axis=0)


def product(later, earlier):
    return dot(later, squared(earlier))


def wide_product(later, earlier):
    parts = []
    for x in (later, squared(earlier)):
        high = x.astype(BF)
        parts.append((high, (x - high.astype(F32)).astype(BF)))
    (lh, ll), (eh, el) = parts
    return dot(jnp.concatenate([lh, lh, ll], axis=1), jnp.concatenate([eh, el, eh], axis=0))


def first_weights(gate):
    real = jnp.concatenate([gate[:, :G], gate[:, :G]], axis=1)
    imag = jnp.concatenate([gate[:, G:], gate[:, G:]], axis=1)
    low = iotas(HALF, 2 * G)[1] < G
    rows = []
    for ch in range(2):
        r, i = (x[ch * HALF : (ch + 1) * HALF] for x in (real, imag))
        for pair in ((r, -i), (i, r)):
            for mask in (low, ~low):
                rows.append(jnp.concatenate([jnp.where(mask, x, 0.0) for x in pair], axis=1))
    return jnp.concatenate(rows, axis=0).astype(BF)


def right_weights(gate, low, in_bit, out_bit):
    k, b = iotas(G, G)
    order = ((k & (HALF - 1)) << 1 | k >> GQ - 1) if low else k ^ in_bit * HALF
    gate = gate.astype(BF)
    t = turned_dot(ones(b == order), jnp.concatenate([gate[:, :G], gate[:, G:]], axis=0)).astype(BF)
    at, n = iotas(2 * G, 8 * G)
    bit = lambda i: n >> i & 1
    to = ((bit(7) ^ out_bit) << GQ - 1) | n & (HALF - 1)
    turn_i = bit(8)
    part = bit(5) ^ turn_i
    sign_i = turn_i & (1 - bit(5))
    ch = iotas(G, 8 * G)[1] >> 6 & 1
    made = []
    for p in range(2):
        minus = sign_i ^ ((1 - part) & p)
        place = jnp.where(at == to + (part ^ p) * G, (1 - 2 * minus).astype(F32), 0.0).astype(BF)
        y = dot(t, place)
        made.append([jnp.where(ch == c, y, 0.0).astype(BF) for c in range(2)])
    if low:
        rows = [made[p][c] for c in range(2) for p in range(2)]
    else:
        rows = [made[p][c][i * HALF : (i + 1) * HALF] for i in range(2) for c in range(2) for p in range(2)]
    return jnp.concatenate(rows, axis=0)


def left_weights(gate, step, out_bit):
    k, a = iotas(G, G)
    rows = dot(ones(a == k ^ out_bit * HALF), gate.astype(BF)).astype(BF)
    k, a = iotas(2 * G, 2 * G)
    return dot(rows, ones(a == k ^ step)).astype(BF)


def last_weights(gate, in_bit):
    k, b = iotas(G, G)
    t = dot(ones(b == ((k & (HALF - 1)) << 1 | k >> GQ - 1)), gate).astype(BF)
    at, n = iotas(2 * G, 4 * G)
    p_in = n >> 5 & 1
    b_in = ((n >> 7 ^ in_bit) << GQ - 1) | n & (HALF - 1)
    ch = iotas(HALF, 4 * G)[1] >> 6 & 1
    rows = []
    for p in range(2):
        minus = (1 - p) * p_in
        place = jnp.where(at == b_in + (p_in ^ p) * G, (1 - 2 * minus).astype(F32), 0.0).astype(BF)
        y = dot(t, place)
        for b0 in range(2):
            for c in range(2):
                rows.append(jnp.where(ch == c, y[b0 * HALF : (b0 + 1) * HALF], 0.0).astype(BF))
    return jnp.concatenate(rows, axis=0)


def turn(parts):
    lane = lax.broadcasted_iota(jnp.int32, (parts[0].shape[0], 128), 1)
    wide = lane < 64
    narrow = (lane & 32) == 0
    out = [[None, None] for _ in range(8)]
    for n in range(2):
        for m in range(2):
            a = [parts[n * 4 + r][:, m * 128 : (m + 1) * 128] for r in range(4)]
            s = [None] * 4
            for r in range(2):
                s[r] = jnp.where(wide, a[r], pltpu.roll(a[r + 2], 64, 1))
                s[r + 2] = jnp.where(wide, pltpu.roll(a[r], 64, 1), a[r + 2])
            for r in (0, 2):
                out[m * 4 + r][n] = jnp.where(narrow, s[r], pltpu.roll(s[r + 1], 32, 1))
                out[m * 4 + r + 1][n] = jnp.where(narrow, pltpu.roll(s[r], 96, 1), s[r + 1])
    return out


def both_gates(x, w, g):
    n = x.shape[0]
    z = jnp.dot(x.reshape(n * G, 4 * G), w, preferred_element_type=F32).astype(BF)
    outs = []
    for k in range(n):
        rows = z[k * G : (k + 1) * G]
        s = jnp.concatenate([rows[:, : 4 * G], rows[:, 4 * G :]], axis=0)
        outs.append(jnp.dot(g, s, preferred_element_type=F32).astype(BF))
    return outs


PLACES = ((1, 0), (1, 1), (0, 1), (0, 0))
APART = (2, 3, 1, 0)


def by_place(blocks):
    return dict(zip(PLACES, blocks))


def store_blocks(outs, at, blocks):
    blocks = by_place(blocks)
    for k, out in enumerate(outs):
        for i in range(2):
            for j in range(2):
                blocks[i, j][at + k] = out[j * HALF : (j + 1) * HALF, i * 128 : (i + 1) * 128]


STEP = 8
CHUNKS = 2


def own_bits():
    hi_bits = lax.axis_size("hi").bit_length() - 1
    hi = lax.axis_index("hi")
    return [hi >> k % hi_bits & 1 for k in range(4)]


def first_kernel(x_ref, gates, *refs):
    *outs, spread, turned, w1_ref = refs
    count = outs[0].shape[0]
    own = own_bits()
    late = product(gate_of(gates, 3, 0), gate_of(gates, 2, 0))
    early = product(gate_of(gates, 1, 0), gate_of(gates, 0, 0))
    w0 = first_weights(wide_product(late, early))
    w1_ref[...] = right_weights(gate_of(gates, 0, 1), True, 0, own[0])
    g = left_weights(product(gate_of(gates, 1, 2), gate_of(gates, 0, 2)), 0, own[1])

    for k in range(G // 8):
        spread[k * 512 : (k + 1) * 512, :] = x_ref[k * 512 : (k + 1) * 512, :].astype(F32)
        x = jnp.concatenate([spread[pl.ds(k * 512 + p, 256, stride=2), :] for p in range(2)], axis=1).astype(BF)
        r = turned_dot(w0, x)
        tiles = turn([r[g * HALF : (g + 1) * HALF] for g in range(8)])
        for q in range(8):
            for n in range(2):
                turned[n, pl.ds(k * 8 + q, HALF, stride=G), :] = tiles[q][n]

    for k in range(0, HALF, STEP):
        rows = slice(k * G, (k + STEP) * G)
        x = jnp.concatenate([turned[0, rows, :], turned[1, rows, :]], axis=1).astype(BF).reshape(STEP, G, 4 * G)
        part = 4 * (k // count)
        store_blocks(both_gates(x, w1_ref[...], g), k % count, outs[part : part + 4])


def weights_kernel(top, gates, w1_ref, g_ref, w_ref):
    own = own_bits()
    w1_ref[...] = right_weights(product(gate_of(gates, 2, 1), gate_of(gates, 1, 1)), False, own[0], own[2])
    step = top * lax.axis_index("lo") if top else 0
    g_ref[...] = left_weights(product(gate_of(gates, 3, 2), gate_of(gates, 2, 2)), step, own[3])
    w_ref[...] = last_weights(gate_of(gates, 3, 1), own[2])


def middle_kernel(*refs):
    *ins, w1_ref, g_ref, o0, o1, o2, o3 = refs
    order = [APART.index(o) for o in range(4)] if len(ins) > 1 else [0]
    for k in range(0, o0.shape[0], STEP):
        ordered = [ins[at] for at in order]
        halves = [jnp.concatenate([x[i, k : k + STEP] for x in ordered], axis=1) for i in range(2)]
        x = jnp.concatenate(halves, axis=2)
        store_blocks(both_gates(x, w1_ref[...], g_ref[...]), k, (o0, o1, o2, o3))


def last_kernel(*refs):
    *ins, w_ref, o_ref, wide, spread = refs
    bit = own_bits()[3]
    count = ins[0].shape[0]
    for k in range(HALF):
        blocks = by_place(ins[4 * (k // count) : 4 * (k // count) + 4])
        for j in range(2):
            rows = pl.ds(pl.multiple_of(k * G + (bit ^ j) * HALF, HALF), HALF)
            for i in range(2):
                wide[i, rows, :] = blocks[i, j][k % count].astype(F32)
    for k in range(G // 8):
        halves = [
            jnp.concatenate([wide[i, pl.ds(k * 8 + q, HALF, stride=G), :] for q in range(8)], axis=0) for i in range(2)
        ]
        x = jnp.concatenate(halves, axis=1).astype(BF)
        r = turned_dot(w_ref[...], x)
        tiles = turn([r[g * HALF : (g + 1) * HALF] for g in range(8)])
        for q in range(8):
            for n in range(2):
                spread[pl.ds((k * 8 + q) * G + n, HALF, stride=2), :] = tiles[q][n]
        o_ref[k * 512 : (k + 1) * 512, :] = spread[k * 512 : (k + 1) * 512, :].astype(BF)


def pick_kernel(regroup, b0, b1, b2, b3, *outs):
    blocks = by_place((b0, b1, b2, b3))
    own = own_bits()[1]
    lo = lax.axis_index("lo")
    rows = outs[0].shape[2]
    for o, out in zip(APART, outs):
        t = regroup[lo ^ o]
        j = t >> 1 ^ own
        at = pl.ds(pl.multiple_of((t & 1) * rows, rows), rows)
        for i in range(2):
            out[i] = jnp.where(j == 0, blocks[i, 0][:, at, :], blocks[i, 1][:, at, :])


VMEM = pl.BlockSpec(memory_space=pltpu.VMEM)
SMEM = pl.BlockSpec(memory_space=pltpu.SMEM)


def call(kernel, outs, args, specs=None, scratch=()):
    return pl.pallas_call(
        kernel,
        out_shape=outs,
        in_specs=specs or [VMEM] * len(args),
        out_specs=jax.tree.map(lambda _: VMEM, outs),
        scratch_shapes=scratch,
        compiler_params=pltpu.CompilerParams(vmem_limit_bytes=40 * 2**20),
    )(*args)


def exchange(blocks, b_bit, a_bit):
    out = []
    for (i, j), block in zip(PLACES, blocks):
        apart = i << b_bit | j << a_bit
        pairs = [(d, d ^ apart) for d in range(lax.axis_size("hi"))]
        out.append(lax.ppermute(block, "hi", pairs) if apart else block)
    return out


def regrouped(blocks, regroup, bit, groups, top):
    count = blocks[0].shape[0]
    if groups == 4:
        part = jax.ShapeDtypeStruct((2, count, top, 128), BF)
        parts = call(pick_kernel, [part] * groups, (regroup, *blocks), specs=[SMEM] + [VMEM] * 4)
        pairs = [[(d, d ^ o) for d in range(groups)] for o in APART]
        return [lax.ppermute(x, "lo", to) if o else x for o, x, to in zip(APART, parts, pairs)]
    own = lax.axis_index("hi") >> bit & 1
    blocks = by_place(blocks)
    halves = [jnp.stack([blocks[i, 0], blocks[i, 1]], axis=1) for i in range(2)]
    both = jnp.stack([jnp.where(own == 0, half, jnp.flip(half, 1)) for half in halves])
    both = jnp.take(both.reshape(2, count, groups, top, 128), regroup, axis=2)
    both = lax.all_to_all(both, "lo", split_axis=2, concat_axis=2, tiled=True)
    return [both.reshape(2, count, G, 128)]


def on_device(state, gates, regroup):
    hi_bits = lax.axis_size("hi").bit_length() - 1
    groups = lax.axis_size("lo")
    bits = [k % hi_bits for k in range(4)]
    top = G // groups
    whole = 2 * state.shape[1] // 128

    count = HALF // CHUNKS
    block = jax.ShapeDtypeStruct((count, HALF, 128), BF)
    turned = pltpu.VMEM((2, HALF * G, 128), F32)
    spread = pltpu.VMEM((whole, 128), F32)
    x = state.reshape(2, -1, 128).transpose(1, 0, 2).reshape(whole, 128)
    scratch = [spread, turned, pltpu.VMEM((4 * G, 8 * G), BF)]
    blocks = call(first_kernel, [block] * (4 * CHUNKS), (x, gates), scratch=scratch)
    shapes = [jax.ShapeDtypeStruct(shape, BF) for shape in ((4 * G, 8 * G), (G, 2 * G), (4 * G, 4 * G))]
    w1, g, w = call(functools.partial(weights_kernel, top if groups == 4 else 0), shapes, (gates,))

    done = []
    for chunk in range(CHUNKS):
        mine = exchange(blocks[4 * chunk : 4 * chunk + 4], bits[0], bits[1])
        parts = regrouped(mine, regroup, bits[1], groups, top)
        mine = call(middle_kernel, [block] * 4, (*parts, w1, g))
        done += exchange(mine, bits[2], bits[3])

    out = call(last_kernel, jax.ShapeDtypeStruct((whole, 128), BF), (*done, w), scratch=[turned, spread])
    return out.reshape(-1, 2, 128).transpose(1, 0, 2).reshape(state.shape)


def solution(mesh):
    placed = (P(None, ("hi", "lo")), P(), P())
    return jax.shard_map(
        on_device, mesh=mesh, in_specs=placed, out_specs=P(None, ("hi", "lo")), check_vma=False
    )
```

```python
import functools

import jax
import jax.numpy as jnp
from jax import lax
from jax.experimental import pallas as pl
from jax.experimental.pallas import tpu as pltpu
from jax.sharding import PartitionSpec as P

GQ = 6
G = 2**GQ
HALF = G // 2
BF = jnp.bfloat16
F32 = jnp.float32


def iotas(rows, columns):
    shape = (rows, columns)
    return lax.broadcasted_iota(jnp.int32, shape, 0), lax.broadcasted_iota(jnp.int32, shape, 1)


def dot(x, y):
    return jnp.dot(x, y, preferred_element_type=F32)


def turned_dot(x, y):
    return lax.dot_general(x, y, (((1,), (1,)), ((), ())), preferred_element_type=F32)


def ones(where):
    return where.astype(F32).astype(BF)


def gate_of(ref, layer, block):
    return jnp.concatenate([ref[layer, block, 0], ref[layer, block, 1]], axis=1)


def squared(gate):
    return jnp.concatenate([gate, jnp.concatenate([-gate[:, G:], gate[:, :G]], axis=1)], axis=0)


def product(later, earlier):
    return dot(later, squared(earlier))


def wide_product(later, earlier):
    parts = []
    for x in (later, squared(earlier)):
        high = x.astype(BF)
        parts.append((high, (x - high.astype(F32)).astype(BF)))
    (lh, ll), (eh, el) = parts
    return dot(jnp.concatenate([lh, lh, ll], axis=1), jnp.concatenate([eh, el, eh], axis=0))


def first_weights(gate):
    real = jnp.concatenate([gate[:, :G], gate[:, :G]], axis=1)
    imag = jnp.concatenate([gate[:, G:], gate[:, G:]], axis=1)
    low = iotas(HALF, 2 * G)[1] < G
    rows = []
    for ch in range(2):
        r, i = (x[ch * HALF : (ch + 1) * HALF] for x in (real, imag))
        for pair in ((r, -i), (i, r)):
            for mask in (low, ~low):
                rows.append(jnp.concatenate([jnp.where(mask, x, 0.0) for x in pair], axis=1))
    return jnp.concatenate(rows, axis=0).astype(BF)


def right_weights(gate, low, in_bit, out_bit):
    k, b = iotas(G, G)
    order = ((k & (HALF - 1)) << 1 | k >> GQ - 1) if low else k ^ in_bit * HALF
    gate = gate.astype(BF)
    t = turned_dot(ones(b == order), jnp.concatenate([gate[:, :G], gate[:, G:]], axis=0)).astype(BF)
    at, n = iotas(2 * G, 8 * G)
    bit = lambda i: n >> i & 1
    to = ((bit(7) ^ out_bit) << GQ - 1) | n & (HALF - 1)
    turn_i = bit(8)
    part = bit(5) ^ turn_i
    sign_i = turn_i & (1 - bit(5))
    ch = iotas(G, 8 * G)[1] >> 6 & 1
    made = []
    for p in range(2):
        minus = sign_i ^ ((1 - part) & p)
        place = jnp.where(at == to + (part ^ p) * G, (1 - 2 * minus).astype(F32), 0.0).astype(BF)
        y = dot(t, place)
        made.append([jnp.where(ch == c, y, 0.0).astype(BF) for c in range(2)])
    if low:
        rows = [made[p][c] for c in range(2) for p in range(2)]
    else:
        rows = [made[p][c][i * HALF : (i + 1) * HALF] for i in range(2) for c in range(2) for p in range(2)]
    return jnp.concatenate(rows, axis=0)


def left_weights(gate, step, out_bit):
    k, a = iotas(G, G)
    rows = dot(ones(a == k ^ out_bit * HALF), gate.astype(BF)).astype(BF)
    k, a = iotas(2 * G, 2 * G)
    return dot(rows, ones(a == k ^ step)).astype(BF)


def last_weights(gate, in_bit):
    k, b = iotas(G, G)
    t = dot(ones(b == ((k & (HALF - 1)) << 1 | k >> GQ - 1)), gate).astype(BF)
    at, n = iotas(2 * G, 4 * G)
    p_in = n >> 5 & 1
    b_in = ((n >> 7 ^ in_bit) << GQ - 1) | n & (HALF - 1)
    ch = iotas(HALF, 4 * G)[1] >> 6 & 1
    rows = []
    for p in range(2):
        minus = (1 - p) * p_in
        place = jnp.where(at == b_in + (p_in ^ p) * G, (1 - 2 * minus).astype(F32), 0.0).astype(BF)
        y = dot(t, place)
        for b0 in range(2):
            for c in range(2):
                rows.append(jnp.where(ch == c, y[b0 * HALF : (b0 + 1) * HALF], 0.0).astype(BF))
    return jnp.concatenate(rows, axis=0)


def turn(parts):
    lane = lax.broadcasted_iota(jnp.int32, (parts[0].shape[0], 128), 1)
    wide = lane < 64
    narrow = (lane & 32) == 0
    out = [[None, None] for _ in range(8)]
    for n in range(2):
        for m in range(2):
            a = [parts[n * 4 + r][:, m * 128 : (m + 1) * 128] for r in range(4)]
            s = [None] * 4
            for r in range(2):
                s[r] = jnp.where(wide, a[r], pltpu.roll(a[r + 2], 64, 1))
                s[r + 2] = jnp.where(wide, pltpu.roll(a[r], 64, 1), a[r + 2])
            for r in (0, 2):
                out[m * 4 + r][n] = jnp.where(narrow, s[r], pltpu.roll(s[r + 1], 32, 1))
                out[m * 4 + r + 1][n] = jnp.where(narrow, pltpu.roll(s[r], 96, 1), s[r + 1])
    return out


def both_gates(x, w, g):
    n = x.shape[0]
    z = jnp.dot(x.reshape(n * G, 4 * G), w, preferred_element_type=F32).astype(BF)
    outs = []
    for k in range(n):
        rows = z[k * G : (k + 1) * G]
        s = jnp.concatenate([rows[:, : 4 * G], rows[:, 4 * G :]], axis=0)
        outs.append(jnp.dot(g, s, preferred_element_type=F32).astype(BF))
    return outs


PLACES = ((1, 0), (1, 1), (0, 1), (0, 0))
APART = (2, 3, 1, 0)


def by_place(blocks):
    return dict(zip(PLACES, blocks))


def store_blocks(outs, at, blocks):
    blocks = by_place(blocks)
    for k, out in enumerate(outs):
        for i in range(2):
            for j in range(2):
                blocks[i, j][at + k] = out[j * HALF : (j + 1) * HALF, i * 128 : (i + 1) * 128]


STEP = 4
EARLY = 12


def own_bits():
    hi_bits = lax.axis_size("hi").bit_length() - 1
    hi = lax.axis_index("hi")
    return [hi >> k % hi_bits & 1 for k in range(4)]


def first_kernel(x_ref, gates, *refs):
    *outs, spread, turned, w1_ref = refs
    early = outs[0].shape[0]
    own = own_bits()
    late = product(gate_of(gates, 3, 0), gate_of(gates, 2, 0))
    soon = product(gate_of(gates, 1, 0), gate_of(gates, 0, 0))
    w0 = first_weights(wide_product(late, soon))
    w1_ref[...] = right_weights(gate_of(gates, 0, 1), True, 0, own[0])
    g = left_weights(product(gate_of(gates, 1, 2), gate_of(gates, 0, 2)), 0, own[1])

    for k in range(G // 8):
        spread[k * 512 : (k + 1) * 512, :] = x_ref[k * 512 : (k + 1) * 512, :].astype(F32)
        x = jnp.concatenate([spread[pl.ds(k * 512 + p, 256, stride=2), :] for p in range(2)], axis=1).astype(BF)
        r = turned_dot(w0, x)
        tiles = turn([r[g * HALF : (g + 1) * HALF] for g in range(8)])
        for q in range(8):
            for n in range(2):
                turned[n, pl.ds(k * 8 + q, HALF, stride=G), :] = tiles[q][n]

    for k in range(0, HALF, STEP):
        rows = slice(k * G, (k + STEP) * G)
        x = jnp.concatenate([turned[0, rows, :], turned[1, rows, :]], axis=1).astype(BF).reshape(STEP, G, 4 * G)
        made = both_gates(x, w1_ref[...], g)
        if k >= early:
            store_blocks(made, k - early, outs[4:])
        else:
            store_blocks(made, k, outs[:4])


def lanes_kernel(b0, b1, b2, b3, w1_ref, moving, staying):
    blocks = by_place((b0, b1, b2, b3))
    w = w1_ref[:, : 4 * G]
    for j in range(2):
        for k in range(0, b0.shape[0], STEP):
            x = jnp.concatenate([blocks[i, j][k : k + STEP] for i in range(2)], axis=2).reshape(STEP * HALF, 4 * G)
            y = dot(x, w).astype(BF)
            staying[j, k : k + STEP] = y[:, :128].reshape(STEP, HALF, 128)
            moving[j, k : k + STEP] = y[:, 128:].reshape(STEP, HALF, 128)


def rows_kernel(*refs):
    *ins, w1_ref, g_ref, m0, m1, s0, s1 = refs
    for k in range(0, m0.shape[0], STEP):
        made = both_gates(joined(ins, k), w1_ref[...], g_ref[...])
        for at, out in enumerate(made):
            for i in range(2):
                lanes = slice(i * 128, (i + 1) * 128)
                (s0, s1)[i][k + at] = out[:HALF, lanes]
                (m0, m1)[i][k + at] = out[HALF:, lanes]


def weights_kernel(top, gates, w1_ref, i_ref, g_ref, w_ref):
    own = own_bits()
    w1_ref[...] = right_weights(product(gate_of(gates, 2, 1), gate_of(gates, 1, 1)), False, own[0], own[2])
    k, a = iotas(G, 2 * G)
    i_ref[...] = right_weights(ones(k == a), False, 0, 0)
    step = top * lax.axis_index("lo") if top else 0
    g_ref[...] = left_weights(product(gate_of(gates, 3, 2), gate_of(gates, 2, 2)), step, own[3])
    w_ref[...] = last_weights(gate_of(gates, 3, 1), own[2])


def joined(ins, k):
    order = [APART.index(o) for o in range(4)] if len(ins) > 1 else [0]
    halves = [jnp.concatenate([ins[at][i, k : k + STEP] for at in order], axis=1) for i in range(2)]
    return jnp.concatenate(halves, axis=2)


def middle_kernel(*refs):
    *ins, w1_ref, g_ref, o0, o1, o2, o3 = refs
    for k in range(0, o0.shape[0], STEP):
        store_blocks(both_gates(joined(ins, k), w1_ref[...], g_ref[...]), k, (o0, o1, o2, o3))


def last_kernel(m0, m1, s0, s1, b0, b1, b2, b3, w_ref, o_ref, wide, spread):
    bit = own_bits()[3]
    blocks = by_place((b0, b1, b2, b3))
    early = m0.shape[0]
    firsts = ((s0, m0), (s1, m1))
    for k in range(HALF):
        for j in range(2):
            rows = pl.ds(pl.multiple_of(k * G + (bit ^ j) * HALF, HALF), HALF)
            for i in range(2):
                block = blocks[i, j][k - early] if k >= early else firsts[i][j][k]
                wide[i, rows, :] = block.astype(F32)
    for k in range(G // 8):
        halves = [
            jnp.concatenate([wide[i, pl.ds(k * 8 + q, HALF, stride=G), :] for q in range(8)], axis=0) for i in range(2)
        ]
        x = jnp.concatenate(halves, axis=1).astype(BF)
        r = turned_dot(w_ref[...], x)
        tiles = turn([r[g * HALF : (g + 1) * HALF] for g in range(8)])
        for q in range(8):
            for n in range(2):
                spread[pl.ds((k * 8 + q) * G + n, HALF, stride=2), :] = tiles[q][n]
        o_ref[k * 512 : (k + 1) * 512, :] = spread[k * 512 : (k + 1) * 512, :].astype(BF)


def pick_kernel(groups, regroup, *refs):
    ins, outs = refs[:-groups], refs[-groups:]
    if len(ins) == 4:
        blocks = by_place(ins)
    else:
        moved, stayed = ins
        blocks = {(i, j): (stayed, moved)[i].at[j] for i, j in PLACES}
    own = own_bits()[1]
    lo = lax.axis_index("lo")
    rows = outs[0].shape[2]
    for o, out in zip(APART, outs):
        t = regroup[lo ^ o]
        j = t >> 1 ^ own
        at = pl.ds(pl.multiple_of((t & 1) * rows, rows), rows)
        for i in range(2):
            out[i] = jnp.where(j == 0, blocks[i, 0][:, at, :], blocks[i, 1][:, at, :])


VMEM = pl.BlockSpec(memory_space=pltpu.VMEM)
SMEM = pl.BlockSpec(memory_space=pltpu.SMEM)


def call(kernel, outs, args, specs=None, scratch=(), after=()):
    specs = specs or [VMEM] * len(args)

    def body(*refs):
        kernel(*refs[: len(args)], *refs[len(args) + len(after) :])

    return pl.pallas_call(
        body,
        out_shape=outs,
        in_specs=specs + [pl.BlockSpec(memory_space=pl.ANY)] * len(after),
        out_specs=jax.tree.map(lambda _: VMEM, outs),
        scratch_shapes=scratch,
        cost_estimate=pl.CostEstimate(flops=1, bytes_accessed=1, transcendentals=0),
        compiler_params=pltpu.CompilerParams(vmem_limit_bytes=40 * 2**20),
    )(*args, *after)


def swapped(x, apart):
    return lax.ppermute(x, "hi", [(d, d ^ apart) for d in range(lax.axis_size("hi"))])


def exchange(blocks, b_bit, a_bit):
    out = []
    for (i, j), block in zip(PLACES, blocks):
        apart = i << b_bit | j << a_bit
        out.append(swapped(block, apart) if apart else block)
    return out


def regrouped(blocks, regroup, bit, groups, top, after=()):
    count = blocks[0].shape[-3]
    if groups == 4:
        part = jax.ShapeDtypeStruct((2, count, top, 128), BF)
        parts = call(functools.partial(pick_kernel, groups), [part] * groups, (regroup, *blocks), [SMEM] + [VMEM] * len(blocks), after=after)
        pairs = [[(d, d ^ o) for d in range(groups)] for o in APART]
        return [lax.ppermute(x, "lo", to) if o else x for o, x, to in zip(APART, parts, pairs)]
    own = lax.axis_index("hi") >> bit & 1
    if len(blocks) == 4:
        blocks = by_place(blocks)
        halves = [jnp.stack([blocks[i, 0], blocks[i, 1]], axis=1) for i in range(2)]
    else:
        halves = [jnp.moveaxis(x, 0, 1) for x in blocks[::-1]]
    both = jnp.stack([jnp.where(own == 0, half, jnp.flip(half, 1)) for half in halves])
    both = jnp.take(both.reshape(2, count, groups, top, 128), regroup, axis=2)
    both = lax.all_to_all(both, "lo", split_axis=2, concat_axis=2, tiled=True)
    return [both.reshape(2, count, G, 128)]


def on_device(state, gates, regroup):
    hi_bits = lax.axis_size("hi").bit_length() - 1
    groups = lax.axis_size("lo")
    bits = [k % hi_bits for k in range(4)]
    top = G // groups
    whole = 2 * state.shape[1] // 128

    block = jax.ShapeDtypeStruct((HALF - EARLY, HALF, 128), BF)
    early_block = jax.ShapeDtypeStruct((EARLY, HALF, 128), BF)
    early_half = jax.ShapeDtypeStruct((2, EARLY, HALF, 128), BF)
    turned = pltpu.VMEM((2, HALF * G, 128), F32)
    spread = pltpu.VMEM((whole, 128), F32)
    lanes, rows = (4 * G, 8 * G), (G, 2 * G)

    x = state.reshape(2, -1, 128).transpose(1, 0, 2).reshape(whole, 128)
    scratch = [spread, turned, pltpu.VMEM(lanes, BF)]
    made = call(first_kernel, [early_block] * 4 + [block] * 4, (x, gates), scratch=scratch)
    early = exchange(made[:4], bits[0], bits[1])
    late = exchange(made[4:], bits[0], bits[1])
    shapes = [jax.ShapeDtypeStruct(shape, BF) for shape in (lanes, lanes, rows, (4 * G, 4 * G))]
    w1, w_i, g, w = call(functools.partial(weights_kernel, top if groups == 4 else 0), shapes, (gates,))

    moving, staying = call(lanes_kernel, [early_half] * 2, (*early, w1))
    early = [swapped(moving, 1 << bits[2]), staying]

    late = regrouped(late, regroup, bits[1], groups, top, after=[staying])
    late = call(middle_kernel, [block] * 4, (*late, w1, g))
    sent = late[3:]
    late = exchange(late, bits[2], bits[3])

    early = regrouped(early, regroup, bits[1], groups, top, after=sent)
    m0, m1, *early = call(rows_kernel, [early_block] * 4, (*early, w_i, g))
    early = [swapped(m0, 1 << bits[3]), swapped(m1, 1 << bits[3]), *early]

    args = (*early, *late, w)
    out = call(last_kernel, jax.ShapeDtypeStruct((whole, 128), BF), args, scratch=[turned, spread])
    return out.reshape(-1, 2, 128).transpose(1, 0, 2).reshape(state.shape)


def solution(mesh):
    placed = (P(None, ("hi", "lo")), P(), P())
    return jax.shard_map(
        on_device, mesh=mesh, in_specs=placed, out_specs=P(None, ("hi", "lo")), check_vma=False
    )
```

```python
import functools

import jax
import jax.numpy as jnp
from jax import lax
from jax.experimental import pallas as pl
from jax.experimental.pallas import tpu as pltpu
from jax.sharding import PartitionSpec as P

GQ = 6
G = 2**GQ
HALF = G // 2
BF = jnp.bfloat16
F32 = jnp.float32


def iotas(rows, columns):
    shape = (rows, columns)
    return lax.broadcasted_iota(jnp.int32, shape, 0), lax.broadcasted_iota(jnp.int32, shape, 1)


def dot(x, y):
    return jnp.dot(x, y, preferred_element_type=F32)


def turned_dot(x, y):
    return lax.dot_general(x, y, (((1,), (1,)), ((), ())), preferred_element_type=F32)


def ones(where):
    return where.astype(F32).astype(BF)


def gate_of(ref, layer, block):
    return jnp.concatenate([ref[layer, block, 0], ref[layer, block, 1]], axis=1)


def squared(gate):
    return jnp.concatenate([gate, jnp.concatenate([-gate[:, G:], gate[:, :G]], axis=1)], axis=0)


def product(later, earlier):
    return dot(later, squared(earlier))


def wide_product(later, earlier):
    parts = []
    for x in (later, squared(earlier)):
        high = x.astype(BF)
        parts.append((high, (x - high.astype(F32)).astype(BF)))
    (lh, ll), (eh, el) = parts
    return dot(jnp.concatenate([lh, lh, ll], axis=1), jnp.concatenate([eh, el, eh], axis=0))


def first_weights(gate):
    real = jnp.concatenate([gate[:, :G], gate[:, :G]], axis=1)
    imag = jnp.concatenate([gate[:, G:], gate[:, G:]], axis=1)
    low = iotas(HALF, 2 * G)[1] < G
    rows = []
    for ch in range(2):
        r, i = (x[ch * HALF : (ch + 1) * HALF] for x in (real, imag))
        for pair in ((r, -i), (i, r)):
            for mask in (low, ~low):
                rows.append(jnp.concatenate([jnp.where(mask, x, 0.0) for x in pair], axis=1))
    return jnp.concatenate(rows, axis=0).astype(BF)


def right_weights(gate, low, in_bit, out_bit):
    k, b = iotas(G, G)
    order = ((k & (HALF - 1)) << 1 | k >> GQ - 1) if low else k ^ in_bit * HALF
    gate = gate.astype(BF)
    t = turned_dot(ones(b == order), jnp.concatenate([gate[:, :G], gate[:, G:]], axis=0)).astype(BF)
    at, n = iotas(2 * G, 8 * G)
    bit = lambda i: n >> i & 1
    to = ((bit(7) ^ out_bit) << GQ - 1) | n & (HALF - 1)
    turn_i = bit(8)
    part = bit(5) ^ turn_i
    sign_i = turn_i & (1 - bit(5))
    ch = iotas(G, 8 * G)[1] >> 6 & 1
    made = []
    for p in range(2):
        minus = sign_i ^ ((1 - part) & p)
        place = jnp.where(at == to + (part ^ p) * G, (1 - 2 * minus).astype(F32), 0.0).astype(BF)
        y = dot(t, place)
        made.append([jnp.where(ch == c, y, 0.0).astype(BF) for c in range(2)])
    if low:
        rows = [made[p][c] for c in range(2) for p in range(2)]
    else:
        rows = [made[p][c][i * HALF : (i + 1) * HALF] for i in range(2) for c in range(2) for p in range(2)]
    return jnp.concatenate(rows, axis=0)


def left_weights(gate, step, out_bit):
    k, a = iotas(G, G)
    rows = dot(ones(a == k ^ out_bit * HALF), gate.astype(BF)).astype(BF)
    k, a = iotas(2 * G, 2 * G)
    return dot(rows, ones(a == k ^ step)).astype(BF)


def last_weights(gate, in_bit):
    k, b = iotas(G, G)
    t = dot(ones(b == ((k & (HALF - 1)) << 1 | k >> GQ - 1)), gate).astype(BF)
    at, n = iotas(2 * G, 4 * G)
    p_in = n >> 5 & 1
    b_in = ((n >> 7 ^ in_bit) << GQ - 1) | n & (HALF - 1)
    ch = iotas(HALF, 4 * G)[1] >> 6 & 1
    rows = []
    for p in range(2):
        minus = (1 - p) * p_in
        place = jnp.where(at == b_in + (p_in ^ p) * G, (1 - 2 * minus).astype(F32), 0.0).astype(BF)
        y = dot(t, place)
        for b0 in range(2):
            for c in range(2):
                rows.append(jnp.where(ch == c, y[b0 * HALF : (b0 + 1) * HALF], 0.0).astype(BF))
    return jnp.concatenate(rows, axis=0)


def turn(parts):
    lane = lax.broadcasted_iota(jnp.int32, (parts[0].shape[0], 128), 1)
    wide = lane < 64
    narrow = (lane & 32) == 0
    out = [[None, None] for _ in range(8)]
    for n in range(2):
        for m in range(2):
            a = [parts[n * 4 + r][:, m * 128 : (m + 1) * 128] for r in range(4)]
            s = [None] * 4
            for r in range(2):
                s[r] = jnp.where(wide, a[r], pltpu.roll(a[r + 2], 64, 1))
                s[r + 2] = jnp.where(wide, pltpu.roll(a[r], 64, 1), a[r + 2])
            for r in (0, 2):
                out[m * 4 + r][n] = jnp.where(narrow, s[r], pltpu.roll(s[r + 1], 32, 1))
                out[m * 4 + r + 1][n] = jnp.where(narrow, pltpu.roll(s[r], 96, 1), s[r + 1])
    return out


def both_gates(x, w, g):
    n = x.shape[0]
    z = jnp.dot(x.reshape(n * G, 4 * G), w, preferred_element_type=F32).astype(BF)
    outs = []
    for k in range(n):
        rows = z[k * G : (k + 1) * G]
        s = jnp.concatenate([rows[:, : 4 * G], rows[:, 4 * G :]], axis=0)
        outs.append(jnp.dot(g, s, preferred_element_type=F32).astype(BF))
    return outs


PLACES = ((1, 0), (1, 1), (0, 1), (0, 0))
APART = (2, 3, 1, 0)


def by_place(blocks):
    return dict(zip(PLACES, blocks))


def store_blocks(outs, at, blocks):
    blocks = by_place(blocks)
    for k, out in enumerate(outs):
        for i in range(2):
            for j in range(2):
                blocks[i, j][at + k] = out[j * HALF : (j + 1) * HALF, i * 128 : (i + 1) * 128]


STEP = 8
EARLY = 12
COST = 2 * 10**9


def own_bits():
    hi_bits = lax.axis_size("hi").bit_length() - 1
    hi = lax.axis_index("hi")
    return [hi >> k % hi_bits & 1 for k in range(4)]


def steps(size):
    return [(k, min(STEP, size - k)) for k in range(0, size, STEP)]


def first_kernel(x_ref, gates, o0, o1, o2, o3, rest, w1_ref, g_ref, spread, turned):
    early = o0.shape[0]
    own = own_bits()
    late = product(gate_of(gates, 3, 0), gate_of(gates, 2, 0))
    soon = product(gate_of(gates, 1, 0), gate_of(gates, 0, 0))
    w0 = first_weights(wide_product(late, soon))
    w1_ref[...] = right_weights(gate_of(gates, 0, 1), True, 0, own[0])
    g_ref[...] = left_weights(product(gate_of(gates, 1, 2), gate_of(gates, 0, 2)), 0, own[1])

    for k in range(G // 8):
        spread[k * 512 : (k + 1) * 512, :] = x_ref[k * 512 : (k + 1) * 512, :].astype(F32)
        x = jnp.concatenate([spread[pl.ds(k * 512 + p, 256, stride=2), :] for p in range(2)], axis=1).astype(BF)
        r = turned_dot(w0, x)
        tiles = turn([r[g * HALF : (g + 1) * HALF] for g in range(8)])
        for q in range(8):
            for n in range(2):
                turned[n, pl.ds(k * 8 + q, HALF, stride=G), :] = tiles[q][n]

    for k, n in steps(early):
        rows = slice(k * G, (k + n) * G)
        x = jnp.concatenate([turned[0, rows, :], turned[1, rows, :]], axis=1).astype(BF).reshape(n, G, 4 * G)
        store_blocks(both_gates(x, w1_ref[...], g_ref[...]), k, (o0, o1, o2, o3))
    for n in range(2):
        rest[n] = turned[n, early * G :, :].astype(BF)


def second_kernel(rest, w1_ref, g_ref, o0, o1, o2, o3):
    for k, n in steps(o0.shape[0]):
        rows = slice(k * G, (k + n) * G)
        x = jnp.concatenate([rest[0, rows, :], rest[1, rows, :]], axis=1).reshape(n, G, 4 * G)
        store_blocks(both_gates(x, w1_ref[...], g_ref[...]), k, (o0, o1, o2, o3))


def lanes_kernel(b0, b1, b2, b3, w1_ref, moving, staying):
    blocks = by_place((b0, b1, b2, b3))
    w = w1_ref[:, : 4 * G]
    for j in range(2):
        for k, n in steps(b0.shape[0]):
            x = jnp.concatenate([blocks[i, j][k : k + n] for i in range(2)], axis=2).reshape(n * HALF, 4 * G)
            y = dot(x, w).astype(BF)
            staying[j, k : k + n] = y[:, :128].reshape(n, HALF, 128)
            moving[j, k : k + n] = y[:, 128:].reshape(n, HALF, 128)


def rows_kernel(*refs):
    *ins, w1_ref, g_ref, m0, m1, s0, s1 = refs
    for k, n in steps(m0.shape[0]):
        made = both_gates(joined(ins, k, n), w1_ref[...], g_ref[...])
        for at, out in enumerate(made):
            for i in range(2):
                lanes = slice(i * 128, (i + 1) * 128)
                (s0, s1)[i][k + at] = out[:HALF, lanes]
                (m0, m1)[i][k + at] = out[HALF:, lanes]


def weights_kernel(top, gates, w1_ref, i_ref, g_ref, w_ref):
    own = own_bits()
    w1_ref[...] = right_weights(product(gate_of(gates, 2, 1), gate_of(gates, 1, 1)), False, own[0], own[2])
    k, a = iotas(G, 2 * G)
    i_ref[...] = right_weights(ones(k == a), False, 0, 0)
    step = top * lax.axis_index("lo") if top else 0
    g_ref[...] = left_weights(product(gate_of(gates, 3, 2), gate_of(gates, 2, 2)), step, own[3])
    w_ref[...] = last_weights(gate_of(gates, 3, 1), own[2])


def joined(ins, k, n):
    order = [APART.index(o) for o in range(4)] if len(ins) > 1 else [0]
    halves = [jnp.concatenate([ins[at][i, k : k + n] for at in order], axis=1) for i in range(2)]
    return jnp.concatenate(halves, axis=2)


def middle_kernel(*refs):
    *ins, w1_ref, g_ref, o0, o1, o2, o3 = refs
    for k, n in steps(o0.shape[0]):
        store_blocks(both_gates(joined(ins, k, n), w1_ref[...], g_ref[...]), k, (o0, o1, o2, o3))


def last_kernel(m0, m1, s0, s1, b0, b1, b2, b3, w_ref, o_ref, wide, spread):
    bit = own_bits()[3]
    blocks = by_place((b0, b1, b2, b3))
    early = m0.shape[0]
    firsts = ((s0, m0), (s1, m1))
    for k in range(HALF):
        for j in range(2):
            rows = pl.ds(pl.multiple_of(k * G + (bit ^ j) * HALF, HALF), HALF)
            for i in range(2):
                block = blocks[i, j][k - early] if k >= early else firsts[i][j][k]
                wide[i, rows, :] = block.astype(F32)
    for k in range(G // 8):
        halves = [
            jnp.concatenate([wide[i, pl.ds(k * 8 + q, HALF, stride=G), :] for q in range(8)], axis=0) for i in range(2)
        ]
        x = jnp.concatenate(halves, axis=1).astype(BF)
        r = turned_dot(w_ref[...], x)
        tiles = turn([r[g * HALF : (g + 1) * HALF] for g in range(8)])
        for q in range(8):
            for n in range(2):
                spread[pl.ds((k * 8 + q) * G + n, HALF, stride=2), :] = tiles[q][n]
        o_ref[k * 512 : (k + 1) * 512, :] = spread[k * 512 : (k + 1) * 512, :].astype(BF)


def pick_kernel(groups, regroup, *refs):
    ins, outs = refs[:-groups], refs[-groups:]
    if len(ins) == 4:
        blocks = by_place(ins)
    else:
        moved, stayed = ins
        blocks = {(i, j): (stayed, moved)[i].at[j] for i, j in PLACES}
    own = own_bits()[1]
    lo = lax.axis_index("lo")
    rows = outs[0].shape[2]
    for o, out in zip(APART, outs):
        t = regroup[lo ^ o]
        j = t >> 1 ^ own
        at = pl.ds(pl.multiple_of((t & 1) * rows, rows), rows)
        for i in range(2):
            out[i] = jnp.where(j == 0, blocks[i, 0][:, at, :], blocks[i, 1][:, at, :])


VMEM = pl.BlockSpec(memory_space=pltpu.VMEM)
SMEM = pl.BlockSpec(memory_space=pltpu.SMEM)


def call(kernel, outs, args, specs=None, scratch=(), after=(), flops=1):
    specs = specs or [VMEM] * len(args)

    def body(*refs):
        kernel(*refs[: len(args)], *refs[len(args) + len(after) :])

    return pl.pallas_call(
        body,
        out_shape=outs,
        in_specs=specs + [pl.BlockSpec(memory_space=pl.ANY)] * len(after),
        out_specs=jax.tree.map(lambda _: VMEM, outs),
        scratch_shapes=scratch,
        cost_estimate=pl.CostEstimate(flops=flops, bytes_accessed=1, transcendentals=0),
        compiler_params=pltpu.CompilerParams(vmem_limit_bytes=40 * 2**20),
    )(*args, *after)


def swapped(x, apart):
    return lax.ppermute(x, "hi", [(d, d ^ apart) for d in range(lax.axis_size("hi"))])


def exchange(blocks, b_bit, a_bit):
    out = []
    for (i, j), block in zip(PLACES, blocks):
        apart = i << b_bit | j << a_bit
        out.append(swapped(block, apart) if apart else block)
    return out


def regrouped(blocks, regroup, bit, groups, top, after=()):
    count = blocks[0].shape[-3]
    if groups == 4:
        part = jax.ShapeDtypeStruct((2, count, top, 128), BF)
        parts = call(functools.partial(pick_kernel, groups), [part] * groups, (regroup, *blocks), [SMEM] + [VMEM] * len(blocks), after=after)
        pairs = [[(d, d ^ o) for d in range(groups)] for o in APART]
        return [lax.ppermute(x, "lo", to) if o else x for o, x, to in zip(APART, parts, pairs)]
    own = lax.axis_index("hi") >> bit & 1
    if len(blocks) == 4:
        blocks = by_place(blocks)
        halves = [jnp.stack([blocks[i, 0], blocks[i, 1]], axis=1) for i in range(2)]
    else:
        halves = [jnp.moveaxis(x, 0, 1) for x in blocks[::-1]]
    both = jnp.stack([jnp.where(own == 0, half, jnp.flip(half, 1)) for half in halves])
    both = jnp.take(both.reshape(2, count, groups, top, 128), regroup, axis=2)
    both = lax.all_to_all(both, "lo", split_axis=2, concat_axis=2, tiled=True)
    return [both.reshape(2, count, G, 128)]


def on_device(state, gates, regroup):
    hi_bits = lax.axis_size("hi").bit_length() - 1
    groups = lax.axis_size("lo")
    bits = [k % hi_bits for k in range(4)]
    top = G // groups
    whole = 2 * state.shape[1] // 128

    block = jax.ShapeDtypeStruct((HALF - EARLY, HALF, 128), BF)
    early_block = jax.ShapeDtypeStruct((EARLY, HALF, 128), BF)
    early_half = jax.ShapeDtypeStruct((2, EARLY, HALF, 128), BF)
    turned = pltpu.VMEM((2, HALF * G, 128), F32)
    spread = pltpu.VMEM((whole, 128), F32)
    lanes, rows = (4 * G, 8 * G), (G, 2 * G)

    x = state.reshape(2, -1, 128).transpose(1, 0, 2).reshape(whole, 128)
    rest = jax.ShapeDtypeStruct((2, (HALF - EARLY) * G, 128), BF)
    *early, rest, w1, g = call(
        first_kernel,
        [early_block] * 4 + [rest, jax.ShapeDtypeStruct(lanes, BF), jax.ShapeDtypeStruct(rows, BF)],
        (x, gates),
        scratch=[spread, turned],
    )
    early = exchange(early, bits[0], bits[1])
    late = call(second_kernel, [block] * 4, (rest, w1, g))
    late = exchange(late, bits[0], bits[1])
    shapes = [jax.ShapeDtypeStruct(shape, BF) for shape in (lanes, lanes, rows, (4 * G, 4 * G))]
    w1, w_i, g, w = call(functools.partial(weights_kernel, top if groups == 4 else 0), shapes, (gates,))

    moving, staying = call(lanes_kernel, [early_half] * 2, (*early, w1), flops=COST)
    early = [swapped(moving, 1 << bits[2]), staying]

    late = regrouped(late, regroup, bits[1], groups, top, after=[staying])
    late = call(middle_kernel, [block] * 4, (*late, w1, g))
    sent = late[3:]
    late = exchange(late, bits[2], bits[3])

    early = regrouped(early, regroup, bits[1], groups, top, after=sent)
    m0, m1, *early = call(rows_kernel, [early_block] * 4, (*early, w_i, g), after=late[:1])
    early = [swapped(m0, 1 << bits[3]), swapped(m1, 1 << bits[3]), *early]

    args = (*early, *late, w)
    out = call(last_kernel, jax.ShapeDtypeStruct((whole, 128), BF), args, scratch=[turned, spread])
    return out.reshape(-1, 2, 128).transpose(1, 0, 2).reshape(state.shape)


def solution(mesh):
    placed = (P(None, ("hi", "lo")), P(), P())
    return jax.shard_map(
        on_device, mesh=mesh, in_specs=placed, out_specs=P(None, ("hi", "lo")), check_vma=False
    )
```

```python
import functools

import jax
import jax.numpy as jnp
from jax import lax
from jax.experimental import pallas as pl
from jax.experimental.pallas import tpu as pltpu
from jax.sharding import PartitionSpec as P

GQ = 6
G = 2**GQ
HALF = G // 2
BF = jnp.bfloat16
F32 = jnp.float32


def iotas(rows, columns):
    shape = (rows, columns)
    return lax.broadcasted_iota(jnp.int32, shape, 0), lax.broadcasted_iota(jnp.int32, shape, 1)


def dot(x, y):
    return jnp.dot(x, y, preferred_element_type=F32)


def turned_dot(x, y):
    return lax.dot_general(x, y, (((1,), (1,)), ((), ())), preferred_element_type=F32)


def ones(where):
    return where.astype(F32).astype(BF)


def gate_of(ref, layer, block):
    return jnp.concatenate([ref[layer, block, 0], ref[layer, block, 1]], axis=1)


def squared(gate):
    return jnp.concatenate([gate, jnp.concatenate([-gate[:, G:], gate[:, :G]], axis=1)], axis=0)


def product(later, earlier):
    return dot(later, squared(earlier))


def wide_product(later, earlier):
    parts = []
    for x in (later, squared(earlier)):
        high = x.astype(BF)
        parts.append((high, (x - high.astype(F32)).astype(BF)))
    (lh, ll), (eh, el) = parts
    return dot(jnp.concatenate([lh, lh, ll], axis=1), jnp.concatenate([eh, el, eh], axis=0))


def first_weights(gate):
    real = jnp.concatenate([gate[:, :G], gate[:, :G]], axis=1)
    imag = jnp.concatenate([gate[:, G:], gate[:, G:]], axis=1)
    low = iotas(HALF, 2 * G)[1] < G
    rows = []
    for ch in range(2):
        r, i = (x[ch * HALF : (ch + 1) * HALF] for x in (real, imag))
        for pair in ((r, -i), (i, r)):
            for mask in (low, ~low):
                rows.append(jnp.concatenate([jnp.where(mask, x, 0.0) for x in pair], axis=1))
    return jnp.concatenate(rows, axis=0).astype(BF)


def right_weights(gate, low, in_bit, out_bit):
    k, b = iotas(G, G)
    order = ((k & (HALF - 1)) << 1 | k >> GQ - 1) if low else k ^ in_bit * HALF
    gate = gate.astype(BF)
    t = turned_dot(ones(b == order), jnp.concatenate([gate[:, :G], gate[:, G:]], axis=0)).astype(BF)
    at, n = iotas(2 * G, 8 * G)
    bit = lambda i: n >> i & 1
    to = ((bit(7) ^ out_bit) << GQ - 1) | n & (HALF - 1)
    turn_i = bit(8)
    part = bit(5) ^ turn_i
    sign_i = turn_i & (1 - bit(5))
    ch = iotas(G, 8 * G)[1] >> 6 & 1
    made = []
    for p in range(2):
        minus = sign_i ^ ((1 - part) & p)
        place = jnp.where(at == to + (part ^ p) * G, (1 - 2 * minus).astype(F32), 0.0).astype(BF)
        y = dot(t, place)
        made.append([jnp.where(ch == c, y, 0.0).astype(BF) for c in range(2)])
    if low:
        rows = [made[p][c] for c in range(2) for p in range(2)]
    else:
        rows = [made[p][c][i * HALF : (i + 1) * HALF] for i in range(2) for c in range(2) for p in range(2)]
    return jnp.concatenate(rows, axis=0)


def left_weights(gate, step, out_bit):
    k, a = iotas(G, G)
    rows = dot(ones(a == k ^ out_bit * HALF), gate.astype(BF)).astype(BF)
    k, a = iotas(2 * G, 2 * G)
    return dot(rows, ones(a == k ^ step)).astype(BF)


def last_weights(gate, in_bit):
    k, b = iotas(G, G)
    t = dot(ones(b == ((k & (HALF - 1)) << 1 | k >> GQ - 1)), gate).astype(BF)
    at, n = iotas(2 * G, 4 * G)
    p_in = n >> 5 & 1
    b_in = ((n >> 7 ^ in_bit) << GQ - 1) | n & (HALF - 1)
    ch = iotas(HALF, 4 * G)[1] >> 6 & 1
    rows = []
    for p in range(2):
        minus = (1 - p) * p_in
        place = jnp.where(at == b_in + (p_in ^ p) * G, (1 - 2 * minus).astype(F32), 0.0).astype(BF)
        y = dot(t, place)
        for b0 in range(2):
            for c in range(2):
                rows.append(jnp.where(ch == c, y[b0 * HALF : (b0 + 1) * HALF], 0.0).astype(BF))
    return jnp.concatenate(rows, axis=0)


def turn(parts):
    lane = lax.broadcasted_iota(jnp.int32, (parts[0].shape[0], 128), 1)
    wide = lane < 64
    narrow = (lane & 32) == 0
    out = [[None, None] for _ in range(8)]
    for n in range(2):
        for m in range(2):
            a = [parts[n * 4 + r][:, m * 128 : (m + 1) * 128] for r in range(4)]
            s = [None] * 4
            for r in range(2):
                s[r] = jnp.where(wide, a[r], pltpu.roll(a[r + 2], 64, 1))
                s[r + 2] = jnp.where(wide, pltpu.roll(a[r], 64, 1), a[r + 2])
            for r in (0, 2):
                out[m * 4 + r][n] = jnp.where(narrow, s[r], pltpu.roll(s[r + 1], 32, 1))
                out[m * 4 + r + 1][n] = jnp.where(narrow, pltpu.roll(s[r], 96, 1), s[r + 1])
    return out


def both_gates(x, w, g):
    n = x.shape[0]
    z = jnp.dot(x.reshape(n * G, 4 * G), w, preferred_element_type=F32).astype(BF)
    outs = []
    for k in range(n):
        rows = z[k * G : (k + 1) * G]
        s = jnp.concatenate([rows[:, : 4 * G], rows[:, 4 * G :]], axis=0)
        outs.append(jnp.dot(g, s, preferred_element_type=F32).astype(BF))
    return outs


PLACES = ((1, 0), (1, 1), (0, 1), (0, 0))
APART = (2, 3, 1, 0)


def by_place(blocks):
    return dict(zip(PLACES, blocks))


def store_blocks(outs, at, blocks):
    blocks = by_place(blocks)
    for k, out in enumerate(outs):
        for i in range(2):
            for j in range(2):
                blocks[i, j][at + k] = out[j * HALF : (j + 1) * HALF, i * 128 : (i + 1) * 128]


STEP = 8
EARLY = 12
COST = 2 * 10**9


def own_bits():
    hi_bits = lax.axis_size("hi").bit_length() - 1
    hi = lax.axis_index("hi")
    return [hi >> k % hi_bits & 1 for k in range(4)]


def steps(size):
    return [(k, min(STEP, size - k)) for k in range(0, size, STEP)]


def first_kernel(x_ref, gates, o0, o1, o2, o3, rest, w1_ref, g_ref, spread, turned):
    early = o0.shape[0]
    own = own_bits()
    late = product(gate_of(gates, 3, 0), gate_of(gates, 2, 0))
    soon = product(gate_of(gates, 1, 0), gate_of(gates, 0, 0))
    w0 = first_weights(wide_product(late, soon))
    w1_ref[...] = right_weights(gate_of(gates, 0, 1), True, 0, own[0])
    g_ref[...] = left_weights(product(gate_of(gates, 1, 2), gate_of(gates, 0, 2)), 0, own[1])

    for k in range(G // 8):
        spread[k * 512 : (k + 1) * 512, :] = x_ref[k * 512 : (k + 1) * 512, :].astype(F32)
        x = jnp.concatenate([spread[pl.ds(k * 512 + p, 256, stride=2), :] for p in range(2)], axis=1).astype(BF)
        r = turned_dot(w0, x)
        tiles = turn([r[g * HALF : (g + 1) * HALF] for g in range(8)])
        for q in range(8):
            for n in range(2):
                turned[n, pl.ds(k * 8 + q, HALF, stride=G), :] = tiles[q][n]

    for k, n in steps(early):
        rows = slice(k * G, (k + n) * G)
        x = jnp.concatenate([turned[0, rows, :], turned[1, rows, :]], axis=1).astype(BF).reshape(n, G, 4 * G)
        store_blocks(both_gates(x, w1_ref[...], g_ref[...]), k, (o0, o1, o2, o3))
    for n in range(2):
        rest[n] = turned[n, early * G :, :].astype(BF)


def second_kernel(rest, w1_ref, g_ref, o0, o1, o2, o3):
    for k, n in steps(o0.shape[0]):
        rows = slice(k * G, (k + n) * G)
        x = jnp.concatenate([rest[0, rows, :], rest[1, rows, :]], axis=1).reshape(n, G, 4 * G)
        store_blocks(both_gates(x, w1_ref[...], g_ref[...]), k, (o0, o1, o2, o3))


def weights_kernel(top, gates, w1_ref, g_ref, w_ref):
    own = own_bits()
    w1_ref[...] = right_weights(product(gate_of(gates, 2, 1), gate_of(gates, 1, 1)), False, own[0], own[2])
    step = top * lax.axis_index("lo") if top else 0
    g_ref[...] = left_weights(product(gate_of(gates, 3, 2), gate_of(gates, 2, 2)), step, own[3])
    w_ref[...] = last_weights(gate_of(gates, 3, 1), own[2])


def joined(ins, k, n):
    order = [APART.index(o) for o in range(4)] if len(ins) > 1 else [0]
    halves = [jnp.concatenate([ins[at][i, k : k + n] for at in order], axis=1) for i in range(2)]
    return jnp.concatenate(halves, axis=2)


def middle_kernel(*refs):
    *ins, w1_ref, g_ref, o0, o1, o2, o3 = refs
    for k, n in steps(o0.shape[0]):
        store_blocks(both_gates(joined(ins, k, n), w1_ref[...], g_ref[...]), k, (o0, o1, o2, o3))


def gather_rows(first, ins, wide):
    bit = own_bits()[3]
    blocks = by_place(ins)
    for k in range(ins[0].shape[0]):
        for j in range(2):
            rows = pl.ds((bit ^ j) * (HALF * HALF) + first + k, HALF, stride=HALF)
            for i in range(2):
                wide[i, rows, :] = blocks[i, j][k].astype(F32)


def gather_kernel(b0, b1, b2, b3, wide):
    gather_rows(0, (b0, b1, b2, b3), wide)


def last_kernel(_, b0, b1, b2, b3, w_ref, o_ref, wide, spread):
    gather_rows(HALF - b0.shape[0], (b0, b1, b2, b3), wide)
    for k in range(G // 8):
        rows = slice(k * 256, (k + 1) * 256)
        x = jnp.concatenate([wide[i, rows, :] for i in range(2)], axis=1).astype(BF)
        r = turned_dot(w_ref[...], x)
        tiles = turn([r[g * HALF : (g + 1) * HALF] for g in range(8)])
        for q in range(8):
            for n in range(2):
                spread[pl.ds((k * 8 + q) * G + n, HALF, stride=2), :] = tiles[q][n]
        o_ref[k * 512 : (k + 1) * 512, :] = spread[k * 512 : (k + 1) * 512, :].astype(BF)


def pick_kernel(groups, regroup, *refs):
    ins, outs = refs[:-groups], refs[-groups:]
    blocks = by_place(ins)
    own = own_bits()[1]
    lo = lax.axis_index("lo")
    rows = outs[0].shape[2]
    for o, out in zip(APART, outs):
        t = regroup[lo ^ o]
        j = t >> 1 ^ own
        at = pl.ds(pl.multiple_of((t & 1) * rows, rows), rows)
        for i in range(2):
            out[i] = jnp.where(j == 0, blocks[i, 0][:, at, :], blocks[i, 1][:, at, :])


VMEM = pl.BlockSpec(memory_space=pltpu.VMEM)
SMEM = pl.BlockSpec(memory_space=pltpu.SMEM)


def call(kernel, outs, args, specs=None, scratch=(), after=(), flops=1, aliases={}):
    specs = specs or [VMEM] * len(args)

    def body(*refs):
        kernel(*refs[: len(args)], *refs[len(args) + len(after) :])

    return pl.pallas_call(
        body,
        out_shape=outs,
        in_specs=specs + [pl.BlockSpec(memory_space=pl.ANY)] * len(after),
        out_specs=jax.tree.map(lambda _: VMEM, outs),
        scratch_shapes=scratch,
        input_output_aliases=aliases,
        cost_estimate=pl.CostEstimate(flops=flops, bytes_accessed=1, transcendentals=0),
        compiler_params=pltpu.CompilerParams(vmem_limit_bytes=40 * 2**20),
    )(*args, *after)


def swapped(x, apart):
    return lax.ppermute(x, "hi", [(d, d ^ apart) for d in range(lax.axis_size("hi"))])


def exchange(blocks, b_bit, a_bit):
    out = []
    for (i, j), block in zip(PLACES, blocks):
        apart = i << b_bit | j << a_bit
        out.append(swapped(block, apart) if apart else block)
    return out


def regrouped(blocks, regroup, bit, groups, top, flops=1, after=()):
    count = blocks[0].shape[-3]
    if groups == 4:
        part = jax.ShapeDtypeStruct((2, count, top, 128), BF)
        parts = call(functools.partial(pick_kernel, groups), [part] * groups, (regroup, *blocks), [SMEM] + [VMEM] * 4, after=after, flops=flops)
        pairs = [[(d, d ^ o) for d in range(groups)] for o in APART]
        return [lax.ppermute(x, "lo", to) if o else x for o, x, to in zip(APART, parts, pairs)]
    own = lax.axis_index("hi") >> bit & 1
    blocks = by_place(blocks)
    halves = [jnp.stack([blocks[i, 0], blocks[i, 1]], axis=1) for i in range(2)]
    both = jnp.stack([jnp.where(own == 0, half, jnp.flip(half, 1)) for half in halves])
    both = jnp.take(both.reshape(2, count, groups, top, 128), regroup, axis=2)
    both = lax.all_to_all(both, "lo", split_axis=2, concat_axis=2, tiled=True)
    return [both.reshape(2, count, G, 128)]


def on_device(state, gates, regroup):
    hi_bits = lax.axis_size("hi").bit_length() - 1
    groups = lax.axis_size("lo")
    bits = [k % hi_bits for k in range(4)]
    top = G // groups
    whole = 2 * state.shape[1] // 128

    block = jax.ShapeDtypeStruct((HALF - EARLY, HALF, 128), BF)
    early_block = jax.ShapeDtypeStruct((EARLY, HALF, 128), BF)
    turned = pltpu.VMEM((2, HALF * G, 128), F32)
    spread = pltpu.VMEM((whole, 128), F32)
    lanes, rows = (4 * G, 8 * G), (G, 2 * G)

    x = state.reshape(2, -1, 128).transpose(1, 0, 2).reshape(whole, 128)
    rest = jax.ShapeDtypeStruct((2, (HALF - EARLY) * G, 128), BF)
    *early, rest, w1, g = call(
        first_kernel,
        [early_block] * 4 + [rest, jax.ShapeDtypeStruct(lanes, BF), jax.ShapeDtypeStruct(rows, BF)],
        (x, gates),
        scratch=[spread, turned],
    )
    early = exchange(early, bits[0], bits[1])
    late = call(second_kernel, [block] * 4, (rest, w1, g))
    late = exchange(late, bits[0], bits[1])
    shapes = [jax.ShapeDtypeStruct(shape, BF) for shape in (lanes, rows, (4 * G, 4 * G))]
    w1, g, w = call(functools.partial(weights_kernel, top if groups == 4 else 0), shapes, (gates,))

    early = regrouped(early, regroup, bits[1], groups, top, COST)
    late = regrouped(late, regroup, bits[1], groups, top, after=early[3:])
    early = call(middle_kernel, [early_block] * 4, (*early, w1, g), flops=COST)
    late = call(middle_kernel, [block] * 4, (*late, w1, g), after=early[3:])
    early = exchange(early, bits[2], bits[3])
    late = exchange(late, bits[2], bits[3])

    wide = jax.ShapeDtypeStruct((2, HALF * G, 128), F32)
    early = call(gather_kernel, wide, early, flops=COST)
    shapes = [jax.ShapeDtypeStruct((whole, 128), BF), wide]
    out, _ = call(last_kernel, shapes, (early, *late, w), scratch=[spread], aliases={0: 1})
    return out.reshape(-1, 2, 128).transpose(1, 0, 2).reshape(state.shape)


def solution(mesh):
    placed = (P(None, ("hi", "lo")), P(), P())
    return jax.shard_map(
        on_device, mesh=mesh, in_specs=placed, out_specs=P(None, ("hi", "lo")), check_vma=False
    )
```

```python
import functools

import jax
import jax.numpy as jnp
from jax import lax
from jax.experimental import pallas as pl
from jax.experimental.pallas import tpu as pltpu
from jax.sharding import PartitionSpec as P

GQ = 6
G = 2**GQ
HALF = G // 2
BF = jnp.bfloat16
F32 = jnp.float32


def iotas(rows, columns):
    shape = (rows, columns)
    return lax.broadcasted_iota(jnp.int32, shape, 0), lax.broadcasted_iota(jnp.int32, shape, 1)


def dot(x, y):
    return jnp.dot(x, y, preferred_element_type=F32)


def turned_dot(x, y):
    return lax.dot_general(x, y, (((1,), (1,)), ((), ())), preferred_element_type=F32)


def ones(where):
    return where.astype(F32).astype(BF)


def gate_of(ref, layer, block):
    return jnp.concatenate([ref[layer, block, 0], ref[layer, block, 1]], axis=1)


def squared(gate):
    return jnp.concatenate([gate, jnp.concatenate([-gate[:, G:], gate[:, :G]], axis=1)], axis=0)


def product(later, earlier):
    return dot(later, squared(earlier))


def wide_product(later, earlier):
    parts = []
    for x in (later, squared(earlier)):
        high = x.astype(BF)
        parts.append((high, (x - high.astype(F32)).astype(BF)))
    (lh, ll), (eh, el) = parts
    return dot(jnp.concatenate([lh, lh, ll], axis=1), jnp.concatenate([eh, el, eh], axis=0))


def first_weights(gate):
    real = jnp.concatenate([gate[:, :G], gate[:, :G]], axis=1)
    imag = jnp.concatenate([gate[:, G:], gate[:, G:]], axis=1)
    low = iotas(HALF, 2 * G)[1] < G
    rows = []
    for ch in range(2):
        r, i = (x[ch * HALF : (ch + 1) * HALF] for x in (real, imag))
        for pair in ((r, -i), (i, r)):
            for mask in (low, ~low):
                rows.append(jnp.concatenate([jnp.where(mask, x, 0.0) for x in pair], axis=1))
    return jnp.concatenate(rows, axis=0).astype(BF)


def right_weights(gate, low, in_bit, out_bit):
    k, b = iotas(G, G)
    order = ((k & (HALF - 1)) << 1 | k >> GQ - 1) if low else k ^ in_bit * HALF
    gate = gate.astype(BF)
    t = turned_dot(ones(b == order), jnp.concatenate([gate[:, :G], gate[:, G:]], axis=0)).astype(BF)
    at, n = iotas(2 * G, 8 * G)
    bit = lambda i: n >> i & 1
    to = ((bit(7) ^ out_bit) << GQ - 1) | n & (HALF - 1)
    turn_i = bit(8)
    part = bit(5) ^ turn_i
    sign_i = turn_i & (1 - bit(5))
    ch = iotas(G, 8 * G)[1] >> 6 & 1
    made = []
    for p in range(2):
        minus = sign_i ^ ((1 - part) & p)
        place = jnp.where(at == to + (part ^ p) * G, (1 - 2 * minus).astype(F32), 0.0).astype(BF)
        y = dot(t, place)
        made.append([jnp.where(ch == c, y, 0.0).astype(BF) for c in range(2)])
    if low:
        rows = [made[p][c] for c in range(2) for p in range(2)]
    else:
        rows = [made[p][c][i * HALF : (i + 1) * HALF] for i in range(2) for c in range(2) for p in range(2)]
    return jnp.concatenate(rows, axis=0)


def left_weights(gate, step, out_bit):
    k, a = iotas(G, G)
    rows = dot(ones(a == k ^ out_bit * HALF), gate.astype(BF)).astype(BF)
    k, a = iotas(2 * G, 2 * G)
    return dot(rows, ones(a == k ^ step)).astype(BF)


def last_weights(gate, in_bit):
    k, b = iotas(G, G)
    t = dot(ones(b == ((k & (HALF - 1)) << 1 | k >> GQ - 1)), gate).astype(BF)
    at, n = iotas(2 * G, 4 * G)
    p_in = n >> 5 & 1
    b_in = ((n >> 7 ^ in_bit) << GQ - 1) | n & (HALF - 1)
    ch = iotas(HALF, 4 * G)[1] >> 6 & 1
    rows = []
    for p in range(2):
        minus = (1 - p) * p_in
        place = jnp.where(at == b_in + (p_in ^ p) * G, (1 - 2 * minus).astype(F32), 0.0).astype(BF)
        y = dot(t, place)
        for b0 in range(2):
            for c in range(2):
                rows.append(jnp.where(ch == c, y[b0 * HALF : (b0 + 1) * HALF], 0.0).astype(BF))
    return jnp.concatenate(rows, axis=0)


def turn(parts):
    lane = lax.broadcasted_iota(jnp.int32, (parts[0].shape[0], 128), 1)
    wide = lane < 64
    narrow = (lane & 32) == 0
    out = [[None, None] for _ in range(8)]
    for n in range(2):
        for m in range(2):
            a = [parts[n * 4 + r][:, m * 128 : (m + 1) * 128] for r in range(4)]
            s = [None] * 4
            for r in range(2):
                s[r] = jnp.where(wide, a[r], pltpu.roll(a[r + 2], 64, 1))
                s[r + 2] = jnp.where(wide, pltpu.roll(a[r], 64, 1), a[r + 2])
            for r in (0, 2):
                out[m * 4 + r][n] = jnp.where(narrow, s[r], pltpu.roll(s[r + 1], 32, 1))
                out[m * 4 + r + 1][n] = jnp.where(narrow, pltpu.roll(s[r], 96, 1), s[r + 1])
    return out


def both_gates(x, w, g):
    n = x.shape[0]
    z = jnp.dot(x.reshape(n * G, 4 * G), w, preferred_element_type=F32).astype(BF)
    outs = []
    for k in range(n):
        rows = z[k * G : (k + 1) * G]
        s = jnp.concatenate([rows[:, : 4 * G], rows[:, 4 * G :]], axis=0)
        outs.append(jnp.dot(g, s, preferred_element_type=F32).astype(BF))
    return outs


PLACES = ((1, 0), (1, 1), (0, 1), (0, 0))
APART = (2, 3, 1, 0)


def by_place(blocks):
    return dict(zip(PLACES, blocks))


def store_blocks(outs, at, blocks):
    blocks = by_place(blocks)
    for k, out in enumerate(outs):
        for i in range(2):
            for j in range(2):
                blocks[i, j][at + k] = out[j * HALF : (j + 1) * HALF, i * 128 : (i + 1) * 128]


STEP = 8
EARLY = 14
COST = 2 * 10**9


def own_bits():
    hi_bits = lax.axis_size("hi").bit_length() - 1
    hi = lax.axis_index("hi")
    return [hi >> k % hi_bits & 1 for k in range(4)]


def steps(size):
    return [(k, min(STEP, size - k)) for k in range(0, size, STEP)]


def first_kernel(x_ref, gates, o0, o1, o2, o3, rest, w1_ref, g_ref, spread, turned):
    early = o0.shape[0]
    own = own_bits()
    late = product(gate_of(gates, 3, 0), gate_of(gates, 2, 0))
    soon = product(gate_of(gates, 1, 0), gate_of(gates, 0, 0))
    w0 = first_weights(wide_product(late, soon))
    w1_ref[...] = right_weights(gate_of(gates, 0, 1), True, 0, own[0])
    g_ref[...] = left_weights(product(gate_of(gates, 1, 2), gate_of(gates, 0, 2)), 0, own[1])

    for k in range(G // 8):
        spread[k * 512 : (k + 1) * 512, :] = x_ref[k * 512 : (k + 1) * 512, :].astype(F32)
        x = jnp.concatenate([spread[pl.ds(k * 512 + p, 256, stride=2), :] for p in range(2)], axis=1).astype(BF)
        r = turned_dot(w0, x)
        tiles = turn([r[g * HALF : (g + 1) * HALF] for g in range(8)])
        for q in range(8):
            for n in range(2):
                turned[n, pl.ds(k * 8 + q, HALF, stride=G), :] = tiles[q][n]

    for k, n in steps(early):
        rows = slice(k * G, (k + n) * G)
        x = jnp.concatenate([turned[0, rows, :], turned[1, rows, :]], axis=1).astype(BF).reshape(n, G, 4 * G)
        store_blocks(both_gates(x, w1_ref[...], g_ref[...]), k, (o0, o1, o2, o3))
    for n in range(2):
        rest[n] = turned[n, early * G :, :].astype(BF)


def second_kernel(rest, w1_ref, g_ref, o0, o1, o2, o3):
    for k, n in steps(o0.shape[0]):
        rows = slice(k * G, (k + n) * G)
        x = jnp.concatenate([rest[0, rows, :], rest[1, rows, :]], axis=1).reshape(n, G, 4 * G)
        store_blocks(both_gates(x, w1_ref[...], g_ref[...]), k, (o0, o1, o2, o3))


def weights_kernel(top, gates, w1_ref, g_ref, w_ref):
    own = own_bits()
    w1_ref[...] = right_weights(product(gate_of(gates, 2, 1), gate_of(gates, 1, 1)), False, own[0], own[2])
    step = top * lax.axis_index("lo") if top else 0
    g_ref[...] = left_weights(product(gate_of(gates, 3, 2), gate_of(gates, 2, 2)), step, own[3])
    w_ref[...] = last_weights(gate_of(gates, 3, 1), own[2])


def joined(ins, k, n):
    order = [APART.index(o) for o in range(4)] if len(ins) > 1 else [0]
    halves = [jnp.concatenate([ins[at][i, k : k + n] for at in order], axis=1) for i in range(2)]
    return jnp.concatenate(halves, axis=2)


def middle_kernel(*refs):
    *ins, w1_ref, g_ref, o0, o1, o2, o3 = refs
    for k, n in steps(o0.shape[0]):
        store_blocks(both_gates(joined(ins, k, n), w1_ref[...], g_ref[...]), k, (o0, o1, o2, o3))


def gather_rows(first, pair, wide):
    for k in range(pair[0].shape[0]):
        for i in range(2):
            wide[i, pl.ds(first + k, HALF, stride=HALF), :] = pair[i][k].astype(F32)


def gather_kernel(b0, b1, b2, b3, *wides):
    blocks = by_place((b0, b1, b2, b3))
    for j, wide in enumerate(wides):
        gather_rows(0, (blocks[0, j], blocks[1, j]), wide)


def last_kernel(j, *refs):
    moved, stayed, w_ref, o_ref, wide, spread, made, sems = refs[-8:]
    gather_rows(HALF - moved.shape[0], (stayed, moved), wide)
    start = (own_bits()[3] ^ j) * (o_ref.shape[0] // 2)
    copies = []
    for k in range(HALF // 8):
        rows = slice(k * 256, (k + 1) * 256)
        x = jnp.concatenate([wide[i, rows, :] for i in range(2)], axis=1).astype(BF)
        r = turned_dot(w_ref[...], x)
        tiles = turn([r[g * HALF : (g + 1) * HALF] for g in range(8)])
        for q in range(8):
            for n in range(2):
                spread[pl.ds((k * 8 + q) * G + n, HALF, stride=2), :] = tiles[q][n]
        rows = slice(k * 512, (k + 1) * 512)
        made[rows, :] = spread[rows, :].astype(BF)
        to = pl.ds(pl.multiple_of(start + k * 512, 512), 512)
        copies.append(pltpu.make_async_copy(made.at[rows], o_ref.at[to], sems.at[k]))
        copies[-1].start()
    for copy in copies:
        copy.wait()


def pick_kernel(groups, regroup, *refs):
    ins, outs = refs[:-groups], refs[-groups:]
    blocks = by_place(ins)
    own = own_bits()[1]
    lo = lax.axis_index("lo")
    rows = outs[0].shape[2]
    for o, out in zip(APART, outs):
        t = regroup[lo ^ o]
        j = t >> 1 ^ own
        at = pl.ds(pl.multiple_of((t & 1) * rows, rows), rows)
        for i in range(2):
            out[i] = jnp.where(j == 0, blocks[i, 0][:, at, :], blocks[i, 1][:, at, :])


VMEM = pl.BlockSpec(memory_space=pltpu.VMEM)
ANY = pl.BlockSpec(memory_space=pl.ANY)
SMEM = pl.BlockSpec(memory_space=pltpu.SMEM)


def call(kernel, outs, args, specs=None, scratch=(), after=(), flops=1, aliases={}, out_specs=None):
    specs = specs or [VMEM] * len(args)

    def body(*refs):
        kernel(*refs[: len(args)], *refs[len(args) + len(after) :])

    return pl.pallas_call(
        body,
        out_shape=outs,
        in_specs=specs + [ANY] * len(after),
        out_specs=out_specs or jax.tree.map(lambda _: VMEM, outs),
        scratch_shapes=scratch,
        input_output_aliases=aliases,
        cost_estimate=pl.CostEstimate(flops=flops, bytes_accessed=1, transcendentals=0),
        compiler_params=pltpu.CompilerParams(vmem_limit_bytes=40 * 2**20),
    )(*args, *after)


def swapped(x, apart):
    return lax.ppermute(x, "hi", [(d, d ^ apart) for d in range(lax.axis_size("hi"))])


def exchange(blocks, b_bit, a_bit):
    out = []
    for (i, j), block in zip(PLACES, blocks):
        apart = i << b_bit | j << a_bit
        out.append(swapped(block, apart) if apart else block)
    return out


def regrouped(blocks, regroup, bit, groups, top, flops=1, after=()):
    count = blocks[0].shape[-3]
    if groups == 4:
        part = jax.ShapeDtypeStruct((2, count, top, 128), BF)
        parts = call(functools.partial(pick_kernel, groups), [part] * groups, (regroup, *blocks), [SMEM] + [VMEM] * 4, after=after, flops=flops)
        pairs = [[(d, d ^ o) for d in range(groups)] for o in APART]
        return [lax.ppermute(x, "lo", to) if o else x for o, x, to in zip(APART, parts, pairs)]
    own = lax.axis_index("hi") >> bit & 1
    blocks = by_place(blocks)
    halves = [jnp.stack([blocks[i, 0], blocks[i, 1]], axis=1) for i in range(2)]
    both = jnp.stack([jnp.where(own == 0, half, jnp.flip(half, 1)) for half in halves])
    both = jnp.take(both.reshape(2, count, groups, top, 128), regroup, axis=2)
    both = lax.all_to_all(both, "lo", split_axis=2, concat_axis=2, tiled=True)
    return [both.reshape(2, count, G, 128)]


def on_device(state, gates, regroup):
    hi_bits = lax.axis_size("hi").bit_length() - 1
    groups = lax.axis_size("lo")
    bits = [k % hi_bits for k in range(4)]
    top = G // groups
    whole = 2 * state.shape[1] // 128

    block = jax.ShapeDtypeStruct((HALF - EARLY, HALF, 128), BF)
    early_block = jax.ShapeDtypeStruct((EARLY, HALF, 128), BF)
    turned = pltpu.VMEM((2, HALF * G, 128), F32)
    spread = pltpu.VMEM((whole, 128), F32)
    lanes, rows = (4 * G, 8 * G), (G, 2 * G)

    x = state.reshape(2, -1, 128).transpose(1, 0, 2).reshape(whole, 128)
    rest = jax.ShapeDtypeStruct((2, (HALF - EARLY) * G, 128), BF)
    *early, rest, w1, g = call(
        first_kernel,
        [early_block] * 4 + [rest, jax.ShapeDtypeStruct(lanes, BF), jax.ShapeDtypeStruct(rows, BF)],
        (x, gates),
        scratch=[spread, turned],
    )
    early = exchange(early, bits[0], bits[1])
    late = call(second_kernel, [block] * 4, (rest, w1, g))
    late = exchange(late, bits[0], bits[1])
    shapes = [jax.ShapeDtypeStruct(shape, BF) for shape in (lanes, rows, (4 * G, 4 * G))]
    w1, g, w = call(functools.partial(weights_kernel, top if groups == 4 else 0), shapes, (gates,))

    early = regrouped(early, regroup, bits[1], groups, top, COST)
    late = regrouped(late, regroup, bits[1], groups, top, after=early[3:])
    early = call(middle_kernel, [early_block] * 4, (*early, w1, g), flops=COST)
    late = call(middle_kernel, [block] * 4, (*late, w1, g), after=early[3:])
    early = exchange(early, bits[2], bits[3])
    late = exchange(late, bits[2], bits[3])

    wide = jax.ShapeDtypeStruct((2, HALF * HALF, 128), F32)
    wides = call(gather_kernel, [wide] * 2, early, flops=COST)
    late = by_place(late)
    scratch = [pltpu.VMEM((whole // 2, 128), F32), pltpu.VMEM((whole // 2, 128), BF), pltpu.SemaphoreType.DMA((HALF // 8,))]
    shapes = [jax.ShapeDtypeStruct((whole, 128), BF), wide]
    out = []
    for j in range(2):
        args = (*out, wides[j], late[1, j], late[0, j], w)
        aliases = {0: 0, 1: 1} if out else {0: 1}
        specs = [ANY] * len(out) + [VMEM] * 4
        kernel = functools.partial(last_kernel, j)
        out = call(kernel, shapes, args, specs, scratch, aliases=aliases, out_specs=[ANY, VMEM])[:1]
    (out,) = out
    return out.reshape(-1, 2, 128).transpose(1, 0, 2).reshape(state.shape)


def solution(mesh):
    placed = (P(None, ("hi", "lo")), P(), P())
    return jax.shard_map(
        on_device, mesh=mesh, in_specs=placed, out_specs=P(None, ("hi", "lo")), check_vma=False
    )
```

```python
import functools

import jax
import jax.numpy as jnp
from jax import lax
from jax.experimental import pallas as pl
from jax.experimental.pallas import tpu as pltpu
from jax.sharding import PartitionSpec as P

GQ = 6
G = 2**GQ
HALF = G // 2
BF = jnp.bfloat16
F32 = jnp.float32


def iotas(rows, columns):
    shape = (rows, columns)
    return lax.broadcasted_iota(jnp.int32, shape, 0), lax.broadcasted_iota(jnp.int32, shape, 1)


def dot(x, y):
    return jnp.dot(x, y, preferred_element_type=F32)


def turned_dot(x, y):
    return lax.dot_general(x, y, (((1,), (1,)), ((), ())), preferred_element_type=F32)


def ones(where):
    return where.astype(F32).astype(BF)


def gate_of(ref, layer, block):
    return jnp.concatenate([ref[layer, block, 0], ref[layer, block, 1]], axis=1)


def squared(gate):
    return jnp.concatenate([gate, jnp.concatenate([-gate[:, G:], gate[:, :G]], axis=1)], axis=0)


def product(later, earlier):
    return dot(later, squared(earlier))


def wide_product(later, earlier):
    parts = []
    for x in (later, squared(earlier)):
        high = x.astype(BF)
        parts.append((high, (x - high.astype(F32)).astype(BF)))
    (lh, ll), (eh, el) = parts
    return dot(jnp.concatenate([lh, lh, ll], axis=1), jnp.concatenate([eh, el, eh], axis=0))


def first_weights(gate, part):
    real = jnp.concatenate([gate[:, :G], gate[:, :G]], axis=1)
    imag = jnp.concatenate([gate[:, G:], gate[:, G:]], axis=1)
    low = iotas(HALF // 2, 2 * G)[1] < G
    rows = []
    for ch in range(2):
        start = ch * HALF + part * HALF // 2
        r, i = (x[start : start + HALF // 2] for x in (real, imag))
        for pair in ((r, -i), (i, r)):
            for mask in (low, ~low):
                rows.append(jnp.concatenate([jnp.where(mask, x, 0.0) for x in pair], axis=1))
    return jnp.concatenate(rows, axis=0).astype(BF)


def right_weights(gate, low, in_bit, out_bit):
    k, b = iotas(G, G)
    order = ((k & (HALF - 1)) << 1 | k >> GQ - 1) if low else k ^ in_bit * HALF
    gate = gate.astype(BF)
    t = turned_dot(ones(b == order), jnp.concatenate([gate[:, :G], gate[:, G:]], axis=0)).astype(BF)
    at, n = iotas(2 * G, 8 * G)
    bit = lambda i: n >> i & 1
    to = ((bit(7) ^ out_bit) << GQ - 1) | n & (HALF - 1)
    turn_i = bit(8)
    part = bit(5) ^ turn_i
    sign_i = turn_i & (1 - bit(5))
    ch = iotas(G, 8 * G)[1] >> 6 & 1
    made = []
    for p in range(2):
        minus = sign_i ^ ((1 - part) & p)
        place = jnp.where(at == to + (part ^ p) * G, (1 - 2 * minus).astype(F32), 0.0).astype(BF)
        y = dot(t, place)
        made.append([jnp.where(ch == c, y, 0.0).astype(BF) for c in range(2)])
    if low:
        rows = [made[p][c] for c in range(2) for p in range(2)]
    else:
        rows = [made[p][c][i * HALF : (i + 1) * HALF] for i in range(2) for c in range(2) for p in range(2)]
    return jnp.concatenate(rows, axis=0)


def left_weights(gate, step, out_bit):
    k, a = iotas(G, G)
    rows = dot(ones(a == k ^ out_bit * HALF), gate.astype(BF)).astype(BF)
    k, a = iotas(2 * G, 2 * G)
    return dot(rows, ones(a == k ^ step)).astype(BF)


def last_weights(gate, in_bit):
    k, b = iotas(G, G)
    t = dot(ones(b == ((k & (HALF - 1)) << 1 | k >> GQ - 1)), gate).astype(BF)
    at, n = iotas(2 * G, 4 * G)
    p_in = n >> 5 & 1
    b_in = ((n >> 7 ^ in_bit) << GQ - 1) | n & (HALF - 1)
    ch = iotas(HALF, 4 * G)[1] >> 6 & 1
    rows = []
    for p in range(2):
        minus = (1 - p) * p_in
        place = jnp.where(at == b_in + (p_in ^ p) * G, (1 - 2 * minus).astype(F32), 0.0).astype(BF)
        y = dot(t, place)
        for b0 in range(2):
            for c in range(2):
                rows.append(jnp.where(ch == c, y[b0 * HALF : (b0 + 1) * HALF], 0.0).astype(BF))
    return jnp.concatenate(rows, axis=0)


def turn(parts):
    lane = lax.broadcasted_iota(jnp.int32, (parts[0].shape[0], 128), 1)
    wide = lane < 64
    narrow = (lane & 32) == 0
    out = [[None, None] for _ in range(8)]
    for n in range(2):
        for m in range(2):
            a = [parts[n * 4 + r][:, m * 128 : (m + 1) * 128] for r in range(4)]
            s = [None] * 4
            for r in range(2):
                s[r] = jnp.where(wide, a[r], pltpu.roll(a[r + 2], 64, 1))
                s[r + 2] = jnp.where(wide, pltpu.roll(a[r], 64, 1), a[r + 2])
            for r in (0, 2):
                out[m * 4 + r][n] = jnp.where(narrow, s[r], pltpu.roll(s[r + 1], 32, 1))
                out[m * 4 + r + 1][n] = jnp.where(narrow, pltpu.roll(s[r], 96, 1), s[r + 1])
    return out


def both_gates(x, w, g):
    n = x.shape[0]
    z = jnp.dot(x.reshape(n * G, 4 * G), w, preferred_element_type=F32).astype(BF)
    outs = []
    for k in range(n):
        rows = z[k * G : (k + 1) * G]
        s = jnp.concatenate([rows[:, : 4 * G], rows[:, 4 * G :]], axis=0)
        outs.append(jnp.dot(g, s, preferred_element_type=F32).astype(BF))
    return outs


PLACES = ((1, 0), (1, 1), (0, 1), (0, 0))
APART = (2, 3, 1, 0)


def by_place(blocks):
    return dict(zip(PLACES, blocks))


def store_blocks(outs, at, blocks):
    blocks = by_place(blocks)
    for k, out in enumerate(outs):
        for i in range(2):
            for j in range(2):
                blocks[i, j][at + k] = out[j * HALF : (j + 1) * HALF, i * 128 : (i + 1) * 128]


STEP = 22
PITCH = G + 1
NARROW = HALF + 1
EARLY = 12
COST = 2 * 10**9


def own_bits():
    hi_bits = lax.axis_size("hi").bit_length() - 1
    hi = lax.axis_index("hi")
    return [hi >> k % hi_bits & 1 for k in range(4)]


def steps(size):
    parts = -(-size // STEP)
    ends = [size * k // parts for k in range(parts + 1)]
    return [(k, end - k) for k, end in zip(ends, ends[1:])]


def split_rows(k, x, w, turned):
    r = turned_dot(w, x)
    some = HALF // 2
    tiles = turn([r[g * some : (g + 1) * some] for g in range(8)])
    for q in range(8):
        for n in range(2):
            turned[n, pl.ds(k * 8 + q, some, stride=PITCH), :] = tiles[q][n]


def rows_of(turned, first, last):
    halves = [jnp.stack([turned[i, cp * PITCH : cp * PITCH + G, :] for cp in range(first, last)]) for i in range(2)]
    return jnp.concatenate(halves, axis=2).astype(BF)


def first_kernel(x_ref, gates, o0, o1, o2, o3, mixed, rest, w0_ref, w1_ref, g_ref, spread, turned):
    early = o0.shape[0]
    own = own_bits()
    late = product(gate_of(gates, 3, 0), gate_of(gates, 2, 0))
    soon = product(gate_of(gates, 1, 0), gate_of(gates, 0, 0))
    gate = wide_product(late, soon)
    w0 = first_weights(gate, 0)
    w0_ref[...] = first_weights(gate, 1)
    w1_ref[...] = right_weights(gate_of(gates, 0, 1), True, 0, own[0])
    g_ref[...] = left_weights(product(gate_of(gates, 1, 2), gate_of(gates, 0, 2)), 0, own[1])

    for k in range(G // 8):
        spread[k * 512 : (k + 1) * 512, :] = x_ref[k * 512 : (k + 1) * 512, :].astype(F32)
        x = jnp.concatenate([spread[pl.ds(k * 512 + p, 256, stride=2), :] for p in range(2)], axis=1).astype(BF)
        mixed[k * 256 : (k + 1) * 256, :] = x
        split_rows(k, x, w0, turned)

    store_blocks(both_gates(rows_of(turned, 0, early), w1_ref[...], g_ref[...]), 0, (o0, o1, o2, o3))
    rest[...] = rows_of(turned, early, HALF // 2)


def second_kernel(mixed, rest, w0_ref, w1_ref, g_ref, o0, o1, o2, o3, turned):
    blocks = (o0, o1, o2, o3)
    store_blocks(both_gates(rest[...], w1_ref[...], g_ref[...]), 0, blocks)
    for k in range(G // 8):
        split_rows(k, mixed[k * 256 : (k + 1) * 256, :], w0_ref[...], turned)
    made = both_gates(rows_of(turned, 0, HALF // 2), w1_ref[...], g_ref[...])
    store_blocks(made, rest.shape[0], blocks)


def weights_kernel(top, gates, w1_ref, g_ref, w_ref):
    own = own_bits()
    w1_ref[...] = right_weights(product(gate_of(gates, 2, 1), gate_of(gates, 1, 1)), False, own[0], own[2])
    step = top * lax.axis_index("lo") if top else 0
    g_ref[...] = left_weights(product(gate_of(gates, 3, 2), gate_of(gates, 2, 2)), step, own[3])
    w_ref[...] = last_weights(gate_of(gates, 3, 1), own[2])


def joined(ins, k, n):
    order = [APART.index(o) for o in range(4)] if len(ins) > 1 else [0]
    halves = [jnp.concatenate([ins[at][i, k : k + n] for at in order], axis=1) for i in range(2)]
    return jnp.concatenate(halves, axis=2)


def middle_kernel(*refs):
    *ins, w1_ref, g_ref, o0, o1, o2, o3 = refs
    for k, n in steps(o0.shape[0]):
        store_blocks(both_gates(joined(ins, k, n), w1_ref[...], g_ref[...]), k, (o0, o1, o2, o3))


def gather_rows(first, pair, wide):
    for k in range(pair[0].shape[0]):
        for i in range(2):
            wide[i, pl.ds(first + k, HALF, stride=NARROW), :] = pair[i][k].astype(F32)


def gather_kernel(b0, b1, b2, b3, *wides):
    blocks = by_place((b0, b1, b2, b3))
    for j, wide in enumerate(wides):
        gather_rows(0, (blocks[0, j], blocks[1, j]), wide)


def last_kernel(j, *refs):
    moved, stayed, w_ref, o_ref, wide, spread, made, sems = refs[-8:]
    gather_rows(HALF - moved.shape[0], (stayed, moved), wide)
    start = (own_bits()[3] ^ j) * (o_ref.shape[0] // 2)
    copies = []
    for k in range(HALF // 8):
        starts = [(k * 8 + q) * NARROW for q in range(8)]
        halves = [jnp.concatenate([wide[i, at : at + HALF, :] for at in starts], axis=0) for i in range(2)]
        x = jnp.concatenate(halves, axis=1).astype(BF)
        r = turned_dot(w_ref[...], x)
        tiles = turn([r[g * HALF : (g + 1) * HALF] for g in range(8)])
        for q in range(8):
            for n in range(2):
                spread[pl.ds((k * 8 + q) * G + n, HALF, stride=2), :] = tiles[q][n]
        rows = slice(k * 512, (k + 1) * 512)
        made[rows, :] = spread[rows, :].astype(BF)
        to = pl.ds(pl.multiple_of(start + k * 512, 512), 512)
        copies.append(pltpu.make_async_copy(made.at[rows], o_ref.at[to], sems.at[k]))
        copies[-1].start()
    for copy in copies:
        copy.wait()


def pick_kernel(groups, regroup, *refs):
    ins, outs = refs[:-groups], refs[-groups:]
    blocks = by_place(ins)
    own = own_bits()[1]
    lo = lax.axis_index("lo")
    rows = outs[0].shape[2]
    for o, out in zip(APART, outs):
        t = regroup[lo ^ o]
        j = t >> 1 ^ own
        at = pl.ds(pl.multiple_of((t & 1) * rows, rows), rows)
        for i in range(2):
            out[i] = jnp.where(j == 0, blocks[i, 0][:, at, :], blocks[i, 1][:, at, :])


VMEM = pl.BlockSpec(memory_space=pltpu.VMEM)
ANY = pl.BlockSpec(memory_space=pl.ANY)
SMEM = pl.BlockSpec(memory_space=pltpu.SMEM)


def call(kernel, outs, args, specs=None, scratch=(), after=(), flops=1, aliases={}, out_specs=None):
    specs = specs or [VMEM] * len(args)

    def body(*refs):
        kernel(*refs[: len(args)], *refs[len(args) + len(after) :])

    return pl.pallas_call(
        body,
        out_shape=outs,
        in_specs=specs + [ANY] * len(after),
        out_specs=out_specs or jax.tree.map(lambda _: VMEM, outs),
        scratch_shapes=scratch,
        input_output_aliases=aliases,
        cost_estimate=pl.CostEstimate(flops=flops, bytes_accessed=1, transcendentals=0),
        compiler_params=pltpu.CompilerParams(vmem_limit_bytes=40 * 2**20),
    )(*args, *after)


def swapped(x, apart):
    return lax.ppermute(x, "hi", [(d, d ^ apart) for d in range(lax.axis_size("hi"))])


def exchange(blocks, b_bit, a_bit):
    out = []
    for (i, j), block in zip(PLACES, blocks):
        apart = i << b_bit | j << a_bit
        out.append(swapped(block, apart) if apart else block)
    return out


def regrouped(blocks, regroup, bit, groups, top, flops=1, after=()):
    count = blocks[0].shape[-3]
    if groups == 4:
        part = jax.ShapeDtypeStruct((2, count, top, 128), BF)
        parts = call(functools.partial(pick_kernel, groups), [part] * groups, (regroup, *blocks), [SMEM] + [VMEM] * 4, after=after, flops=flops)
        pairs = [[(d, d ^ o) for d in range(groups)] for o in APART]
        return [lax.ppermute(x, "lo", to) if o else x for o, x, to in zip(APART, parts, pairs)]
    own = lax.axis_index("hi") >> bit & 1
    blocks = by_place(blocks)
    halves = [jnp.stack([blocks[i, 0], blocks[i, 1]], axis=1) for i in range(2)]
    both = jnp.stack([jnp.where(own == 0, half, jnp.flip(half, 1)) for half in halves])
    both = jnp.take(both.reshape(2, count, groups, top, 128), regroup, axis=2)
    both = lax.all_to_all(both, "lo", split_axis=2, concat_axis=2, tiled=True)
    return [both.reshape(2, count, G, 128)]


def on_device(state, gates, regroup):
    hi_bits = lax.axis_size("hi").bit_length() - 1
    groups = lax.axis_size("lo")
    bits = [k % hi_bits for k in range(4)]
    top = G // groups
    whole = 2 * state.shape[1] // 128

    block = jax.ShapeDtypeStruct((HALF - EARLY, HALF, 128), BF)
    early_block = jax.ShapeDtypeStruct((EARLY, HALF, 128), BF)
    turned = pltpu.VMEM((2, HALF // 2 * PITCH, 128), F32)
    spread = pltpu.VMEM((whole, 128), F32)
    lanes, rows = (4 * G, 8 * G), (G, 2 * G)

    x = state.reshape(2, -1, 128).transpose(1, 0, 2).reshape(whole, 128)
    shapes = [(whole // 2, 4 * G), (HALF // 2 - EARLY, G, 4 * G), (2 * G, 4 * G), lanes, rows]
    shapes = [jax.ShapeDtypeStruct(shape, BF) for shape in shapes]
    *early, mixed, rest, w0, w1, g = call(first_kernel, [early_block] * 4 + shapes, (x, gates), scratch=[spread, turned])
    early = exchange(early, bits[0], bits[1])
    late = call(second_kernel, [block] * 4, (mixed, rest, w0, w1, g), scratch=[turned])
    late = exchange(late, bits[0], bits[1])
    shapes = [jax.ShapeDtypeStruct(shape, BF) for shape in (lanes, rows, (4 * G, 4 * G))]
    w1, g, w = call(functools.partial(weights_kernel, top if groups == 4 else 0), shapes, (gates,))

    early = regrouped(early, regroup, bits[1], groups, top, COST)
    late = regrouped(late, regroup, bits[1], groups, top, after=early[3:])
    early = call(middle_kernel, [early_block] * 4, (*early, w1, g), flops=COST)
    late = call(middle_kernel, [block] * 4, (*late, w1, g), after=early[3:])
    early = exchange(early, bits[2], bits[3])
    late = exchange(late, bits[2], bits[3])

    wide = jax.ShapeDtypeStruct((2, HALF * NARROW, 128), F32)
    wides = call(gather_kernel, [wide] * 2, early, flops=COST)
    late = by_place(late)
    scratch = [pltpu.VMEM((whole // 2, 128), F32), pltpu.VMEM((whole // 2, 128), BF), pltpu.SemaphoreType.DMA((HALF // 8,))]
    shapes = [jax.ShapeDtypeStruct((whole, 128), BF), wide]
    out = []
    for j in range(2):
        args = (*out, wides[j], late[1, j], late[0, j], w)
        aliases = {0: 0, 1: 1} if out else {0: 1}
        specs = [ANY] * len(out) + [VMEM] * 4
        kernel = functools.partial(last_kernel, j)
        out = call(kernel, shapes, args, specs, scratch, aliases=aliases, out_specs=[ANY, VMEM])[:1]
    (out,) = out
    return out.reshape(-1, 2, 128).transpose(1, 0, 2).reshape(state.shape)


def solution(mesh):
    placed = (P(None, ("hi", "lo")), P(), P())
    return jax.shard_map(
        on_device, mesh=mesh, in_specs=placed, out_specs=P(None, ("hi", "lo")), check_vma=False
    )
```

```python
import functools

import jax
import jax.numpy as jnp
from jax import lax
from jax.experimental import pallas as pl
from jax.experimental.pallas import tpu as pltpu
from jax.sharding import PartitionSpec as P

GQ = 6
G = 2**GQ
HALF = G // 2
BF = jnp.bfloat16
F32 = jnp.float32


def iotas(rows, columns):
    shape = (rows, columns)
    return lax.broadcasted_iota(jnp.int32, shape, 0), lax.broadcasted_iota(jnp.int32, shape, 1)


def dot(x, y):
    return jnp.dot(x, y, preferred_element_type=F32)


def turned_dot(x, y):
    return lax.dot_general(x, y, (((1,), (1,)), ((), ())), preferred_element_type=F32)


def ones(where):
    return where.astype(F32).astype(BF)


def gate_of(ref, layer, block):
    return jnp.concatenate([ref[layer, block, 0], ref[layer, block, 1]], axis=1)


def squared(gate):
    return jnp.concatenate([gate, jnp.concatenate([-gate[:, G:], gate[:, :G]], axis=1)], axis=0)


def product(later, earlier):
    return dot(later, squared(earlier))


def wide_product(later, earlier):
    parts = []
    for x in (later, squared(earlier)):
        high = x.astype(BF)
        parts.append((high, (x - high.astype(F32)).astype(BF)))
    (lh, ll), (eh, el) = parts
    return dot(jnp.concatenate([lh, lh, ll], axis=1), jnp.concatenate([eh, el, eh], axis=0))


def first_weights(gate, part):
    real = jnp.concatenate([gate[:, :G], gate[:, :G]], axis=1)
    imag = jnp.concatenate([gate[:, G:], gate[:, G:]], axis=1)
    low = iotas(HALF // 2, 2 * G)[1] < G
    rows = []
    for ch in range(2):
        start = ch * HALF + part * HALF // 2
        r, i = (x[start : start + HALF // 2] for x in (real, imag))
        for pair in ((r, -i), (i, r)):
            for mask in (low, ~low):
                rows.append(jnp.concatenate([jnp.where(mask, x, 0.0) for x in pair], axis=1))
    return jnp.concatenate(rows, axis=0).astype(BF)


def right_weights(gate, low, in_bit, out_bit):
    k, b = iotas(G, G)
    order = ((k & (HALF - 1)) << 1 | k >> GQ - 1) if low else k ^ in_bit * HALF
    gate = gate.astype(BF)
    t = turned_dot(ones(b == order), jnp.concatenate([gate[:, :G], gate[:, G:]], axis=0)).astype(BF)
    at, n = iotas(2 * G, 8 * G)
    bit = lambda i: n >> i & 1
    to = ((bit(7) ^ out_bit) << GQ - 1) | n & (HALF - 1)
    turn_i = bit(8)
    part = bit(5) ^ turn_i
    sign_i = turn_i & (1 - bit(5))
    ch = iotas(G, 8 * G)[1] >> 6 & 1
    made = []
    for p in range(2):
        minus = sign_i ^ ((1 - part) & p)
        place = jnp.where(at == to + (part ^ p) * G, (1 - 2 * minus).astype(F32), 0.0).astype(BF)
        y = dot(t, place)
        made.append([jnp.where(ch == c, y, 0.0).astype(BF) for c in range(2)])
    if low:
        rows = [made[p][c] for c in range(2) for p in range(2)]
    else:
        rows = [made[p][c][i * HALF : (i + 1) * HALF] for i in range(2) for c in range(2) for p in range(2)]
    return jnp.concatenate(rows, axis=0)


def left_weights(gate, step, out_bit):
    k, a = iotas(G, G)
    rows = dot(ones(a == k ^ out_bit * HALF), gate.astype(BF)).astype(BF)
    k, a = iotas(2 * G, 2 * G)
    return dot(rows, ones(a == k ^ step)).astype(BF)


def last_weights(gate, in_bit):
    k, b = iotas(G, G)
    t = dot(ones(b == ((k & (HALF - 1)) << 1 | k >> GQ - 1)), gate).astype(BF)
    at, n = iotas(2 * G, 4 * G)
    p_in = n >> 5 & 1
    b_in = ((n >> 7 ^ in_bit) << GQ - 1) | n & (HALF - 1)
    ch = iotas(HALF, 4 * G)[1] >> 6 & 1
    rows = []
    for p in range(2):
        minus = (1 - p) * p_in
        place = jnp.where(at == b_in + (p_in ^ p) * G, (1 - 2 * minus).astype(F32), 0.0).astype(BF)
        y = dot(t, place)
        for b0 in range(2):
            for c in range(2):
                rows.append(jnp.where(ch == c, y[b0 * HALF : (b0 + 1) * HALF], 0.0).astype(BF))
    return jnp.concatenate(rows, axis=0)


def turn(parts):
    lane = lax.broadcasted_iota(jnp.int32, (parts[0].shape[0], 128), 1)
    wide = lane < 64
    narrow = (lane & 32) == 0
    out = [[None, None] for _ in range(8)]
    for n in range(2):
        for m in range(2):
            a = [parts[n * 4 + r][:, m * 128 : (m + 1) * 128] for r in range(4)]
            s = [None] * 4
            for r in range(2):
                s[r] = jnp.where(wide, a[r], pltpu.roll(a[r + 2], 64, 1))
                s[r + 2] = jnp.where(wide, pltpu.roll(a[r], 64, 1), a[r + 2])
            for r in (0, 2):
                out[m * 4 + r][n] = jnp.where(narrow, s[r], pltpu.roll(s[r + 1], 32, 1))
                out[m * 4 + r + 1][n] = jnp.where(narrow, pltpu.roll(s[r], 96, 1), s[r + 1])
    return out


def both_gates(x, w, g):
    n = x.shape[0]
    z = jnp.dot(x.reshape(n * G, 4 * G), w, preferred_element_type=F32).astype(BF)
    outs = []
    for k in range(n):
        rows = z[k * G : (k + 1) * G]
        s = jnp.concatenate([rows[:, : 4 * G], rows[:, 4 * G :]], axis=0)
        outs.append(jnp.dot(g, s, preferred_element_type=F32).astype(BF))
    return outs


PLACES = ((1, 0), (1, 1), (0, 1), (0, 0))
APART = (2, 3, 1, 0)


def by_place(blocks):
    return dict(zip(PLACES, blocks))


def store_blocks(outs, at, blocks):
    blocks = by_place(blocks)
    for k, out in enumerate(outs):
        for i in range(2):
            for j in range(2):
                blocks[i, j][at + k] = out[j * HALF : (j + 1) * HALF, i * 128 : (i + 1) * 128]


STEP = 22
PITCH = G + 1
NARROW = HALF + 1
EARLY = 13
COST = 2 * 10**9


def own_bits():
    hi_bits = lax.axis_size("hi").bit_length() - 1
    hi = lax.axis_index("hi")
    return [hi >> k % hi_bits & 1 for k in range(4)]


def steps(size):
    parts = -(-size // STEP)
    ends = [size * k // parts for k in range(parts + 1)]
    return [(k, end - k) for k, end in zip(ends, ends[1:])]


def split_rows(k, x, w, turned):
    r = turned_dot(w, x).astype(BF)
    some = HALF // 2
    tiles = turn([r[g * some : (g + 1) * some] for g in range(8)])
    for q in range(8):
        for n in range(2):
            turned[n, pl.ds(k * 8 + q, some, stride=PITCH), :] = tiles[q][n].astype(F32)


def rows_of(turned, first, last):
    halves = [jnp.stack([turned[i, cp * PITCH : cp * PITCH + G, :] for cp in range(first, last)]) for i in range(2)]
    return jnp.concatenate(halves, axis=2).astype(BF)


def first_kernel(x_ref, gates, o0, o1, o2, o3, mixed, rest, w0_ref, w1_ref, g_ref, spread, turned):
    early = o0.shape[0]
    own = own_bits()
    late = product(gate_of(gates, 3, 0), gate_of(gates, 2, 0))
    soon = product(gate_of(gates, 1, 0), gate_of(gates, 0, 0))
    gate = wide_product(late, soon)
    w0 = first_weights(gate, 0)
    w0_ref[...] = first_weights(gate, 1)
    w1_ref[...] = right_weights(gate_of(gates, 0, 1), True, 0, own[0])
    g_ref[...] = left_weights(product(gate_of(gates, 1, 2), gate_of(gates, 0, 2)), 0, own[1])

    for k in range(G // 8):
        spread[k * 512 : (k + 1) * 512, :] = x_ref[k * 512 : (k + 1) * 512, :].astype(F32)
        x = jnp.concatenate([spread[pl.ds(k * 512 + p, 256, stride=2), :] for p in range(2)], axis=1).astype(BF)
        mixed[k * 256 : (k + 1) * 256, :] = x
        split_rows(k, x, w0, turned)

    store_blocks(both_gates(rows_of(turned, 0, early), w1_ref[...], g_ref[...]), 0, (o0, o1, o2, o3))
    rest[...] = rows_of(turned, early, HALF // 2)


def later_weights(top, gates, w1_ref, g_ref, w_ref):
    own = own_bits()
    w1_ref[...] = right_weights(product(gate_of(gates, 2, 1), gate_of(gates, 1, 1)), False, own[0], own[2])
    step = top * lax.axis_index("lo") if top else 0
    g_ref[...] = left_weights(product(gate_of(gates, 3, 2), gate_of(gates, 2, 2)), step, own[3])
    w_ref[...] = last_weights(gate_of(gates, 3, 1), own[2])


def second_kernel(top, mixed, rest, w0_ref, w1_ref, g_ref, gates, *refs):
    *blocks, turned = refs[:4] + refs[7:]
    later_weights(top, gates, *refs[4:7])
    store_blocks(both_gates(rest[...], w1_ref[...], g_ref[...]), 0, blocks)
    for k in range(G // 8):
        split_rows(k, mixed[k * 256 : (k + 1) * 256, :], w0_ref[...], turned)
    made = both_gates(rows_of(turned, 0, HALF // 2), w1_ref[...], g_ref[...])
    store_blocks(made, rest.shape[0], blocks)


def joined(ins, k, n):
    order = [APART.index(o) for o in range(4)] if len(ins) > 1 else [0]
    halves = [jnp.concatenate([ins[at][i, k : k + n] for at in order], axis=1) for i in range(2)]
    return jnp.concatenate(halves, axis=2)


def middle_kernel(*refs):
    *ins, w1_ref, g_ref, o0, o1, o2, o3 = refs
    for k, n in steps(o0.shape[0]):
        store_blocks(both_gates(joined(ins, k, n), w1_ref[...], g_ref[...]), k, (o0, o1, o2, o3))


def gather_rows(first, pair, wide):
    for k in range(pair[0].shape[0]):
        for i in range(2):
            wide[i, pl.ds(first + k, HALF, stride=NARROW), :] = pair[i][k].astype(F32)


def gather_kernel(b0, b1, b2, b3, *wides):
    blocks = by_place((b0, b1, b2, b3))
    for j, wide in enumerate(wides):
        gather_rows(0, (blocks[0, j], blocks[1, j]), wide)


def last_kernel(j, *refs):
    moved, stayed, w_ref, o_ref, wide, spread, made, sems = refs[-8:]
    gather_rows(HALF - moved.shape[0], (stayed, moved), wide)
    start = (own_bits()[3] ^ j) * (o_ref.shape[0] // 2)
    copies = []
    for k in range(HALF // 8):
        starts = [(k * 8 + q) * NARROW for q in range(8)]
        halves = [jnp.concatenate([wide[i, at : at + HALF, :] for at in starts], axis=0) for i in range(2)]
        x = jnp.concatenate(halves, axis=1).astype(BF)
        r = turned_dot(w_ref[...], x).astype(BF)
        tiles = turn([r[g * HALF : (g + 1) * HALF] for g in range(8)])
        for q in range(8):
            for n in range(2):
                spread[pl.ds((k * 8 + q) * G + n, HALF, stride=2), :] = tiles[q][n].astype(F32)
        rows = slice(k * 512, (k + 1) * 512)
        made[rows, :] = spread[rows, :].astype(BF)
        to = pl.ds(pl.multiple_of(start + k * 512, 512), 512)
        copies.append(pltpu.make_async_copy(made.at[rows], o_ref.at[to], sems.at[k]))
        copies[-1].start()
    for copy in copies:
        copy.wait()


def pick_kernel(groups, regroup, *refs):
    ins, outs = refs[:-groups], refs[-groups:]
    blocks = by_place(ins)
    own = own_bits()[1]
    lo = lax.axis_index("lo")
    rows = outs[0].shape[2]
    for o, out in zip(APART, outs):
        t = regroup[lo ^ o]
        j = t >> 1 ^ own
        at = pl.ds(pl.multiple_of((t & 1) * rows, rows), rows)
        for i in range(2):
            out[i] = jnp.where(j == 0, blocks[i, 0][:, at, :], blocks[i, 1][:, at, :])


VMEM = pl.BlockSpec(memory_space=pltpu.VMEM)
ANY = pl.BlockSpec(memory_space=pl.ANY)
SMEM = pl.BlockSpec(memory_space=pltpu.SMEM)


def call(kernel, outs, args, specs=None, scratch=(), after=(), flops=1, aliases={}, out_specs=None):
    specs = specs or [VMEM] * len(args)

    def body(*refs):
        kernel(*refs[: len(args)], *refs[len(args) + len(after) :])

    return pl.pallas_call(
        body,
        out_shape=outs,
        in_specs=specs + [ANY] * len(after),
        out_specs=out_specs or jax.tree.map(lambda _: VMEM, outs),
        scratch_shapes=scratch,
        input_output_aliases=aliases,
        cost_estimate=pl.CostEstimate(flops=flops, bytes_accessed=1, transcendentals=0),
        compiler_params=pltpu.CompilerParams(vmem_limit_bytes=40 * 2**20),
    )(*args, *after)


def swapped(x, apart):
    return lax.ppermute(x, "hi", [(d, d ^ apart) for d in range(lax.axis_size("hi"))])


def exchange(blocks, b_bit, a_bit):
    out = []
    for (i, j), block in zip(PLACES, blocks):
        apart = i << b_bit | j << a_bit
        out.append(swapped(block, apart) if apart else block)
    return out


def regrouped(blocks, regroup, bit, groups, top, flops=1, after=()):
    count = blocks[0].shape[-3]
    if groups == 4:
        part = jax.ShapeDtypeStruct((2, count, top, 128), BF)
        parts = call(functools.partial(pick_kernel, groups), [part] * groups, (regroup, *blocks), [SMEM] + [VMEM] * 4, after=after, flops=flops)
        pairs = [[(d, d ^ o) for d in range(groups)] for o in APART]
        return [lax.ppermute(x, "lo", to) if o else x for o, x, to in zip(APART, parts, pairs)]
    own = lax.axis_index("hi") >> bit & 1
    blocks = by_place(blocks)
    halves = [jnp.stack([blocks[i, 0], blocks[i, 1]], axis=1) for i in range(2)]
    both = jnp.stack([jnp.where(own == 0, half, jnp.flip(half, 1)) for half in halves])
    both = jnp.take(both.reshape(2, count, groups, top, 128), regroup, axis=2)
    both = lax.all_to_all(both, "lo", split_axis=2, concat_axis=2, tiled=True)
    return [both.reshape(2, count, G, 128)]


def on_device(state, gates, regroup):
    hi_bits = lax.axis_size("hi").bit_length() - 1
    groups = lax.axis_size("lo")
    bits = [k % hi_bits for k in range(4)]
    top = G // groups
    whole = 2 * state.shape[1] // 128

    block = jax.ShapeDtypeStruct((HALF - EARLY, HALF, 128), BF)
    early_block = jax.ShapeDtypeStruct((EARLY, HALF, 128), BF)
    turned = pltpu.VMEM((2, HALF // 2 * PITCH, 128), F32)
    spread = pltpu.VMEM((whole, 128), F32)
    lanes, rows = (4 * G, 8 * G), (G, 2 * G)

    x = state.reshape(2, -1, 128).transpose(1, 0, 2).reshape(whole, 128)
    shapes = [(whole // 2, 4 * G), (HALF // 2 - EARLY, G, 4 * G), (2 * G, 4 * G), lanes, rows]
    shapes = [jax.ShapeDtypeStruct(shape, BF) for shape in shapes]
    *early, mixed, rest, w0, w1, g = call(first_kernel, [early_block] * 4 + shapes, (x, gates), scratch=[spread, turned])
    early = exchange(early, bits[0], bits[1])
    shapes = [jax.ShapeDtypeStruct(shape, BF) for shape in (lanes, rows, (4 * G, 4 * G))]
    kernel = functools.partial(second_kernel, top if groups == 4 else 0)
    *late, w1, g, w = call(kernel, [block] * 4 + shapes, (mixed, rest, w0, w1, g, gates), scratch=[turned])
    late = exchange(late, bits[0], bits[1])
    early = regrouped(early, regroup, bits[1], groups, top, COST)
    late = regrouped(late, regroup, bits[1], groups, top, after=early[3:])
    early = call(middle_kernel, [early_block] * 4, (*early, w1, g), flops=COST)
    late = call(middle_kernel, [block] * 4, (*late, w1, g), after=early[3:])
    early = exchange(early, bits[2], bits[3])
    late = exchange(late, bits[2], bits[3])

    wide = jax.ShapeDtypeStruct((2, HALF * NARROW, 128), F32)
    wides = call(gather_kernel, [wide] * 2, early, flops=COST)
    late = by_place(late)
    scratch = [pltpu.VMEM((whole // 2, 128), F32), pltpu.VMEM((whole // 2, 128), BF), pltpu.SemaphoreType.DMA((HALF // 8,))]
    shapes = [jax.ShapeDtypeStruct((whole, 128), BF), wide]
    out = []
    for j in range(2):
        args = (*out, wides[j], late[1, j], late[0, j], w)
        aliases = {0: 0, 1: 1} if out else {0: 1}
        specs = [ANY] * len(out) + [VMEM] * 4
        kernel = functools.partial(last_kernel, j)
        out = call(kernel, shapes, args, specs, scratch, aliases=aliases, out_specs=[ANY, VMEM])[:1]
    (out,) = out
    return out.reshape(-1, 2, 128).transpose(1, 0, 2).reshape(state.shape)


def solution(mesh):
    placed = (P(None, ("hi", "lo")), P(), P())
    return jax.shard_map(
        on_device, mesh=mesh, in_specs=placed, out_specs=P(None, ("hi", "lo")), check_vma=False
    )
```

```python
import functools

import jax
import jax.numpy as jnp
from jax import lax
from jax.experimental import pallas as pl
from jax.experimental.pallas import tpu as pltpu
from jax.sharding import PartitionSpec as P

GQ = 6
G = 2**GQ
HALF = G // 2
BF = jnp.bfloat16
F32 = jnp.float32


def iotas(rows, columns):
    shape = (rows, columns)
    return lax.broadcasted_iota(jnp.int32, shape, 0), lax.broadcasted_iota(jnp.int32, shape, 1)


def dot(x, y):
    return jnp.dot(x, y, preferred_element_type=F32)


def turned_dot(x, y):
    return lax.dot_general(x, y, (((1,), (1,)), ((), ())), preferred_element_type=F32)


def ones(where):
    return where.astype(F32).astype(BF)


def gate_of(ref, layer, block):
    return jnp.concatenate([ref[layer, block, 0], ref[layer, block, 1]], axis=1)


def squared(gate):
    return jnp.concatenate([gate, jnp.concatenate([-gate[:, G:], gate[:, :G]], axis=1)], axis=0)


def product(later, earlier):
    return dot(later, squared(earlier))


def wide_product(later, earlier):
    parts = []
    for x in (later, squared(earlier)):
        high = x.astype(BF)
        parts.append((high, (x - high.astype(F32)).astype(BF)))
    (lh, ll), (eh, el) = parts
    return dot(jnp.concatenate([lh, lh, ll], axis=1), jnp.concatenate([eh, el, eh], axis=0))


def first_weights(gate, part):
    real = jnp.concatenate([gate[:, :G], gate[:, :G]], axis=1)
    imag = jnp.concatenate([gate[:, G:], gate[:, G:]], axis=1)
    low = iotas(HALF // 2, 2 * G)[1] < G
    rows = []
    for ch in range(2):
        start = ch * HALF + part * HALF // 2
        r, i = (x[start : start + HALF // 2] for x in (real, imag))
        for pair in ((r, -i), (i, r)):
            for mask in (low, ~low):
                rows.append(jnp.concatenate([jnp.where(mask, x, 0.0) for x in pair], axis=1))
    return jnp.concatenate(rows, axis=0).astype(BF)


def columns(size):
    return lax.broadcasted_iota(jnp.int32, (1, size), 1)


def placed(rows, to, minus):
    at = iotas(rows, to.shape[1])[0]
    return jnp.where(at == to, (1 - 2 * minus).astype(F32), 0.0).astype(BF)


def right_weights(gate, low, in_bit, out_bit):
    k, b = iotas(G, G)
    order = ((k & (HALF - 1)) << 1 | k >> GQ - 1) if low else k ^ in_bit * HALF
    gate = gate.astype(BF)
    t = turned_dot(ones(b == order), jnp.concatenate([gate[:, :G], gate[:, G:]], axis=0)).astype(BF)
    n = columns(8 * G)
    bit = lambda i: n >> i & 1
    to = ((bit(7) ^ out_bit) << GQ - 1) | n & (HALF - 1)
    turn_i = bit(8)
    part = bit(5) ^ turn_i
    sign_i = turn_i & (1 - bit(5))
    made = []
    for p in range(2):
        y = dot(t, placed(2 * G, to + (part ^ p) * G, sign_i ^ ((1 - part) & p)))
        made.append([jnp.where(bit(6) == c, y, 0.0).astype(BF) for c in range(2)])
    if low:
        rows = [made[p][c] for c in range(2) for p in range(2)]
    else:
        rows = [made[p][c][i * HALF : (i + 1) * HALF] for i in range(2) for c in range(2) for p in range(2)]
    return jnp.concatenate(rows, axis=0)


def left_weights(gate, step, out_bit):
    k, a = iotas(G, G)
    rows = dot(ones(a == k ^ out_bit * HALF), gate.astype(BF)).astype(BF)
    k, a = iotas(2 * G, 2 * G)
    return dot(rows, ones(a == k ^ step)).astype(BF)


def last_weights(gate, in_bit):
    k, b = iotas(G, G)
    t = dot(ones(b == ((k & (HALF - 1)) << 1 | k >> GQ - 1)), gate).astype(BF)
    n = columns(4 * G)
    p_in = n >> 5 & 1
    b_in = ((n >> 7 ^ in_bit) << GQ - 1) | n & (HALF - 1)
    ch = n >> 6 & 1
    rows = []
    for p in range(2):
        y = dot(t, placed(2 * G, b_in + (p_in ^ p) * G, (1 - p) * p_in))
        for b0 in range(2):
            for c in range(2):
                rows.append(jnp.where(ch == c, y[b0 * HALF : (b0 + 1) * HALF], 0.0).astype(BF))
    return jnp.concatenate(rows, axis=0)


def turn(parts):
    lane = lax.broadcasted_iota(jnp.int32, (parts[0].shape[0], 128), 1)
    wide = lane < 64
    narrow = (lane & 32) == 0
    out = [[None, None] for _ in range(8)]
    for n in range(2):
        for m in range(2):
            a = [parts[n * 4 + r][:, m * 128 : (m + 1) * 128] for r in range(4)]
            s = [None] * 4
            for r in range(2):
                s[r] = jnp.where(wide, a[r], pltpu.roll(a[r + 2], 64, 1))
                s[r + 2] = jnp.where(wide, pltpu.roll(a[r], 64, 1), a[r + 2])
            for r in (0, 2):
                out[m * 4 + r][n] = jnp.where(narrow, s[r], pltpu.roll(s[r + 1], 32, 1))
                out[m * 4 + r + 1][n] = jnp.where(narrow, pltpu.roll(s[r], 96, 1), s[r + 1])
    return out


def both_gates(x, w, g):
    n = x.shape[0]
    z = jnp.dot(x.reshape(n * G, 4 * G), w, preferred_element_type=F32).astype(BF)
    outs = []
    for k in range(n):
        rows = z[k * G : (k + 1) * G]
        s = jnp.concatenate([rows[:, : 4 * G], rows[:, 4 * G :]], axis=0)
        outs.append(jnp.dot(g, s, preferred_element_type=F32).astype(BF))
    return outs


PLACES = ((1, 0), (1, 1), (0, 1), (0, 0))
APART = (2, 3, 1, 0)


def by_place(blocks):
    return dict(zip(PLACES, blocks))


def store_blocks(outs, at, blocks):
    blocks = by_place(blocks)
    for k, out in enumerate(outs):
        for i in range(2):
            for j in range(2):
                blocks[i, j][at + k] = out[j * HALF : (j + 1) * HALF, i * 128 : (i + 1) * 128]


STEP = 22
PITCH = G + 1
NARROW = HALF + 1
EARLY = 13
COST = 2 * 10**9


def own_bits():
    hi_bits = lax.axis_size("hi").bit_length() - 1
    hi = lax.axis_index("hi")
    return [hi >> k % hi_bits & 1 for k in range(4)]


def steps(size):
    parts = -(-size // STEP)
    ends = [size * k // parts for k in range(parts + 1)]
    return [(k, end - k) for k, end in zip(ends, ends[1:])]


def split_rows(k, x, w, turned):
    r = turned_dot(w, x).astype(BF)
    some = HALF // 2
    tiles = turn([r[g * some : (g + 1) * some] for g in range(8)])
    for q in range(8):
        for n in range(2):
            turned[n, pl.ds(k * 8 + q, some, stride=PITCH), :] = tiles[q][n].astype(F32)


def rows_of(turned, first, last):
    halves = [jnp.stack([turned[i, cp * PITCH : cp * PITCH + G, :] for cp in range(first, last)]) for i in range(2)]
    return jnp.concatenate(halves, axis=2).astype(BF)


def first_weights_kernel(gates, early_w0_ref, w0_ref, w1_ref, g_ref):
    own = own_bits()
    late = product(gate_of(gates, 3, 0), gate_of(gates, 2, 0))
    soon = product(gate_of(gates, 1, 0), gate_of(gates, 0, 0))
    gate = wide_product(late, soon)
    early_w0_ref[...] = first_weights(gate, 0)
    w0_ref[...] = first_weights(gate, 1)
    w1_ref[...] = right_weights(gate_of(gates, 0, 1), True, 0, own[0])
    g_ref[...] = left_weights(product(gate_of(gates, 1, 2), gate_of(gates, 0, 2)), 0, own[1])


def first_kernel(x_ref, w0_ref, w1_ref, g_ref, o0, o1, o2, o3, mixed, rest, spread, turned):
    early = o0.shape[0]
    for k in range(G // 8):
        spread[k * 512 : (k + 1) * 512, :] = x_ref[k * 512 : (k + 1) * 512, :].astype(F32)
        x = jnp.concatenate([spread[pl.ds(k * 512 + p, 256, stride=2), :] for p in range(2)], axis=1).astype(BF)
        mixed[k * 256 : (k + 1) * 256, :] = x
        split_rows(k, x, w0_ref[...], turned)

    store_blocks(both_gates(rows_of(turned, 0, early), w1_ref[...], g_ref[...]), 0, (o0, o1, o2, o3))
    rest[...] = rows_of(turned, early, HALF // 2)


def later_weights(top, gates, w1_ref, g_ref, w_ref):
    own = own_bits()
    w1_ref[...] = right_weights(product(gate_of(gates, 2, 1), gate_of(gates, 1, 1)), False, own[0], own[2])
    step = top * lax.axis_index("lo") if top else 0
    g_ref[...] = left_weights(product(gate_of(gates, 3, 2), gate_of(gates, 2, 2)), step, own[3])
    w_ref[...] = last_weights(gate_of(gates, 3, 1), own[2])


def second_kernel(top, mixed, rest, w0_ref, w1_ref, g_ref, gates, *refs):
    *blocks, turned = refs[:4] + refs[7:]
    later_weights(top, gates, *refs[4:7])
    store_blocks(both_gates(rest[...], w1_ref[...], g_ref[...]), 0, blocks)
    for k in range(G // 8):
        split_rows(k, mixed[k * 256 : (k + 1) * 256, :], w0_ref[...], turned)
    made = both_gates(rows_of(turned, 0, HALF // 2), w1_ref[...], g_ref[...])
    store_blocks(made, rest.shape[0], blocks)


def joined(ins, k, n):
    order = [APART.index(o) for o in range(4)] if len(ins) > 1 else [0]
    halves = [jnp.concatenate([ins[at][i, k : k + n] for at in order], axis=1) for i in range(2)]
    return jnp.concatenate(halves, axis=2)


def middle_kernel(*refs):
    *ins, w1_ref, g_ref, o0, o1, o2, o3 = refs
    for k, n in steps(o0.shape[0]):
        store_blocks(both_gates(joined(ins, k, n), w1_ref[...], g_ref[...]), k, (o0, o1, o2, o3))


def gather_rows(first, pair, wide):
    for k in range(pair[0].shape[0]):
        for i in range(2):
            wide[i, pl.ds(first + k, HALF, stride=NARROW), :] = pair[i][k].astype(F32)


def gather_kernel(b0, b1, b2, b3, *wides):
    blocks = by_place((b0, b1, b2, b3))
    for j, wide in enumerate(wides):
        gather_rows(0, (blocks[0, j], blocks[1, j]), wide)


def last_kernel(j, *refs):
    moved, stayed, w_ref, o_ref, wide, spread, made, sems = refs[-8:]
    gather_rows(HALF - moved.shape[0], (stayed, moved), wide)
    start = (own_bits()[3] ^ j) * (o_ref.shape[0] // 2)
    copies = []
    for k in range(HALF // 8):
        starts = [(k * 8 + q) * NARROW for q in range(8)]
        halves = [jnp.concatenate([wide[i, at : at + HALF, :] for at in starts], axis=0) for i in range(2)]
        x = jnp.concatenate(halves, axis=1).astype(BF)
        r = turned_dot(w_ref[...], x).astype(BF)
        tiles = turn([r[g * HALF : (g + 1) * HALF] for g in range(8)])
        for q in range(8):
            for n in range(2):
                spread[pl.ds((k * 8 + q) * G + n, HALF, stride=2), :] = tiles[q][n].astype(F32)
        rows = slice(k * 512, (k + 1) * 512)
        made[rows, :] = spread[rows, :].astype(BF)
        to = pl.ds(pl.multiple_of(start + k * 512, 512), 512)
        copies.append(pltpu.make_async_copy(made.at[rows], o_ref.at[to], sems.at[k]))
        copies[-1].start()
    for copy in copies:
        copy.wait()


def pick_kernel(groups, regroup, *refs):
    ins, outs = refs[:-groups], refs[-groups:]
    blocks = by_place(ins)
    own = own_bits()[1]
    lo = lax.axis_index("lo")
    rows = outs[0].shape[2]
    for o, out in zip(APART, outs):
        t = regroup[lo ^ o]
        j = t >> 1 ^ own
        at = pl.ds(pl.multiple_of((t & 1) * rows, rows), rows)
        for i in range(2):
            out[i] = jnp.where(j == 0, blocks[i, 0][:, at, :], blocks[i, 1][:, at, :])


VMEM = pl.BlockSpec(memory_space=pltpu.VMEM)
ANY = pl.BlockSpec(memory_space=pl.ANY)
SMEM = pl.BlockSpec(memory_space=pltpu.SMEM)


def call(kernel, outs, args, specs=None, scratch=(), after=(), flops=1, aliases={}, out_specs=None):
    specs = specs or [VMEM] * len(args)

    def body(*refs):
        kernel(*refs[: len(args)], *refs[len(args) + len(after) :])

    return pl.pallas_call(
        body,
        out_shape=outs,
        in_specs=specs + [ANY] * len(after),
        out_specs=out_specs or jax.tree.map(lambda _: VMEM, outs),
        scratch_shapes=scratch,
        input_output_aliases=aliases,
        cost_estimate=pl.CostEstimate(flops=flops, bytes_accessed=1, transcendentals=0),
        compiler_params=pltpu.CompilerParams(vmem_limit_bytes=40 * 2**20),
    )(*args, *after)


def swapped(x, apart):
    return lax.ppermute(x, "hi", [(d, d ^ apart) for d in range(lax.axis_size("hi"))])


def exchange(blocks, b_bit, a_bit):
    out = []
    for (i, j), block in zip(PLACES, blocks):
        apart = i << b_bit | j << a_bit
        out.append(swapped(block, apart) if apart else block)
    return out


def regrouped(blocks, regroup, bit, groups, top, flops=1, after=()):
    count = blocks[0].shape[-3]
    if groups == 4:
        part = jax.ShapeDtypeStruct((2, count, top, 128), BF)
        parts = call(functools.partial(pick_kernel, groups), [part] * groups, (regroup, *blocks), [SMEM] + [VMEM] * 4, after=after, flops=flops)
        pairs = [[(d, d ^ o) for d in range(groups)] for o in APART]
        return [lax.ppermute(x, "lo", to) if o else x for o, x, to in zip(APART, parts, pairs)]
    own = lax.axis_index("hi") >> bit & 1
    blocks = by_place(blocks)
    halves = [jnp.stack([blocks[i, 0], blocks[i, 1]], axis=1) for i in range(2)]
    both = jnp.stack([jnp.where(own == 0, half, jnp.flip(half, 1)) for half in halves])
    both = jnp.take(both.reshape(2, count, groups, top, 128), regroup, axis=2)
    both = lax.all_to_all(both, "lo", split_axis=2, concat_axis=2, tiled=True)
    return [both.reshape(2, count, G, 128)]


def on_device(state, gates, regroup):
    hi_bits = lax.axis_size("hi").bit_length() - 1
    groups = lax.axis_size("lo")
    bits = [k % hi_bits for k in range(4)]
    top = G // groups
    whole = 2 * state.shape[1] // 128

    block = jax.ShapeDtypeStruct((HALF - EARLY, HALF, 128), BF)
    early_block = jax.ShapeDtypeStruct((EARLY, HALF, 128), BF)
    turned = pltpu.VMEM((2, HALF // 2 * PITCH, 128), F32)
    spread = pltpu.VMEM((whole, 128), F32)
    lanes, rows = (4 * G, 8 * G), (G, 2 * G)

    x = state.reshape(2, -1, 128).transpose(1, 0, 2).reshape(whole, 128)
    shapes = [jax.ShapeDtypeStruct(shape, BF) for shape in ((2 * G, 4 * G), (2 * G, 4 * G), lanes, rows)]
    early_w0, w0, w1, g = call(first_weights_kernel, shapes, (gates,), flops=COST)
    shapes = [jax.ShapeDtypeStruct(shape, BF) for shape in ((whole // 2, 4 * G), (HALF // 2 - EARLY, G, 4 * G))]
    *early, mixed, rest = call(first_kernel, [early_block] * 4 + shapes, (x, early_w0, w1, g), scratch=[spread, turned])
    early = exchange(early, bits[0], bits[1])
    shapes = [jax.ShapeDtypeStruct(shape, BF) for shape in (lanes, rows, (4 * G, 4 * G))]
    kernel = functools.partial(second_kernel, top if groups == 4 else 0)
    *late, w1, g, w = call(kernel, [block] * 4 + shapes, (mixed, rest, w0, w1, g, gates), scratch=[turned])
    late = exchange(late, bits[0], bits[1])
    early = regrouped(early, regroup, bits[1], groups, top, COST)
    late = regrouped(late, regroup, bits[1], groups, top, after=early[3:])
    early = call(middle_kernel, [early_block] * 4, (*early, w1, g), flops=COST)
    late = call(middle_kernel, [block] * 4, (*late, w1, g), after=early[3:])
    early = exchange(early, bits[2], bits[3])
    late = exchange(late, bits[2], bits[3])

    wide = jax.ShapeDtypeStruct((2, HALF * NARROW, 128), F32)
    wides = call(gather_kernel, [wide] * 2, early, flops=COST)
    late = by_place(late)
    scratch = [pltpu.VMEM((whole // 2, 128), F32), pltpu.VMEM((whole // 2, 128), BF), pltpu.SemaphoreType.DMA((HALF // 8,))]
    shapes = [jax.ShapeDtypeStruct((whole, 128), BF), wide]
    out = []
    for j in range(2):
        args = (*out, wides[j], late[1, j], late[0, j], w)
        aliases = {0: 0, 1: 1} if out else {0: 1}
        specs = [ANY] * len(out) + [VMEM] * 4
        kernel = functools.partial(last_kernel, j)
        out = call(kernel, shapes, args, specs, scratch, aliases=aliases, out_specs=[ANY, VMEM])[:1]
    (out,) = out
    return out.reshape(-1, 2, 128).transpose(1, 0, 2).reshape(state.shape)


def solution(mesh):
    placed = (P(None, ("hi", "lo")), P(), P())
    return jax.shard_map(
        on_device, mesh=mesh, in_specs=placed, out_specs=P(None, ("hi", "lo")), check_vma=False
    )
```

```python
import functools

import jax
import jax.numpy as jnp
from jax import lax
from jax.experimental import pallas as pl
from jax.experimental.pallas import tpu as pltpu
from jax.sharding import PartitionSpec as P

GQ = 6
G = 2**GQ
HALF = G // 2
BF = jnp.bfloat16
F32 = jnp.float32


def iotas(rows, columns):
    shape = (rows, columns)
    return lax.broadcasted_iota(jnp.int32, shape, 0), lax.broadcasted_iota(jnp.int32, shape, 1)


def dot(x, y):
    return jnp.dot(x, y, preferred_element_type=F32)


def turned_dot(x, y):
    return lax.dot_general(x, y, (((1,), (1,)), ((), ())), preferred_element_type=F32)


def ones(where):
    return where.astype(F32).astype(BF)


def gate_of(ref, layer, block):
    return jnp.concatenate([ref[layer, block, 0], ref[layer, block, 1]], axis=1)


def squared(gate):
    return jnp.concatenate([gate, jnp.concatenate([-gate[:, G:], gate[:, :G]], axis=1)], axis=0)


def product(later, earlier):
    return dot(later, squared(earlier))


def wide_product(later, earlier):
    parts = []
    for x in (later, squared(earlier)):
        high = x.astype(BF)
        parts.append((high, (x - high.astype(F32)).astype(BF)))
    (lh, ll), (eh, el) = parts
    return dot(jnp.concatenate([lh, lh, ll], axis=1), jnp.concatenate([eh, el, eh], axis=0))


def first_weights(gate, part):
    real = jnp.concatenate([gate[:, :G], gate[:, :G]], axis=1)
    imag = jnp.concatenate([gate[:, G:], gate[:, G:]], axis=1)
    low = iotas(HALF // 2, 2 * G)[1] < G
    rows = []
    for ch in range(2):
        start = ch * HALF + part * HALF // 2
        r, i = (x[start : start + HALF // 2] for x in (real, imag))
        for pair in ((r, -i), (i, r)):
            for mask in (low, ~low):
                rows.append(jnp.concatenate([jnp.where(mask, x, 0.0) for x in pair], axis=1))
    return jnp.concatenate(rows, axis=0).astype(BF)


def columns(size):
    return lax.broadcasted_iota(jnp.int32, (1, size), 1)


def placed(rows, to, minus):
    at = iotas(rows, to.shape[1])[0]
    return jnp.where(at == to, (1 - 2 * minus).astype(F32), 0.0).astype(BF)


def right_weights(gate, low, in_bit, out_bit):
    k, b = iotas(G, G)
    order = ((k & (HALF - 1)) << 1 | k >> GQ - 1) if low else k ^ in_bit * HALF
    gate = gate.astype(BF)
    t = turned_dot(ones(b == order), jnp.concatenate([gate[:, :G], gate[:, G:]], axis=0)).astype(BF)
    n = columns(8 * G)
    bit = lambda i: n >> i & 1
    to = ((bit(7) ^ out_bit) << GQ - 1) | n & (HALF - 1)
    turn_i = bit(8)
    part = bit(5) ^ turn_i
    sign_i = turn_i & (1 - bit(5))
    made = []
    for p in range(2):
        y = dot(t, placed(2 * G, to + (part ^ p) * G, sign_i ^ ((1 - part) & p)))
        made.append([jnp.where(bit(6) == c, y, 0.0).astype(BF) for c in range(2)])
    if low:
        rows = [made[p][c] for c in range(2) for p in range(2)]
    else:
        rows = [made[p][c][i * HALF : (i + 1) * HALF] for i in range(2) for c in range(2) for p in range(2)]
    return jnp.concatenate(rows, axis=0)


def left_weights(gate, step, out_bit):
    k, a = iotas(G, G)
    rows = dot(ones(a == k ^ out_bit * HALF), gate.astype(BF)).astype(BF)
    k, a = iotas(2 * G, 2 * G)
    return dot(rows, ones(a == k ^ step)).astype(BF)


def last_weights(gate, in_bit):
    k, b = iotas(2 * G, G)
    t = dot(ones(b == ((k >> 1 & (HALF - 1)) << 1 | k >> GQ)), gate).astype(BF)
    n = columns(4 * G)
    p_in = n >> 5 & 1
    b_in = ((n >> 7 ^ in_bit) << GQ - 1) | n & (HALF - 1)
    ch = n >> 6 & 1
    real, imag = (dot(t, placed(2 * G, b_in + (p_in ^ p) * G, (1 - p) * p_in)) for p in range(2))
    y = jnp.where((iotas(2 * G, 4 * G)[0] & 1) == 0, real, imag)
    rows = [jnp.where(ch == c, y[b0 * G : (b0 + 1) * G], 0.0) for b0 in range(2) for c in range(2)]
    return jnp.concatenate(rows, axis=0).astype(BF)


def turn_four(a):
    lane = lax.broadcasted_iota(jnp.int32, a[0].shape, 1)
    wide = lane < 64
    narrow = (lane & 32) == 0
    s, out = [None] * 4, [None] * 4
    for r in range(2):
        s[r] = jnp.where(wide, a[r], pltpu.roll(a[r + 2], 64, 1))
        s[r + 2] = jnp.where(wide, pltpu.roll(a[r], 64, 1), a[r + 2])
    for r in (0, 2):
        out[r] = jnp.where(narrow, s[r], pltpu.roll(s[r + 1], 32, 1))
        out[r + 1] = jnp.where(narrow, pltpu.roll(s[r], 96, 1), s[r + 1])
    return out


def turn(parts):
    out = [[None, None] for _ in range(8)]
    for n in range(2):
        for m in range(2):
            four = turn_four([part[:, m * 128 : (m + 1) * 128] for part in parts[n * 4 : n * 4 + 4]])
            for q in range(4):
                out[m * 4 + q][n] = four[q]
    return out


def both_gates(x, w, g):
    n = x.shape[0]
    z = jnp.dot(x.reshape(n * G, 4 * G), w, preferred_element_type=F32).astype(BF)
    outs = []
    for k in range(n):
        rows = z[k * G : (k + 1) * G]
        s = jnp.concatenate([rows[:, : 4 * G], rows[:, 4 * G :]], axis=0)
        outs.append(jnp.dot(g, s, preferred_element_type=F32).astype(BF))
    return outs


PLACES = ((1, 0), (1, 1), (0, 1), (0, 0))
APART = (2, 3, 1, 0)


def by_place(blocks):
    return dict(zip(PLACES, blocks))


def store_blocks(outs, at, blocks):
    blocks = by_place(blocks)
    for k, out in enumerate(outs):
        for i in range(2):
            for j in range(2):
                blocks[i, j][at + k] = out[j * HALF : (j + 1) * HALF, i * 128 : (i + 1) * 128]


STEP = 22
PITCH = G + 1
NARROW = HALF + 1
EARLY = 14
COST = 2 * 10**9


def own_bits():
    hi_bits = lax.axis_size("hi").bit_length() - 1
    hi = lax.axis_index("hi")
    return [hi >> k % hi_bits & 1 for k in range(4)]


def steps(size):
    parts = -(-size // STEP)
    ends = [size * k // parts for k in range(parts + 1)]
    return [(k, end - k) for k, end in zip(ends, ends[1:])]


def split_rows(k, x, w, turned):
    r = turned_dot(w, x).astype(BF)
    some = HALF // 2
    tiles = turn([r[g * some : (g + 1) * some] for g in range(8)])
    for q in range(8):
        for n in range(2):
            turned[n, pl.ds(k * 8 + q, some, stride=PITCH), :] = tiles[q][n].astype(F32)


def rows_of(turned, first, last):
    halves = [jnp.stack([turned[i, cp * PITCH : cp * PITCH + G, :] for cp in range(first, last)]) for i in range(2)]
    return jnp.concatenate(halves, axis=2).astype(BF)


def first_weights_kernel(gates, early_w0_ref, w0_ref, w1_ref, g_ref):
    own = own_bits()
    late = product(gate_of(gates, 3, 0), gate_of(gates, 2, 0))
    soon = product(gate_of(gates, 1, 0), gate_of(gates, 0, 0))
    gate = wide_product(late, soon)
    early_w0_ref[...] = first_weights(gate, 0)
    w0_ref[...] = first_weights(gate, 1)
    w1_ref[...] = right_weights(gate_of(gates, 0, 1), True, 0, own[0])
    g_ref[...] = left_weights(product(gate_of(gates, 1, 2), gate_of(gates, 0, 2)), 0, own[1])


def first_kernel(x_ref, w0_ref, w1_ref, g_ref, o0, o1, o2, o3, mixed, rest, spread, turned):
    early = o0.shape[0]
    for k in range(G // 8):
        spread[k * 512 : (k + 1) * 512, :] = x_ref[k * 512 : (k + 1) * 512, :].astype(F32)
        x = jnp.concatenate([spread[pl.ds(k * 512 + p, 256, stride=2), :] for p in range(2)], axis=1).astype(BF)
        mixed[k * 256 : (k + 1) * 256, :] = x
        split_rows(k, x, w0_ref[...], turned)

    store_blocks(both_gates(rows_of(turned, 0, early), w1_ref[...], g_ref[...]), 0, (o0, o1, o2, o3))
    rest[...] = rows_of(turned, early, HALF // 2)


def later_weights(top, gates, w1_ref, g_ref, w_ref):
    own = own_bits()
    w1_ref[...] = right_weights(product(gate_of(gates, 2, 1), gate_of(gates, 1, 1)), False, own[0], own[2])
    step = top * lax.axis_index("lo") if top else 0
    g_ref[...] = left_weights(product(gate_of(gates, 3, 2), gate_of(gates, 2, 2)), step, own[3])
    w_ref[...] = last_weights(gate_of(gates, 3, 1), own[2])


def second_kernel(top, mixed, rest, w0_ref, w1_ref, g_ref, gates, *refs):
    *blocks, turned = refs[:4] + refs[7:]
    later_weights(top, gates, *refs[4:7])
    store_blocks(both_gates(rest[...], w1_ref[...], g_ref[...]), 0, blocks)
    for k in range(G // 8):
        split_rows(k, mixed[k * 256 : (k + 1) * 256, :], w0_ref[...], turned)
    made = both_gates(rows_of(turned, 0, HALF // 2), w1_ref[...], g_ref[...])
    store_blocks(made, rest.shape[0], blocks)


def joined(ins, k, n):
    order = [APART.index(o) for o in range(4)] if len(ins) > 1 else [0]
    halves = [jnp.concatenate([ins[at][i, k : k + n] for at in order], axis=1) for i in range(2)]
    return jnp.concatenate(halves, axis=2)


def middle_kernel(*refs):
    *ins, w1_ref, g_ref, o0, o1, o2, o3 = refs
    for k, n in steps(o0.shape[0]):
        store_blocks(both_gates(joined(ins, k, n), w1_ref[...], g_ref[...]), k, (o0, o1, o2, o3))


def gather_rows(first, pair, wide):
    for k in range(pair[0].shape[0]):
        for i in range(2):
            wide[i, pl.ds(first + k, HALF, stride=NARROW), :] = pair[i][k].astype(F32)


def gather_kernel(b0, b1, b2, b3, *wides):
    blocks = by_place((b0, b1, b2, b3))
    for j, wide in enumerate(wides):
        gather_rows(0, (blocks[0, j], blocks[1, j]), wide)


def last_kernel(j, *refs):
    moved, stayed, w_ref, o_ref, wide, made, sems = refs[-7:]
    gather_rows(HALF - moved.shape[0], (stayed, moved), wide)
    start = (own_bits()[3] ^ j) * (o_ref.shape[0] // 2)
    copies = []
    for k in range(HALF // 8):
        starts = [(k * 8 + q) * NARROW for q in range(8)]
        halves = [jnp.concatenate([wide[i, at : at + HALF, :] for at in starts], axis=0) for i in range(2)]
        x = jnp.concatenate(halves, axis=1).astype(BF)
        r = turned_dot(w_ref[...], x).astype(BF)
        for m in range(2):
            tiles = turn_four([r[g * G : (g + 1) * G, m * 128 : (m + 1) * 128] for g in range(4)])
            for q in range(4):
                at = (k * 8 + m * 4 + q) * G
                made[at : at + G, :] = tiles[q]
        rows = slice(k * 512, (k + 1) * 512)
        to = pl.ds(pl.multiple_of(start + k * 512, 512), 512)
        copies.append(pltpu.make_async_copy(made.at[rows], o_ref.at[to], sems.at[k]))
        copies[-1].start()
    for copy in copies:
        copy.wait()


def pick_kernel(groups, regroup, *refs):
    ins, outs = refs[:-groups], refs[-groups:]
    blocks = by_place(ins)
    own = own_bits()[1]
    lo = lax.axis_index("lo")
    rows = outs[0].shape[2]
    for o, out in zip(APART, outs):
        t = jnp.sum(jnp.where(columns(groups) == lo ^ o, regroup[...], 0))
        j = t >> 1 ^ own
        at = pl.ds(pl.multiple_of((t & 1) * rows, rows), rows)
        for half in range(2):

            @pl.when(j == half)
            def _():
                for i in range(2):
                    out[i] = blocks[i, half][:, at, :]


VMEM = pl.BlockSpec(memory_space=pltpu.VMEM)
ANY = pl.BlockSpec(memory_space=pl.ANY)
SMEM = pl.BlockSpec(memory_space=pltpu.SMEM)


def call(kernel, outs, args, specs=None, scratch=(), after=(), flops=1, aliases={}, out_specs=None):
    specs = specs or [VMEM] * len(args)

    def body(*refs):
        kernel(*refs[: len(args)], *refs[len(args) + len(after) :])

    return pl.pallas_call(
        body,
        out_shape=outs,
        in_specs=specs + [ANY] * len(after),
        out_specs=out_specs or jax.tree.map(lambda _: VMEM, outs),
        scratch_shapes=scratch,
        input_output_aliases=aliases,
        cost_estimate=pl.CostEstimate(flops=flops, bytes_accessed=1, transcendentals=0),
        compiler_params=pltpu.CompilerParams(vmem_limit_bytes=40 * 2**20),
    )(*args, *after)


def swapped(x, apart):
    return lax.ppermute(x, "hi", [(d, d ^ apart) for d in range(lax.axis_size("hi"))])


def exchange(blocks, b_bit, a_bit):
    out = []
    for (i, j), block in zip(PLACES, blocks):
        apart = i << b_bit | j << a_bit
        out.append(swapped(block, apart) if apart else block)
    return out


def regrouped(blocks, regroup, bit, groups, top, flops=1, after=()):
    count = blocks[0].shape[-3]
    if groups == 4:
        part = jax.ShapeDtypeStruct((2, count, top, 128), BF)
        parts = call(functools.partial(pick_kernel, groups), [part] * groups, (regroup.reshape(1, groups), *blocks), after=after, flops=flops)
        pairs = [[(d, d ^ o) for d in range(groups)] for o in APART]
        return [lax.ppermute(x, "lo", to) if o else x for o, x, to in zip(APART, parts, pairs)]
    own = lax.axis_index("hi") >> bit & 1
    blocks = by_place(blocks)
    halves = [jnp.stack([blocks[i, 0], blocks[i, 1]], axis=1) for i in range(2)]
    both = jnp.stack([jnp.where(own == 0, half, jnp.flip(half, 1)) for half in halves])
    both = jnp.take(both.reshape(2, count, groups, top, 128), regroup, axis=2)
    both = lax.all_to_all(both, "lo", split_axis=2, concat_axis=2, tiled=True)
    return [both.reshape(2, count, G, 128)]


def on_device(state, gates, regroup):
    hi_bits = lax.axis_size("hi").bit_length() - 1
    groups = lax.axis_size("lo")
    bits = [k % hi_bits for k in range(4)]
    top = G // groups
    whole = 2 * state.shape[1] // 128

    block = jax.ShapeDtypeStruct((HALF - EARLY, HALF, 128), BF)
    early_block = jax.ShapeDtypeStruct((EARLY, HALF, 128), BF)
    turned = pltpu.VMEM((2, HALF // 2 * PITCH, 128), F32)
    spread = pltpu.VMEM((whole, 128), F32)
    lanes, rows = (4 * G, 8 * G), (G, 2 * G)

    x = state.reshape(2, -1, 128).transpose(1, 0, 2).reshape(whole, 128)
    shapes = [jax.ShapeDtypeStruct(shape, BF) for shape in ((2 * G, 4 * G), (2 * G, 4 * G), lanes, rows)]
    early_w0, w0, w1, g = call(first_weights_kernel, shapes, (gates,), flops=COST)
    shapes = [jax.ShapeDtypeStruct(shape, BF) for shape in ((whole // 2, 4 * G), (HALF // 2 - EARLY, G, 4 * G))]
    *early, mixed, rest = call(first_kernel, [early_block] * 4 + shapes, (x, early_w0, w1, g), scratch=[spread, turned])
    early = exchange(early, bits[0], bits[1])
    shapes = [jax.ShapeDtypeStruct(shape, BF) for shape in (lanes, rows, (4 * G, 4 * G))]
    kernel = functools.partial(second_kernel, top if groups == 4 else 0)
    *late, w1, g, w = call(kernel, [block] * 4 + shapes, (mixed, rest, w0, w1, g, gates), scratch=[turned])
    late = exchange(late, bits[0], bits[1])
    early = regrouped(early, regroup, bits[1], groups, top, COST)
    late = regrouped(late, regroup, bits[1], groups, top, after=early[3:])
    early = call(middle_kernel, [early_block] * 4, (*early, w1, g), flops=COST)
    late = call(middle_kernel, [block] * 4, (*late, w1, g), after=early[3:])
    early = exchange(early, bits[2], bits[3])
    late = exchange(late, bits[2], bits[3])

    wide = jax.ShapeDtypeStruct((2, HALF * NARROW, 128), F32)
    wides = call(gather_kernel, [wide] * 2, early, flops=COST)
    late = by_place(late)
    scratch = [pltpu.VMEM((whole // 2, 128), BF), pltpu.SemaphoreType.DMA((HALF // 8,))]
    shapes = [jax.ShapeDtypeStruct((whole, 128), BF), wide]
    out = []
    for j in range(2):
        args = (*out, wides[j], late[1, j], late[0, j], w)
        aliases = {0: 0, 1: 1} if out else {0: 1}
        specs = [ANY] * len(out) + [VMEM] * 4
        kernel = functools.partial(last_kernel, j)
        out = call(kernel, shapes, args, specs, scratch, aliases=aliases, out_specs=[ANY, VMEM])[:1]
    (out,) = out
    return out.reshape(-1, 2, 128).transpose(1, 0, 2).reshape(state.shape)


def solution(mesh):
    placed = (P(None, ("hi", "lo")), P(), P())
    return jax.shard_map(
        on_device, mesh=mesh, in_specs=placed, out_specs=P(None, ("hi", "lo")), check_vma=False
    )
```

```python
import functools

import jax
import jax.numpy as jnp
from jax import lax
from jax.experimental import pallas as pl
from jax.experimental.pallas import tpu as pltpu
from jax.sharding import PartitionSpec as P

GQ = 6
G = 2**GQ
HALF = G // 2
BF = jnp.bfloat16
F32 = jnp.float32


def iotas(rows, columns):
    shape = (rows, columns)
    return lax.broadcasted_iota(jnp.int32, shape, 0), lax.broadcasted_iota(jnp.int32, shape, 1)


def dot(x, y):
    return jnp.dot(x, y, preferred_element_type=F32)


def turned_dot(x, y):
    return lax.dot_general(x, y, (((1,), (1,)), ((), ())), preferred_element_type=F32)


def ones(where):
    return where.astype(F32).astype(BF)


def gate_of(ref, layer, block):
    return jnp.concatenate([ref[layer, block, 0], ref[layer, block, 1]], axis=1)


def squared(gate):
    return jnp.concatenate([gate, jnp.concatenate([-gate[:, G:], gate[:, :G]], axis=1)], axis=0)


def product(later, earlier):
    return dot(later, squared(earlier))


def wide_product(later, earlier):
    parts = []
    for x in (later, squared(earlier)):
        high = x.astype(BF)
        parts.append((high, (x - high.astype(F32)).astype(BF)))
    (lh, ll), (eh, el) = parts
    return dot(jnp.concatenate([lh, lh, ll], axis=1), jnp.concatenate([eh, el, eh], axis=0))


def first_weights(gate, part):
    real = jnp.concatenate([gate[:, :G], gate[:, :G]], axis=1)
    imag = jnp.concatenate([gate[:, G:], gate[:, G:]], axis=1)
    low = iotas(HALF // 2, 2 * G)[1] < G
    rows = []
    for ch in range(2):
        start = ch * HALF + part * HALF // 2
        r, i = (x[start : start + HALF // 2] for x in (real, imag))
        for pair in ((r, -i), (i, r)):
            for mask in (low, ~low):
                rows.append(jnp.concatenate([jnp.where(mask, x, 0.0) for x in pair], axis=1))
    return jnp.concatenate(rows, axis=0).astype(BF)


def columns(size):
    return lax.broadcasted_iota(jnp.int32, (1, size), 1)


def placed(rows, to, minus):
    at = iotas(rows, to.shape[1])[0]
    return jnp.where(at == to, (1 - 2 * minus).astype(F32), 0.0).astype(BF)


def right_weights(gate, low, in_bit, out_bit):
    k, b = iotas(G, G)
    order = ((k & (HALF - 1)) << 1 | k >> GQ - 1) if low else k ^ in_bit * HALF
    gate = gate.astype(BF)
    t = turned_dot(ones(b == order), jnp.concatenate([gate[:, :G], gate[:, G:]], axis=0)).astype(BF)
    n = columns(8 * G)
    bit = lambda i: n >> i & 1
    to = ((bit(7) ^ out_bit) << GQ - 1) | n & (HALF - 1)
    turn_i = bit(8)
    part = bit(5) ^ turn_i
    sign_i = turn_i & (1 - bit(5))
    made = []
    for p in range(2):
        y = dot(t, placed(2 * G, to + (part ^ p) * G, sign_i ^ ((1 - part) & p)))
        made.append([jnp.where(bit(6) == c, y, 0.0).astype(BF) for c in range(2)])
    if low:
        rows = [made[p][c] for c in range(2) for p in range(2)]
    else:
        rows = [made[p][c][i * HALF : (i + 1) * HALF] for i in range(2) for c in range(2) for p in range(2)]
    return jnp.concatenate(rows, axis=0)


def left_weights(gate, step, out_bit):
    k, a = iotas(G, G)
    rows = dot(ones(a == k ^ out_bit * HALF), gate.astype(BF)).astype(BF)
    k, a = iotas(2 * G, 2 * G)
    return dot(rows, ones(a == k ^ step)).astype(BF)


def last_weights(gate, in_bit):
    k, b = iotas(2 * G, G)
    t = dot(ones(b == ((k >> 1 & (HALF - 1)) << 1 | k >> GQ)), gate).astype(BF)
    n = columns(4 * G)
    p_in = n >> 5 & 1
    b_in = ((n >> 7 ^ in_bit) << GQ - 1) | n & (HALF - 1)
    ch = n >> 6 & 1
    real, imag = (dot(t, placed(2 * G, b_in + (p_in ^ p) * G, (1 - p) * p_in)) for p in range(2))
    y = jnp.where((iotas(2 * G, 4 * G)[0] & 1) == 0, real, imag)
    rows = [jnp.where(ch == c, y[b0 * G : (b0 + 1) * G], 0.0) for b0 in range(2) for c in range(2)]
    return jnp.concatenate(rows, axis=0).astype(BF)


def turn_four(a):
    lane = lax.broadcasted_iota(jnp.int32, a[0].shape, 1)
    wide = lane < 64
    narrow = (lane & 32) == 0
    s, out = [None] * 4, [None] * 4
    for r in range(2):
        s[r] = jnp.where(wide, a[r], pltpu.roll(a[r + 2], 64, 1))
        s[r + 2] = jnp.where(wide, pltpu.roll(a[r], 64, 1), a[r + 2])
    for r in (0, 2):
        out[r] = jnp.where(narrow, s[r], pltpu.roll(s[r + 1], 32, 1))
        out[r + 1] = jnp.where(narrow, pltpu.roll(s[r], 96, 1), s[r + 1])
    return out


def turn(parts):
    out = [[None, None] for _ in range(8)]
    for n in range(2):
        for m in range(2):
            four = turn_four([part[:, m * 128 : (m + 1) * 128] for part in parts[n * 4 : n * 4 + 4]])
            for q in range(4):
                out[m * 4 + q][n] = four[q]
    return out


def both_gates(x, w, g):
    n = x.shape[0]
    z = jnp.dot(x.reshape(n * G, 4 * G), w, preferred_element_type=F32).astype(BF)
    outs = []
    for k in range(n):
        rows = z[k * G : (k + 1) * G]
        s = jnp.concatenate([rows[:, : 4 * G], rows[:, 4 * G :]], axis=0)
        outs.append(jnp.dot(g, s, preferred_element_type=F32).astype(BF))
    return outs


PLACES = ((1, 0), (1, 1), (0, 1), (0, 0))
APART = (2, 3, 1, 0)


def by_place(blocks):
    return dict(zip(PLACES, blocks))


def store_blocks(outs, at, blocks):
    blocks = by_place(blocks)
    for k, out in enumerate(outs):
        for i in range(2):
            for j in range(2):
                blocks[i, j][at + k] = out[j * HALF : (j + 1) * HALF, i * 128 : (i + 1) * 128]


PITCH = G + 1
NARROW = HALF + 1
EARLY = 14
COST = 2 * 10**9


def own_bits():
    hi_bits = lax.axis_size("hi").bit_length() - 1
    hi = lax.axis_index("hi")
    return [hi >> k % hi_bits & 1 for k in range(4)]


def split_rows(k, x, w, turned):
    r = turned_dot(w, x).astype(BF)
    some = HALF // 2
    tiles = turn([r[g * some : (g + 1) * some] for g in range(8)])
    for q in range(8):
        for n in range(2):
            turned[n, pl.ds(k * 8 + q, some, stride=PITCH), :] = tiles[q][n].astype(F32)


def rows_of(turned, first, last):
    halves = [jnp.stack([turned[i, cp * PITCH : cp * PITCH + G, :] for cp in range(first, last)]) for i in range(2)]
    return jnp.concatenate(halves, axis=2).astype(BF)


def first_weights_kernel(gates, early_w0_ref, w0_ref, w1_ref, g_ref):
    own = own_bits()
    late = product(gate_of(gates, 3, 0), gate_of(gates, 2, 0))
    soon = product(gate_of(gates, 1, 0), gate_of(gates, 0, 0))
    gate = wide_product(late, soon)
    early_w0_ref[...] = first_weights(gate, 0)
    w0_ref[...] = first_weights(gate, 1)
    w1_ref[...] = right_weights(gate_of(gates, 0, 1), True, 0, own[0])
    g_ref[...] = left_weights(product(gate_of(gates, 1, 2), gate_of(gates, 0, 2)), 0, own[1])


def first_kernel(x_ref, w0_ref, w1_ref, g_ref, o0, o1, o2, o3, mixed, rest, spread, turned):
    early = o0.shape[0]
    for k in range(G // 8):
        spread[k * 512 : (k + 1) * 512, :] = x_ref[k * 512 : (k + 1) * 512, :].astype(F32)
        x = jnp.concatenate([spread[pl.ds(k * 512 + p, 256, stride=2), :] for p in range(2)], axis=1).astype(BF)
        mixed[k * 256 : (k + 1) * 256, :] = x
        split_rows(k, x, w0_ref[...], turned)

    store_blocks(both_gates(rows_of(turned, 0, early), w1_ref[...], g_ref[...]), 0, (o0, o1, o2, o3))
    rest[...] = rows_of(turned, early, HALF // 2)


def later_weights(top, gates, w1_ref, g_ref, w_ref):
    own = own_bits()
    w1_ref[...] = right_weights(product(gate_of(gates, 2, 1), gate_of(gates, 1, 1)), False, own[0], own[2])
    step = top * lax.axis_index("lo") if top else 0
    g_ref[...] = left_weights(product(gate_of(gates, 3, 2), gate_of(gates, 2, 2)), step, own[3])
    w_ref[...] = last_weights(gate_of(gates, 3, 1), own[2])


def second_kernel(top, mixed, rest, w0_ref, w1_ref, g_ref, gates, *refs):
    *blocks, turned = refs[:4] + refs[7:]
    later_weights(top, gates, *refs[4:7])
    store_blocks(both_gates(rest[...], w1_ref[...], g_ref[...]), 0, blocks)
    for k in range(G // 8):
        split_rows(k, mixed[k * 256 : (k + 1) * 256, :], w0_ref[...], turned)
    made = both_gates(rows_of(turned, 0, HALF // 2), w1_ref[...], g_ref[...])
    store_blocks(made, rest.shape[0], blocks)


def joined(ins):
    order = [APART.index(o) for o in range(4)] if len(ins) > 1 else [0]
    halves = [jnp.concatenate([ins[at][i] for at in order], axis=1) for i in range(2)]
    return jnp.concatenate(halves, axis=2)


def middle_kernel(*refs):
    *ins, w1_ref, g_ref, o0, o1, o2, o3 = refs
    store_blocks(both_gates(joined(ins), w1_ref[...], g_ref[...]), 0, (o0, o1, o2, o3))


def gather_rows(first, pair, wide):
    for k in range(pair[0].shape[0]):
        for i in range(2):
            wide[i, pl.ds(first + k, HALF, stride=NARROW), :] = pair[i][k].astype(F32)


def gather_kernel(b0, b1, b2, b3, *wides):
    blocks = by_place((b0, b1, b2, b3))
    for j, wide in enumerate(wides):
        gather_rows(0, (blocks[0, j], blocks[1, j]), wide)


def last_kernel(j, *refs):
    moved, stayed, w_ref, o_ref, wide, made, sems = refs[-7:]
    gather_rows(HALF - moved.shape[0], (stayed, moved), wide)
    start = (own_bits()[3] ^ j) * (o_ref.shape[0] // 2)
    copies = []
    for k in range(HALF // 8):
        starts = [(k * 8 + q) * NARROW for q in range(8)]
        halves = [jnp.concatenate([wide[i, at : at + HALF, :] for at in starts], axis=0) for i in range(2)]
        x = jnp.concatenate(halves, axis=1).astype(BF)
        r = turned_dot(w_ref[...], x).astype(BF)
        for m in range(2):
            tiles = turn_four([r[g * G : (g + 1) * G, m * 128 : (m + 1) * 128] for g in range(4)])
            for q in range(4):
                at = (k * 8 + m * 4 + q) * G
                made[at : at + G, :] = tiles[q]
        rows = slice(k * 512, (k + 1) * 512)
        to = pl.ds(pl.multiple_of(start + k * 512, 512), 512)
        copies.append(pltpu.make_async_copy(made.at[rows], o_ref.at[to], sems.at[k]))
        copies[-1].start()
    for copy in copies:
        copy.wait()


def pick_kernel(groups, regroup, *refs):
    ins, outs = refs[:-groups], refs[-groups:]
    blocks = by_place(ins)
    own = own_bits()[1]
    lo = lax.axis_index("lo")
    rows = outs[0].shape[2]
    for o, out in zip(APART, outs):
        t = jnp.sum(jnp.where(columns(groups) == lo ^ o, regroup[...], 0))
        j = t >> 1 ^ own
        at = pl.ds(pl.multiple_of((t & 1) * rows, rows), rows)
        for half in range(2):

            @pl.when(j == half)
            def _():
                for i in range(2):
                    out[i] = blocks[i, half][:, at, :]


VMEM = pl.BlockSpec(memory_space=pltpu.VMEM)
ANY = pl.BlockSpec(memory_space=pl.ANY)
SMEM = pl.BlockSpec(memory_space=pltpu.SMEM)


def call(kernel, outs, args, specs=None, scratch=(), after=(), flops=1, aliases={}, out_specs=None):
    specs = specs or [VMEM] * len(args)

    def body(*refs):
        kernel(*refs[: len(args)], *refs[len(args) + len(after) :])

    return pl.pallas_call(
        body,
        out_shape=outs,
        in_specs=specs + [ANY] * len(after),
        out_specs=out_specs or jax.tree.map(lambda _: VMEM, outs),
        scratch_shapes=scratch,
        input_output_aliases=aliases,
        cost_estimate=pl.CostEstimate(flops=flops, bytes_accessed=1, transcendentals=0),
        compiler_params=pltpu.CompilerParams(vmem_limit_bytes=40 * 2**20),
    )(*args, *after)


def swapped(x, apart):
    return lax.ppermute(x, "hi", [(d, d ^ apart) for d in range(lax.axis_size("hi"))])


def exchange(blocks, b_bit, a_bit):
    out = []
    for (i, j), block in zip(PLACES, blocks):
        apart = i << b_bit | j << a_bit
        out.append(swapped(block, apart) if apart else block)
    return out


def regrouped(blocks, regroup, bit, groups, top, flops=1, after=()):
    count = blocks[0].shape[-3]
    if groups == 4:
        part = jax.ShapeDtypeStruct((2, count, top, 128), BF)
        parts = call(functools.partial(pick_kernel, groups), [part] * groups, (regroup.reshape(1, groups), *blocks), after=after, flops=flops)
        pairs = [[(d, d ^ o) for d in range(groups)] for o in APART]
        return [lax.ppermute(x, "lo", to) if o else x for o, x, to in zip(APART, parts, pairs)]
    own = lax.axis_index("hi") >> bit & 1
    blocks = by_place(blocks)
    halves = [jnp.stack([blocks[i, 0], blocks[i, 1]], axis=1) for i in range(2)]
    both = jnp.stack([jnp.where(own == 0, half, jnp.flip(half, 1)) for half in halves])
    both = jnp.take(both.reshape(2, count, groups, top, 128), regroup, axis=2)
    both = lax.all_to_all(both, "lo", split_axis=2, concat_axis=2, tiled=True)
    return [both.reshape(2, count, G, 128)]


def padded(rows):
    return -(-(rows + PITCH) // 8) * 8


def on_device(state, gates, regroup):
    hi_bits = lax.axis_size("hi").bit_length() - 1
    groups = lax.axis_size("lo")
    bits = [k % hi_bits for k in range(4)]
    top = G // groups
    whole = 2 * state.shape[1] // 128

    block = jax.ShapeDtypeStruct((HALF - EARLY, HALF, 128), BF)
    early_block = jax.ShapeDtypeStruct((EARLY, HALF, 128), BF)
    turned = pltpu.VMEM((2, padded(HALF // 2 * PITCH), 128), F32)
    spread = pltpu.VMEM((padded(whole), 128), F32)
    lanes, rows = (4 * G, 8 * G), (G, 2 * G)

    x = state.reshape(2, -1, 128).transpose(1, 0, 2).reshape(whole, 128)
    shapes = [jax.ShapeDtypeStruct(shape, BF) for shape in ((2 * G, 4 * G), (2 * G, 4 * G), lanes, rows)]
    early_w0, w0, w1, g = call(first_weights_kernel, shapes, (gates,), flops=COST)
    shapes = [jax.ShapeDtypeStruct(shape, BF) for shape in ((whole // 2, 4 * G), (HALF // 2 - EARLY, G, 4 * G))]
    *early, mixed, rest = call(first_kernel, [early_block] * 4 + shapes, (x, early_w0, w1, g), scratch=[spread, turned])
    early = exchange(early, bits[0], bits[1])
    shapes = [jax.ShapeDtypeStruct(shape, BF) for shape in (lanes, rows, (4 * G, 4 * G))]
    kernel = functools.partial(second_kernel, top if groups == 4 else 0)
    *late, w1, g, w = call(kernel, [block] * 4 + shapes, (mixed, rest, w0, w1, g, gates), scratch=[turned])
    late = exchange(late, bits[0], bits[1])
    early = regrouped(early, regroup, bits[1], groups, top, COST)
    late = regrouped(late, regroup, bits[1], groups, top, after=early[3:])
    early = call(middle_kernel, [early_block] * 4, (*early, w1, g), flops=COST)
    late = call(middle_kernel, [block] * 4, (*late, w1, g), after=early[3:])
    early = exchange(early, bits[2], bits[3])
    late = exchange(late, bits[2], bits[3])

    wide = jax.ShapeDtypeStruct((2, padded(HALF * NARROW), 128), F32)
    wides = call(gather_kernel, [wide] * 2, early, flops=COST)
    late = by_place(late)
    scratch = [pltpu.VMEM((whole // 2, 128), BF), pltpu.SemaphoreType.DMA((HALF // 8,))]
    shapes = [jax.ShapeDtypeStruct((whole, 128), BF), wide]
    out = []
    for j in range(2):
        args = (*out, wides[j], late[1, j], late[0, j], w)
        aliases = {0: 0, 1: 1} if out else {0: 1}
        specs = [ANY] * len(out) + [VMEM] * 4
        kernel = functools.partial(last_kernel, j)
        out = call(kernel, shapes, args, specs, scratch, aliases=aliases, out_specs=[ANY, VMEM])[:1]
    (out,) = out
    return out.reshape(-1, 2, 128).transpose(1, 0, 2).reshape(state.shape)


def solution(mesh):
    placed = (P(None, ("hi", "lo")), P(), P())
    return jax.shard_map(
        on_device, mesh=mesh, in_specs=placed, out_specs=P(None, ("hi", "lo")), check_vma=False
    )
```

```python
import functools

import jax
import jax.numpy as jnp
from jax import lax
from jax.experimental import pallas as pl
from jax.experimental.pallas import tpu as pltpu
from jax.sharding import PartitionSpec as P

GQ = 6
G = 2**GQ
HALF = G // 2
BF = jnp.bfloat16
F32 = jnp.float32


def iotas(rows, columns):
    shape = (rows, columns)
    return lax.broadcasted_iota(jnp.int32, shape, 0), lax.broadcasted_iota(jnp.int32, shape, 1)


def dot(x, y):
    return jnp.dot(x, y, preferred_element_type=F32)


def turned_dot(x, y):
    return lax.dot_general(x, y, (((1,), (1,)), ((), ())), preferred_element_type=F32)


def ones(where):
    return where.astype(F32).astype(BF)


def gate_of(ref, layer, block):
    return jnp.concatenate([ref[layer, block, 0], ref[layer, block, 1]], axis=1)


def squared(gate):
    return jnp.concatenate([gate, jnp.concatenate([-gate[:, G:], gate[:, :G]], axis=1)], axis=0)


def product(later, earlier):
    return dot(later, squared(earlier))


def wide_product(later, earlier):
    parts = []
    for x in (later, squared(earlier)):
        high = x.astype(BF)
        parts.append((high, (x - high.astype(F32)).astype(BF)))
    (lh, ll), (eh, el) = parts
    return dot(jnp.concatenate([lh, lh, ll], axis=1), jnp.concatenate([eh, el, eh], axis=0))


def first_weights(gate, part):
    real = jnp.concatenate([gate[:, :G], gate[:, :G]], axis=1)
    imag = jnp.concatenate([gate[:, G:], gate[:, G:]], axis=1)
    low = iotas(HALF // 2, 2 * G)[1] < G
    rows = []
    for ch in range(2):
        start = ch * HALF + part * HALF // 2
        r, i = (x[start : start + HALF // 2] for x in (real, imag))
        for pair in ((r, -i), (i, r)):
            for mask in (low, ~low):
                rows.append(jnp.concatenate([jnp.where(mask, x, 0.0) for x in pair], axis=1))
    return jnp.concatenate(rows, axis=0).astype(BF)


def columns(size):
    return lax.broadcasted_iota(jnp.int32, (1, size), 1)


def placed(rows, to, minus):
    at = iotas(rows, to.shape[1])[0]
    return jnp.where(at == to, (1 - 2 * minus).astype(F32), 0.0).astype(BF)


def right_weights(gate, low, in_bit, out_bit):
    k, b = iotas(G, G)
    order = ((k & (HALF - 1)) << 1 | k >> GQ - 1) if low else k ^ in_bit * HALF
    gate = gate.astype(BF)
    t = turned_dot(ones(b == order), jnp.concatenate([gate[:, :G], gate[:, G:]], axis=0)).astype(BF)
    n = columns(8 * G)
    bit = lambda i: n >> i & 1
    to = ((bit(7) ^ out_bit) << GQ - 1) | n & (HALF - 1)
    turn_i = bit(8)
    part = bit(5) ^ turn_i
    sign_i = turn_i & (1 - bit(5))
    made = []
    for p in range(2):
        y = dot(t, placed(2 * G, to + (part ^ p) * G, sign_i ^ ((1 - part) & p)))
        made.append([jnp.where(bit(6) == c, y, 0.0).astype(BF) for c in range(2)])
    if low:
        rows = [made[p][c] for c in range(2) for p in range(2)]
    else:
        rows = [made[p][c][i * HALF : (i + 1) * HALF] for i in range(2) for c in range(2) for p in range(2)]
    return jnp.concatenate(rows, axis=0)


def left_weights(gate, step, out_bit):
    k, a = iotas(G, G)
    rows = dot(ones(a == k ^ out_bit * HALF), gate.astype(BF)).astype(BF)
    k, a = iotas(2 * G, 2 * G)
    return dot(rows, ones(a == k ^ step)).astype(BF)


def last_weights(gate, in_bit):
    k, b = iotas(2 * G, G)
    t = dot(ones(b == ((k >> 1 & (HALF - 1)) << 1 | k >> GQ)), gate).astype(BF)
    n = columns(4 * G)
    p_in = n >> 5 & 1
    b_in = ((n >> 7 ^ in_bit) << GQ - 1) | n & (HALF - 1)
    ch = n >> 6 & 1
    real, imag = (dot(t, placed(2 * G, b_in + (p_in ^ p) * G, (1 - p) * p_in)) for p in range(2))
    y = jnp.where((iotas(2 * G, 4 * G)[0] & 1) == 0, real, imag)
    rows = [jnp.where(ch == c, y[b0 * G : (b0 + 1) * G], 0.0) for b0 in range(2) for c in range(2)]
    return jnp.concatenate(rows, axis=0).astype(BF)


def turn_four(a):
    lane = lax.broadcasted_iota(jnp.int32, a[0].shape, 1)
    wide = lane < 64
    narrow = (lane & 32) == 0
    s, out = [None] * 4, [None] * 4
    for r in range(2):
        s[r] = jnp.where(wide, a[r], pltpu.roll(a[r + 2], 64, 1))
        s[r + 2] = jnp.where(wide, pltpu.roll(a[r], 64, 1), a[r + 2])
    for r in (0, 2):
        out[r] = jnp.where(narrow, s[r], pltpu.roll(s[r + 1], 32, 1))
        out[r + 1] = jnp.where(narrow, pltpu.roll(s[r], 96, 1), s[r + 1])
    return out


def turn(parts):
    out = [[None, None] for _ in range(8)]
    for n in range(2):
        for m in range(2):
            four = turn_four([part[:, m * 128 : (m + 1) * 128] for part in parts[n * 4 : n * 4 + 4]])
            for q in range(4):
                out[m * 4 + q][n] = four[q]
    return out


def both_gates(x, w, g):
    n = x.shape[0]
    z = jnp.dot(x.reshape(n * G, 4 * G), w, preferred_element_type=F32).astype(BF)
    outs = []
    for k in range(n):
        rows = z[k * G : (k + 1) * G]
        s = jnp.concatenate([rows[:, : 4 * G], rows[:, 4 * G :]], axis=0)
        outs.append(jnp.dot(g, s, preferred_element_type=F32).astype(BF))
    return outs


PLACES = ((1, 0), (1, 1), (0, 1), (0, 0))
APART = (3, 2, 1, 0)


def by_place(blocks):
    return dict(zip(PLACES, blocks))


def store_blocks(outs, at, blocks):
    blocks = by_place(blocks)
    for k, out in enumerate(outs):
        for i in range(2):
            for j in range(2):
                blocks[i, j][at + k] = out[j * HALF : (j + 1) * HALF, i * 128 : (i + 1) * 128]


PITCH = G + 1
NARROW = HALF + 1
EARLY = 14
COST = 2 * 10**9


def own_bits():
    hi_bits = lax.axis_size("hi").bit_length() - 1
    hi = lax.axis_index("hi")
    return [hi >> k % hi_bits & 1 for k in range(4)]


def split_rows(k, x, w, turned):
    r = turned_dot(w, x).astype(BF)
    some = HALF // 2
    tiles = turn([r[g * some : (g + 1) * some] for g in range(8)])
    for q in range(8):
        for n in range(2):
            turned[n, pl.ds(k * 8 + q, some, stride=PITCH), :] = tiles[q][n].astype(F32)


def rows_of(turned, first, last):
    halves = [jnp.stack([turned[i, cp * PITCH : cp * PITCH + G, :] for cp in range(first, last)]) for i in range(2)]
    return jnp.concatenate(halves, axis=2).astype(BF)


def first_weights_kernel(gates, early_w0_ref, w0_ref, w1_ref, g_ref):
    own = own_bits()
    late = product(gate_of(gates, 3, 0), gate_of(gates, 2, 0))
    soon = product(gate_of(gates, 1, 0), gate_of(gates, 0, 0))
    gate = wide_product(late, soon)
    early_w0_ref[...] = first_weights(gate, 0)
    w0_ref[...] = first_weights(gate, 1)
    w1_ref[...] = right_weights(gate_of(gates, 0, 1), True, 0, own[0])
    g_ref[...] = left_weights(product(gate_of(gates, 1, 2), gate_of(gates, 0, 2)), 0, own[1])


def first_kernel(x_ref, w0_ref, w1_ref, g_ref, o0, o1, o2, o3, mixed, rest, spread, turned):
    early = o0.shape[0]
    for k in range(G // 8):
        spread[k * 512 : (k + 1) * 512, :] = x_ref[k * 512 : (k + 1) * 512, :].astype(F32)
        x = jnp.concatenate([spread[pl.ds(k * 512 + p, 256, stride=2), :] for p in range(2)], axis=1).astype(BF)
        mixed[k * 256 : (k + 1) * 256, :] = x
        split_rows(k, x, w0_ref[...], turned)

    store_blocks(both_gates(rows_of(turned, 0, early), w1_ref[...], g_ref[...]), 0, (o0, o1, o2, o3))
    rest[...] = rows_of(turned, early, HALF // 2)


def later_weights(top, gates, w1_ref, g_ref, w_ref):
    own = own_bits()
    w1_ref[...] = right_weights(product(gate_of(gates, 2, 1), gate_of(gates, 1, 1)), False, own[0], own[2])
    step = top * lax.axis_index("lo") if top else 0
    g_ref[...] = left_weights(product(gate_of(gates, 3, 2), gate_of(gates, 2, 2)), step, own[3])
    w_ref[...] = last_weights(gate_of(gates, 3, 1), own[2])


def second_kernel(top, mixed, rest, w0_ref, w1_ref, g_ref, gates, *refs):
    *blocks, turned = refs[:4] + refs[7:]
    later_weights(top, gates, *refs[4:7])
    store_blocks(both_gates(rest[...], w1_ref[...], g_ref[...]), 0, blocks)
    for k in range(G // 8):
        split_rows(k, mixed[k * 256 : (k + 1) * 256, :], w0_ref[...], turned)
    made = both_gates(rows_of(turned, 0, HALF // 2), w1_ref[...], g_ref[...])
    store_blocks(made, rest.shape[0], blocks)


def joined(ins):
    order = [APART.index(o) for o in range(4)] if len(ins) > 1 else [0]
    halves = [jnp.concatenate([ins[at][i] for at in order], axis=1) for i in range(2)]
    return jnp.concatenate(halves, axis=2)


def middle_kernel(*refs):
    *ins, w1_ref, g_ref, o0, o1, o2, o3 = refs
    store_blocks(both_gates(joined(ins), w1_ref[...], g_ref[...]), 0, (o0, o1, o2, o3))


def gather_rows(first, pair, wide):
    for k in range(pair[0].shape[0]):
        for i in range(2):
            wide[i, pl.ds(first + k, HALF, stride=NARROW), :] = pair[i][k].astype(F32)


def gather_kernel(b0, b1, b2, b3, *wides):
    blocks = by_place((b0, b1, b2, b3))
    for j, wide in enumerate(wides):
        gather_rows(0, (blocks[0, j], blocks[1, j]), wide)


def last_kernel(j, *refs):
    moved, stayed, w_ref, o_ref, wide, made, sems = refs[-7:]
    gather_rows(HALF - moved.shape[0], (stayed, moved), wide)
    start = (own_bits()[3] ^ j) * (o_ref.shape[0] // 2)
    copies = []
    for k in range(HALF // 8):
        starts = [(k * 8 + q) * NARROW for q in range(8)]
        halves = [jnp.concatenate([wide[i, at : at + HALF, :] for at in starts], axis=0) for i in range(2)]
        x = jnp.concatenate(halves, axis=1).astype(BF)
        r = turned_dot(w_ref[...], x).astype(BF)
        for m in range(2):
            tiles = turn_four([r[g * G : (g + 1) * G, m * 128 : (m + 1) * 128] for g in range(4)])
            for q in range(4):
                at = (k * 8 + m * 4 + q) * G
                made[at : at + G, :] = tiles[q]
        rows = slice(k * 512, (k + 1) * 512)
        to = pl.ds(pl.multiple_of(start + k * 512, 512), 512)
        copies.append(pltpu.make_async_copy(made.at[rows], o_ref.at[to], sems.at[k]))
        copies[-1].start()
    for copy in copies:
        copy.wait()


def pick_kernel(groups, regroup, *refs):
    ins, outs = refs[:-groups], refs[-groups:]
    blocks = by_place(ins)
    own = own_bits()[1]
    lo = lax.axis_index("lo")
    rows = outs[0].shape[2]
    for o, out in zip(APART, outs):
        t = jnp.sum(jnp.where(columns(groups) == lo ^ o, regroup[...], 0))
        j = t >> 1 ^ own
        at = pl.ds(pl.multiple_of((t & 1) * rows, rows), rows)
        for half in range(2):

            @pl.when(j == half)
            def _():
                for i in range(2):
                    out[i] = blocks[i, half][:, at, :]


VMEM = pl.BlockSpec(memory_space=pltpu.VMEM)
ANY = pl.BlockSpec(memory_space=pl.ANY)
SMEM = pl.BlockSpec(memory_space=pltpu.SMEM)


def call(kernel, outs, args, specs=None, scratch=(), after=(), flops=1, aliases={}, out_specs=None):
    specs = specs or [VMEM] * len(args)

    def body(*refs):
        kernel(*refs[: len(args)], *refs[len(args) + len(after) :])

    return pl.pallas_call(
        body,
        out_shape=outs,
        in_specs=specs + [ANY] * len(after),
        out_specs=out_specs or jax.tree.map(lambda _: VMEM, outs),
        scratch_shapes=scratch,
        input_output_aliases=aliases,
        cost_estimate=pl.CostEstimate(flops=flops, bytes_accessed=1, transcendentals=0),
        compiler_params=pltpu.CompilerParams(vmem_limit_bytes=40 * 2**20),
    )(*args, *after)


def swapped(x, apart):
    return lax.ppermute(x, "hi", [(d, d ^ apart) for d in range(lax.axis_size("hi"))])


def exchange(blocks, b_bit, a_bit):
    out = []
    for (i, j), block in zip(PLACES, blocks):
        apart = i << b_bit | j << a_bit
        out.append(swapped(block, apart) if apart else block)
    return out


def regrouped(blocks, regroup, bit, groups, top, flops=1, after=()):
    count = blocks[0].shape[-3]
    if groups == 4:
        part = jax.ShapeDtypeStruct((2, count, top, 128), BF)
        parts = call(functools.partial(pick_kernel, groups), [part] * groups, (regroup.reshape(1, groups), *blocks), after=after, flops=flops)
        pairs = [[(d, d ^ o) for d in range(groups)] for o in APART]
        return [lax.ppermute(x, "lo", to) if o else x for o, x, to in zip(APART, parts, pairs)]
    own = lax.axis_index("hi") >> bit & 1
    blocks = by_place(blocks)
    halves = [jnp.stack([blocks[i, 0], blocks[i, 1]], axis=1) for i in range(2)]
    both = jnp.stack([jnp.where(own == 0, half, jnp.flip(half, 1)) for half in halves])
    both = jnp.take(both.reshape(2, count, groups, top, 128), regroup, axis=2)
    both = lax.all_to_all(both, "lo", split_axis=2, concat_axis=2, tiled=True)
    return [both.reshape(2, count, G, 128)]


def padded(rows):
    return -(-(rows + PITCH) // 8) * 8


def on_device(state, gates, regroup):
    hi_bits = lax.axis_size("hi").bit_length() - 1
    groups = lax.axis_size("lo")
    bits = [k % hi_bits for k in range(4)]
    top = G // groups
    whole = 2 * state.shape[1] // 128

    block = jax.ShapeDtypeStruct((HALF - EARLY, HALF, 128), BF)
    early_block = jax.ShapeDtypeStruct((EARLY, HALF, 128), BF)
    turned = pltpu.VMEM((2, padded(HALF // 2 * PITCH), 128), F32)
    spread = pltpu.VMEM((padded(whole), 128), F32)
    lanes, rows = (4 * G, 8 * G), (G, 2 * G)

    x = state.reshape(2, -1, 128).transpose(1, 0, 2).reshape(whole, 128)
    shapes = [jax.ShapeDtypeStruct(shape, BF) for shape in ((2 * G, 4 * G), (2 * G, 4 * G), lanes, rows)]
    early_w0, w0, w1, g = call(first_weights_kernel, shapes, (gates,), flops=COST)
    shapes = [jax.ShapeDtypeStruct(shape, BF) for shape in ((whole // 2, 4 * G), (HALF // 2 - EARLY, G, 4 * G))]
    *early, mixed, rest = call(first_kernel, [early_block] * 4 + shapes, (x, early_w0, w1, g), scratch=[spread, turned])
    early = exchange(early, bits[0], bits[1])
    shapes = [jax.ShapeDtypeStruct(shape, BF) for shape in (lanes, rows, (4 * G, 4 * G))]
    kernel = functools.partial(second_kernel, top if groups == 4 else 0)
    *late, w1, g, w = call(kernel, [block] * 4 + shapes, (mixed, rest, w0, w1, g, gates), scratch=[turned])
    late = exchange(late, bits[0], bits[1])
    early = regrouped(early, regroup, bits[1], groups, top, COST)
    late = regrouped(late, regroup, bits[1], groups, top, after=early[3:])
    early = call(middle_kernel, [early_block] * 4, (*early, w1, g), flops=COST)
    late = call(middle_kernel, [block] * 4, (*late, w1, g), after=early[3:])
    early = exchange(early, bits[2], bits[3])
    late = exchange(late, bits[2], bits[3])

    wide = jax.ShapeDtypeStruct((2, padded(HALF * NARROW), 128), F32)
    wides = call(gather_kernel, [wide] * 2, early, flops=COST)
    late = by_place(late)
    scratch = [pltpu.VMEM((whole // 2, 128), BF), pltpu.SemaphoreType.DMA((HALF // 8,))]
    shapes = [jax.ShapeDtypeStruct((whole, 128), BF), wide]
    out = []
    for j in range(2):
        args = (*out, wides[j], late[1, j], late[0, j], w)
        aliases = {0: 0, 1: 1} if out else {0: 1}
        specs = [ANY] * len(out) + [VMEM] * 4
        kernel = functools.partial(last_kernel, j)
        out = call(kernel, shapes, args, specs, scratch, aliases=aliases, out_specs=[ANY, VMEM])[:1]
    (out,) = out
    return out.reshape(-1, 2, 128).transpose(1, 0, 2).reshape(state.shape)


def solution(mesh):
    placed = (P(None, ("hi", "lo")), P(), P())
    return jax.shard_map(
        on_device, mesh=mesh, in_specs=placed, out_specs=P(None, ("hi", "lo")), check_vma=False
    )
```

```python
import functools

import jax
import jax.numpy as jnp
from jax import lax
from jax.experimental import pallas as pl
from jax.experimental.pallas import tpu as pltpu
from jax.sharding import PartitionSpec as P

GQ = 6
G = 2**GQ
HALF = G // 2
BF = jnp.bfloat16
F32 = jnp.float32


def iotas(rows, columns):
    shape = (rows, columns)
    return lax.broadcasted_iota(jnp.int32, shape, 0), lax.broadcasted_iota(jnp.int32, shape, 1)


def dot(x, y):
    return jnp.dot(x, y, preferred_element_type=F32)


def turned_dot(x, y):
    return lax.dot_general(x, y, (((1,), (1,)), ((), ())), preferred_element_type=F32)


def ones(where):
    return where.astype(F32).astype(BF)


def gate_of(ref, layer, block):
    return jnp.concatenate([ref[layer, block, 0], ref[layer, block, 1]], axis=1)


def squared(gate):
    return jnp.concatenate([gate, jnp.concatenate([-gate[:, G:], gate[:, :G]], axis=1)], axis=0)


def product(later, earlier):
    return dot(later, squared(earlier))


def wide_product(later, earlier):
    parts = []
    for x in (later, squared(earlier)):
        high = x.astype(BF)
        parts.append((high, (x - high.astype(F32)).astype(BF)))
    (lh, ll), (eh, el) = parts
    return dot(jnp.concatenate([lh, lh, ll], axis=1), jnp.concatenate([eh, el, eh], axis=0))


def first_weights(gate, part):
    real = jnp.concatenate([gate[:, :G], gate[:, :G]], axis=1)
    imag = jnp.concatenate([gate[:, G:], gate[:, G:]], axis=1)
    low = iotas(HALF // 2, 2 * G)[1] < G
    rows = []
    for ch in range(2):
        start = ch * HALF + part * HALF // 2
        r, i = (x[start : start + HALF // 2] for x in (real, imag))
        for pair in ((r, -i), (i, r)):
            for mask in (low, ~low):
                rows.append(jnp.concatenate([jnp.where(mask, x, 0.0) for x in pair], axis=1))
    return jnp.concatenate(rows, axis=0).astype(BF)


def columns(size):
    return lax.broadcasted_iota(jnp.int32, (1, size), 1)


def placed(rows, to, minus):
    at = iotas(rows, to.shape[1])[0]
    return jnp.where(at == to, (1 - 2 * minus).astype(F32), 0.0).astype(BF)


def right_weights(gate, low, in_bit, out_bit):
    k, b = iotas(G, G)
    order = ((k & (HALF - 1)) << 1 | k >> GQ - 1) if low else k ^ in_bit * HALF
    gate = gate.astype(BF)
    t = turned_dot(ones(b == order), jnp.concatenate([gate[:, :G], gate[:, G:]], axis=0)).astype(BF)
    n = columns(8 * G)
    bit = lambda i: n >> i & 1
    to = ((bit(7) ^ out_bit) << GQ - 1) | n & (HALF - 1)
    turn_i = bit(8)
    part = bit(5) ^ turn_i
    sign_i = turn_i & (1 - bit(5))
    made = []
    for p in range(2):
        y = dot(t, placed(2 * G, to + (part ^ p) * G, sign_i ^ ((1 - part) & p)))
        made.append([jnp.where(bit(6) == c, y, 0.0).astype(BF) for c in range(2)])
    if low:
        rows = [made[p][c] for c in range(2) for p in range(2)]
    else:
        rows = [made[p][c][i * HALF : (i + 1) * HALF] for i in range(2) for c in range(2) for p in range(2)]
    return jnp.concatenate(rows, axis=0)


def left_weights(gate, step, out_bit):
    k, a = iotas(G, G)
    rows = dot(ones(a == k ^ out_bit * HALF), gate.astype(BF)).astype(BF)
    k, a = iotas(2 * G, 2 * G)
    return dot(rows, ones(a == k ^ step)).astype(BF)


def last_weights(gate, in_bit):
    k, b = iotas(2 * G, G)
    t = dot(ones(b == ((k >> 1 & (HALF - 1)) << 1 | k >> GQ)), gate).astype(BF)
    n = columns(4 * G)
    p_in = n >> 5 & 1
    b_in = ((n >> 7 ^ in_bit) << GQ - 1) | n & (HALF - 1)
    ch = n >> 6 & 1
    real, imag = (dot(t, placed(2 * G, b_in + (p_in ^ p) * G, (1 - p) * p_in)) for p in range(2))
    y = jnp.where((iotas(2 * G, 4 * G)[0] & 1) == 0, real, imag)
    rows = [jnp.where(ch == c, y[b0 * G : (b0 + 1) * G], 0.0) for b0 in range(2) for c in range(2)]
    return jnp.concatenate(rows, axis=0).astype(BF)


def turn_four(a):
    lane = lax.broadcasted_iota(jnp.int32, a[0].shape, 1)
    wide = lane < 64
    narrow = (lane & 32) == 0
    s, out = [None] * 4, [None] * 4
    for r in range(2):
        s[r] = jnp.where(wide, a[r], pltpu.roll(a[r + 2], 64, 1))
        s[r + 2] = jnp.where(wide, pltpu.roll(a[r], 64, 1), a[r + 2])
    for r in (0, 2):
        out[r] = jnp.where(narrow, s[r], pltpu.roll(s[r + 1], 32, 1))
        out[r + 1] = jnp.where(narrow, pltpu.roll(s[r], 96, 1), s[r + 1])
    return out


def turn(parts):
    out = [[None, None] for _ in range(8)]
    for n in range(2):
        for m in range(2):
            four = turn_four([part[:, m * 128 : (m + 1) * 128] for part in parts[n * 4 : n * 4 + 4]])
            for q in range(4):
                out[m * 4 + q][n] = four[q]
    return out


def both_gates(x, w, g):
    n = x.shape[0]
    z = jnp.dot(x.reshape(n * G, 4 * G), w, preferred_element_type=F32).astype(BF)
    outs = []
    for k in range(n):
        rows = z[k * G : (k + 1) * G]
        s = jnp.concatenate([rows[:, : 4 * G], rows[:, 4 * G :]], axis=0)
        outs.append(jnp.dot(g, s, preferred_element_type=F32).astype(BF))
    return outs


PLACES = ((1, 0), (1, 1), (0, 1), (0, 0))
APART = (2, 3, 1, 0)


def by_place(blocks):
    return dict(zip(PLACES, blocks))


def store_blocks(outs, at, blocks):
    blocks = by_place(blocks)
    for k, out in enumerate(outs):
        for i in range(2):
            for j in range(2):
                blocks[i, j][at + k] = out[j * HALF : (j + 1) * HALF, i * 128 : (i + 1) * 128]


PITCH = G + 1
NARROW = HALF + 1
EARLY = 15
COST = 2 * 10**9


def own_bits():
    hi_bits = lax.axis_size("hi").bit_length() - 1
    hi = lax.axis_index("hi")
    return [hi >> k % hi_bits & 1 for k in range(4)]


def split_rows(k, x, w, turned):
    r = turned_dot(w, x).astype(BF)
    some = HALF // 2
    tiles = turn([r[g * some : (g + 1) * some] for g in range(8)])
    for q in range(8):
        for n in range(2):
            turned[n, pl.ds(k * 8 + q, some, stride=PITCH), :] = tiles[q][n].astype(F32)


def rows_of(turned, first, last):
    halves = [jnp.stack([turned[i, cp * PITCH : cp * PITCH + G, :] for cp in range(first, last)]) for i in range(2)]
    return jnp.concatenate(halves, axis=2).astype(BF)


def first_weights_kernel(gates, early_w0_ref, w0_ref, w1_ref, g_ref):
    own = own_bits()
    late = product(gate_of(gates, 3, 0), gate_of(gates, 2, 0))
    soon = product(gate_of(gates, 1, 0), gate_of(gates, 0, 0))
    gate = wide_product(late, soon)
    early_w0_ref[...] = first_weights(gate, 0)
    w0_ref[...] = first_weights(gate, 1)
    w1_ref[...] = right_weights(gate_of(gates, 0, 1), True, 0, own[0])
    g_ref[...] = left_weights(product(gate_of(gates, 1, 2), gate_of(gates, 0, 2)), 0, own[1])


def first_kernel(x_ref, w0_ref, w1_ref, g_ref, o0, o1, o2, o3, mixed, rest, spread, turned):
    early = o0.shape[0]
    for k in range(G // 8):
        spread[k * 512 : (k + 1) * 512, :] = x_ref[k * 512 : (k + 1) * 512, :].astype(F32)
        x = jnp.concatenate([spread[pl.ds(k * 512 + p, 256, stride=2), :] for p in range(2)], axis=1).astype(BF)
        mixed[k * 256 : (k + 1) * 256, :] = x
        split_rows(k, x, w0_ref[...], turned)

    store_blocks(both_gates(rows_of(turned, 0, early), w1_ref[...], g_ref[...]), 0, (o0, o1, o2, o3))
    rest[...] = rows_of(turned, early, HALF // 2)


def later_weights(top, gates, w1_ref, g_ref, w_ref):
    own = own_bits()
    w1_ref[...] = right_weights(product(gate_of(gates, 2, 1), gate_of(gates, 1, 1)), False, own[0], own[2])
    step = top * lax.axis_index("lo") if top else 0
    g_ref[...] = left_weights(product(gate_of(gates, 3, 2), gate_of(gates, 2, 2)), step, own[3])
    w_ref[...] = last_weights(gate_of(gates, 3, 1), own[2])


def second_kernel(top, mixed, rest, w0_ref, w1_ref, g_ref, gates, *refs):
    *blocks, turned = refs[:4] + refs[7:]
    later_weights(top, gates, *refs[4:7])
    store_blocks(both_gates(rest[...], w1_ref[...], g_ref[...]), 0, blocks)
    for k in range(G // 8):
        split_rows(k, mixed[k * 256 : (k + 1) * 256, :], w0_ref[...], turned)
    made = both_gates(rows_of(turned, 0, HALF // 2), w1_ref[...], g_ref[...])
    store_blocks(made, rest.shape[0], blocks)


def joined(ins):
    order = [APART.index(o) for o in range(4)] if len(ins) > 1 else [0]
    halves = [jnp.concatenate([ins[at][i] for at in order], axis=1) for i in range(2)]
    return jnp.concatenate(halves, axis=2)


def middle_kernel(*refs):
    *ins, w1_ref, g_ref, o0, o1, o2, o3 = refs
    store_blocks(both_gates(joined(ins), w1_ref[...], g_ref[...]), 0, (o0, o1, o2, o3))


def gather_rows(first, pair, wide):
    for k in range(pair[0].shape[0]):
        for i in range(2):
            wide[i, pl.ds(first + k, HALF, stride=NARROW), :] = pair[i][k].astype(F32)


def gather_kernel(b0, b1, b2, b3, *wides):
    blocks = by_place((b0, b1, b2, b3))
    for j, wide in enumerate(wides):
        gather_rows(0, (blocks[0, j], blocks[1, j]), wide)


def last_kernel(j, *refs):
    moved, stayed, w_ref, o_ref, wide, made, sems = refs[-7:]
    gather_rows(HALF - moved.shape[0], (stayed, moved), wide)
    start = (own_bits()[3] ^ j) * (o_ref.shape[0] // 2)
    copies = []
    for k in range(HALF // 8):
        starts = [(k * 8 + q) * NARROW for q in range(8)]
        halves = [jnp.concatenate([wide[i, at : at + HALF, :] for at in starts], axis=0) for i in range(2)]
        x = jnp.concatenate(halves, axis=1).astype(BF)
        r = turned_dot(w_ref[...], x).astype(BF)
        for m in range(2):
            tiles = turn_four([r[g * G : (g + 1) * G, m * 128 : (m + 1) * 128] for g in range(4)])
            for q in range(4):
                at = (k * 8 + m * 4 + q) * G
                made[at : at + G, :] = tiles[q]
        rows = slice(k * 512, (k + 1) * 512)
        to = pl.ds(pl.multiple_of(start + k * 512, 512), 512)
        copies.append(pltpu.make_async_copy(made.at[rows], o_ref.at[to], sems.at[k]))
        copies[-1].start()
    for copy in copies:
        copy.wait()


def pick_kernel(groups, regroup, *refs):
    ins, outs = refs[:-groups], refs[-groups:]
    blocks = by_place(ins)
    own = own_bits()[1]
    lo = lax.axis_index("lo")
    rows = outs[0].shape[2]
    for o, out in zip(APART, outs):
        t = jnp.sum(jnp.where(columns(groups) == lo ^ o, regroup[...], 0))
        j = t >> 1 ^ own
        at = pl.ds(pl.multiple_of((t & 1) * rows, rows), rows)
        for half in range(2):

            @pl.when(j == half)
            def _():
                for i in range(2):
                    out[i] = blocks[i, half][:, at, :]


VMEM = pl.BlockSpec(memory_space=pltpu.VMEM)
ANY = pl.BlockSpec(memory_space=pl.ANY)
SMEM = pl.BlockSpec(memory_space=pltpu.SMEM)


def call(kernel, outs, args, specs=None, scratch=(), after=(), flops=1, aliases={}, out_specs=None):
    specs = specs or [VMEM] * len(args)

    def body(*refs):
        kernel(*refs[: len(args)], *refs[len(args) + len(after) :])

    return pl.pallas_call(
        body,
        out_shape=outs,
        in_specs=specs + [ANY] * len(after),
        out_specs=out_specs or jax.tree.map(lambda _: VMEM, outs),
        scratch_shapes=scratch,
        input_output_aliases=aliases,
        cost_estimate=pl.CostEstimate(flops=flops, bytes_accessed=1, transcendentals=0),
        compiler_params=pltpu.CompilerParams(vmem_limit_bytes=40 * 2**20),
    )(*args, *after)


def swapped(x, apart):
    return lax.ppermute(x, "hi", [(d, d ^ apart) for d in range(lax.axis_size("hi"))])


def exchange(blocks, b_bit, a_bit):
    out = []
    for (i, j), block in zip(PLACES, blocks):
        apart = i << b_bit | j << a_bit
        out.append(swapped(block, apart) if apart else block)
    return out


def regrouped(blocks, regroup, bit, groups, top, flops=1, after=()):
    count = blocks[0].shape[-3]
    if groups == 4:
        part = jax.ShapeDtypeStruct((2, count, top, 128), BF)
        parts = call(functools.partial(pick_kernel, groups), [part] * groups, (regroup.reshape(1, groups), *blocks), after=after, flops=flops)
        pairs = [[(d, d ^ o) for d in range(groups)] for o in APART]
        return [lax.ppermute(x, "lo", to) if o else x for o, x, to in zip(APART, parts, pairs)]
    own = lax.axis_index("hi") >> bit & 1
    blocks = by_place(blocks)
    halves = [jnp.stack([blocks[i, 0], blocks[i, 1]], axis=1) for i in range(2)]
    both = jnp.stack([jnp.where(own == 0, half, jnp.flip(half, 1)) for half in halves])
    both = jnp.take(both.reshape(2, count, groups, top, 128), regroup, axis=2)
    both = lax.all_to_all(both, "lo", split_axis=2, concat_axis=2, tiled=True)
    return [both.reshape(2, count, G, 128)]


def padded(rows):
    return -(-(rows + PITCH) // 8) * 8


def on_device(state, gates, regroup):
    hi_bits = lax.axis_size("hi").bit_length() - 1
    groups = lax.axis_size("lo")
    bits = [k % hi_bits for k in range(4)]
    top = G // groups
    whole = 2 * state.shape[1] // 128

    block = jax.ShapeDtypeStruct((HALF - EARLY, HALF, 128), BF)
    early_block = jax.ShapeDtypeStruct((EARLY, HALF, 128), BF)
    turned = pltpu.VMEM((2, padded(HALF // 2 * PITCH), 128), F32)
    spread = pltpu.VMEM((padded(whole), 128), F32)
    lanes, rows = (4 * G, 8 * G), (G, 2 * G)

    x = state.reshape(2, -1, 128).transpose(1, 0, 2).reshape(whole, 128)
    shapes = [jax.ShapeDtypeStruct(shape, BF) for shape in ((2 * G, 4 * G), (2 * G, 4 * G), lanes, rows)]
    early_w0, w0, w1, g = call(first_weights_kernel, shapes, (gates,), flops=COST)
    shapes = [jax.ShapeDtypeStruct(shape, BF) for shape in ((whole // 2, 4 * G), (HALF // 2 - EARLY, G, 4 * G))]
    *early, mixed, rest = call(first_kernel, [early_block] * 4 + shapes, (x, early_w0, w1, g), scratch=[spread, turned])
    early = exchange(early, bits[0], bits[1])
    shapes = [jax.ShapeDtypeStruct(shape, BF) for shape in (lanes, rows, (4 * G, 4 * G))]
    kernel = functools.partial(second_kernel, top if groups == 4 else 0)
    *late, w1, g, w = call(kernel, [block] * 4 + shapes, (mixed, rest, w0, w1, g, gates), scratch=[turned])
    late = exchange(late, bits[0], bits[1])
    early = regrouped(early, regroup, bits[1], groups, top, COST)
    late = regrouped(late, regroup, bits[1], groups, top, after=early[3:])
    early = call(middle_kernel, [early_block] * 4, (*early, w1, g), flops=COST)
    late = call(middle_kernel, [block] * 4, (*late, w1, g), after=early[3:])
    early = exchange(early, bits[2], bits[3])
    late = exchange(late, bits[2], bits[3])

    wide = jax.ShapeDtypeStruct((2, padded(HALF * NARROW), 128), F32)
    wides = call(gather_kernel, [wide] * 2, early, flops=COST)
    late = by_place(late)
    scratch = [pltpu.VMEM((whole // 2, 128), BF), pltpu.SemaphoreType.DMA((HALF // 8,))]
    shapes = [jax.ShapeDtypeStruct((whole, 128), BF), wide]
    out = []
    for j in range(2):
        args = (*out, wides[j], late[1, j], late[0, j], w)
        aliases = {0: 0, 1: 1} if out else {0: 1}
        specs = [ANY] * len(out) + [VMEM] * 4
        kernel = functools.partial(last_kernel, j)
        out = call(kernel, shapes, args, specs, scratch, aliases=aliases, out_specs=[ANY, VMEM])[:1]
    (out,) = out
    return out.reshape(-1, 2, 128).transpose(1, 0, 2).reshape(state.shape)


def solution(mesh):
    placed = (P(None, ("hi", "lo")), P(), P())
    return jax.shard_map(
        on_device, mesh=mesh, in_specs=placed, out_specs=P(None, ("hi", "lo")), check_vma=False
    )
```
